32 devices in a mesh: dp: 8 (over z, x), mp: 4 (over y, core).
Axes of the slice: x: 2, y: 2, z: 4, core: 2. Of those that a mesh axis runs over, the one named last changes fastest.
Arguments:
- tokens: bfloat16 [16384, 768], P('dp'), may hold values from -6 to 6
- cotangent: bfloat16 [16384, 768], P('dp'), may hold values from -30 to 30
- exit_layer: int32 [16], P('dp'), may hold values from 1 to 12, as said below
- labels: int32 [16], P('dp'), may hold values from 0 to 2
- qkv_weight: float32 [768, 3, 768], P('dp', None, 'mp'), may hold values from -0.21875 to 0.21875
- qkv_first: float32 [768, 3, 768], P('dp', None, 'mp'), may hold values from -80 to 80
- qkv_second: float32 [768, 3, 768], P('dp', None, 'mp'), may hold values from 360.448 to 1425.408
- out_weight: float32 [768, 768], P('mp', 'dp'), may hold values from -6 to 6
- out_first: float32 [768, 768], P('mp', 'dp'), may hold values from -8 to 8
- out_second: float32 [768, 768], P('mp', 'dp'), may hold values from 3.60448 to 14.25408
- up_weight: float32 [768, 3072], P('dp', 'mp'), may hold values from -0.21875 to 0.21875
- up_first: float32 [768, 3072], P('dp', 'mp'), may hold values from -40 to 40
- up_second: float32 [768, 3072], P('dp', 'mp'), may hold values from 88.4736 to 355.5328
- down_weight: float32 [3072, 768], P('mp', 'dp'), may hold values from -0.109375 to 0.109375
- down_first: float32 [3072, 768], P('mp', 'dp'), may hold values from -80 to 80
- down_second: float32 [3072, 768], P('mp', 'dp'), may hold values from 360.448 to 1425.408
- pool_weight: float32 [768, 768], P('dp'), may hold values from -0.21875 to 0.21875
- pool_first: float32 [768, 768], P('dp'), may hold values from -0.0078125 to 0.0078125
- pool_second: float32 [768, 768], P('dp'), may hold values from 3.125e-06 to 1.25e-05
- qv_bias: float32 [2, 768], P(None, 'mp'), may hold values from -0.6 to 0.6
- qv_first: float32 [2, 768], P(None, 'mp'), may hold values from -80 to 80
- qv_second: float32 [2, 768], P(None, 'mp'), may hold values from 360.448 to 1425.408
- up_bias: float32 [3072], P('mp'), may hold values from -3 to 3
- upb_first: float32 [3072], P('mp'), may hold values from -40 to 40
- upb_second: float32 [3072], P('mp'), may hold values from 88.4736 to 355.5328
- layer_vectors: float32 [7, 768], replicated, may hold values from -1.5 to 1.5, as said below
- vector_first: float32 [7, 768], replicated, may hold values from -128 to 128
- vector_second: float32 [7, 768], replicated, may hold values from 901.12 to 3604.48
- class_weight: float32 [769, 3], replicated, may hold values from -0.4375 to 0.4375
- class_first: float32 [769, 3], replicated, may hold values from -0.0625 to 0.0625
- class_second: float32 [769, 3], replicated, may hold values from 0.0002 to 0.0008
Outputs:
- block_out: bfloat16 [16384, 768], P('dp')
- tokens_grad: bfloat16 [16384, 768], P('dp')
- ramp_entropy: float32 [], replicated
- qkv_new: float32 [768, 3, 768], P('dp', None, 'mp')
- qkv_first_new: float32 [768, 3, 768], P('dp', None, 'mp')
- qkv_second_new: float32 [768, 3, 768], P('dp', None, 'mp')
- qkv_copy: bfloat16 [768, 3, 768], P('dp', None, 'mp')
- out_new: float32 [768, 768], P('mp', 'dp')
- out_first_new: float32 [768, 768], P('mp', 'dp')
- out_second_new: float32 [768, 768], P('mp', 'dp')
- out_copy: bfloat16 [768, 768], P('mp', 'dp')
- up_new: float32 [768, 3072], P('dp', 'mp')
- up_first_new: float32 [768, 3072], P('dp', 'mp')
- up_second_new: float32 [768, 3072], P('dp', 'mp')
- up_copy: bfloat16 [768, 3072], P('dp', 'mp')
- down_new: float32 [3072, 768], P('mp', 'dp')
- down_first_new: float32 [3072, 768], P('mp', 'dp')
- down_second_new: float32 [3072, 768], P('mp', 'dp')
- down_copy: bfloat16 [3072, 768], P('mp', 'dp')
- pool_new: float32 [768, 768], P('dp')
- pool_first_new: float32 [768, 768], P('dp')
- pool_second_new: float32 [768, 768], P('dp')
- pool_copy: bfloat16 [768, 768], P('dp')
- qv_new: float32 [2, 768], P(None, 'mp')
- qv_first_new: float32 [2, 768], P(None, 'mp')
- qv_second_new: float32 [2, 768], P(None, 'mp')
- upb_new: float32 [3072], P('mp')
- upb_first_new: float32 [3072], P('mp')
- upb_second_new: float32 [3072], P('mp')
- vector_new: float32 [7, 768], replicated
- vector_first_new: float32 [7, 768], replicated
- vector_second_new: float32 [7, 768], replicated
- class_new: float32 [769, 3], replicated
- class_first_new: float32 [769, 3], replicated
- class_second_new: float32 [769, 3], replicated
The draws below stay inside these ranges and needn't reach their ends.
Inputs may be any that keep to these rules, and one draw needn't show every extreme that they name: `exit_layer`: the first sequence has exit layer 1; the second and the last have 12. `layer_vectors`: rows 0 and 2 lie between 0.5 and 1.5.
All inputs are finite; a program needn't handle non-finite values.
Results may differ from the reference program's by a relative error of at most 0.025.
Values may be sent and summed in bfloat16 or wider, within the bound.
No kernel may reach another device: no remote copies, remote signals or barrier semaphores. Data moves between devices by JAX's collectives and lax.ppermute only.
A program may use at most 192 MiB of HBM per device.

```python
import math
import jax
import jax.numpy as jnp
from jax import lax

D = 768
H = 12
HD = 64
FF = 3072
C = 3
NLAYERS = 12
LAYER = 6
STEP = 10
LEN = 1024
SEQS = 16
TOKENS = 16384
N_MP = 4


def draw_exit_layer(key, part):
    key = jax.random.fold_in(key, 11)
    ticket_key, late_key, early_key = jax.random.split(key, 3)
    position = jnp.arange(SEQS, dtype=jnp.int32)
    ticket = jax.random.randint(ticket_key, (SEQS,), 0, 3 * (SEQS - 1))
    living = ticket < SEQS - 1 + 2 * position
    late_exit = jax.random.randint(late_key, (SEQS,), LAYER, NLAYERS + 1)
    early_exit = jax.random.randint(early_key, (SEQS,), 1, LAYER)
    chosen = jnp.where(living, late_exit, early_exit)
    chosen = chosen.at[0].set(1).at[1].set(NLAYERS).at[SEQS - 1].set(NLAYERS)
    return chosen.astype(jnp.int32)


def draw_layer_vectors(key, part):
    key = jax.random.fold_in(key, 23)
    gain_key, shift_key = jax.random.split(key)
    gains = jax.random.uniform(gain_key, (7, D), jnp.float32, 0.5, 1.5)
    shifts = jnp.clip(0.3 * jax.random.normal(shift_key, (7, D), jnp.float32), -1.5, 1.5)
    row_index = jnp.arange(7)
    is_gain = (row_index == 0) | (row_index == 2)
    return jnp.where(is_gain[:, None], gains, shifts)


def draw_cotangent(key, part):
    key = jax.random.fold_in(key, 37)
    seq_index = jnp.arange(TOKENS, dtype=jnp.int32) // LEN
    along = seq_index.astype(jnp.float32) / max(SEQS - 1, 1)
    base = jnp.clip(jax.random.normal(key, (TOKENS, D), jnp.float32), -6.0, 6.0)
    row_scale = 3.0 - 2.0 * along
    return (base * row_scale[:, None]).astype(jnp.bfloat16)


def touch_ends(values, key, least, high):
    index_at = [jax.random.randint(jax.random.fold_in(key, axis), (), 0, length) for axis, length in enumerate(values.shape)]
    longest = values.shape.index(max(values.shape))
    beside = index_at[:longest] + [(index_at[longest] + 1) % values.shape[longest]] + index_at[longest + 1:]
    return values.at[tuple(index_at)].set(least).at[tuple(beside)].set(high)


def shard_levels(stream_key, dims, cuts, smallest, top_value):
    factor_of, own = 1.0, jax.random.fold_in(stream_key, 6)
    for dim, parts in cuts:
        draws = jnp.exp(jax.random.uniform(jax.random.fold_in(own, dim), (parts,), jnp.float32, smallest / len(cuts), top_value / len(cuts)))
        factor_of = factor_of * jnp.repeat(draws, dims[dim] // parts).reshape([-1 if axis == dim else 1 for axis in range(len(dims))])
    return factor_of


def scatter_about(stream_key, dims, scale, most, pieces=(), kind=jnp.bfloat16):
    array = jax.random.normal(stream_key, dims, jnp.float32) * scale
    if len(pieces) > 0:
        array = shard_levels(stream_key, dims, pieces, -0.22, 0.18) * array
    return jnp.clip(array, min=-most, max=most).astype(kind)


def setup_inputs(seed: int = 0) -> dict:
    key_list = jax.random.split(jax.random.key(seed), 32)
    tokens = scatter_about(key_list[0], (TOKENS, D), 1.0, 6.0, ((0, 8),))
    cotangent = draw_cotangent(jax.random.fold_in(key_list[31], 71), 0)
    exit_layer = draw_exit_layer(jax.random.fold_in(key_list[31], 71), 0)
    labels = touch_ends(jax.random.randint(key_list[3], (SEQS,), 0, C), jax.random.fold_in(key_list[3], 1), 0, C - 1).astype(jnp.int32)
    qkv_weight = scatter_about(key_list[4], (D, 3, D), D ** -0.5, 0.21875, ((0, 8), (2, 4)), jnp.float32)
    qkv_first = scatter_about(key_list[5], (D, 3, D), (0.115 * TOKENS ** 0.5), 80.0, ((0, 8), (2, 4)), jnp.float32)
    qkv_second = jnp.clip(jnp.exp(math.log(1425.408) - 1.3748656 * jax.random.uniform(key_list[6], (D, 3, D), jnp.float32) ** shard_levels(key_list[6], (D, 3, D), ((0, 8), (2, 4)), -0.2, 0.2)), 360.448, 1425.408)
    out_weight = scatter_about(key_list[7], (D, D), (max(1, 2 * D // LEN)) ** -0.5, 6.0, ((0, 4), (1, 8)), jnp.float32)
    out_first = scatter_about(key_list[8], (D, D), (0.0115 * TOKENS ** 0.5), 8.0, ((0, 4), (1, 8)), jnp.float32)
    out_second = jnp.clip(jnp.exp(math.log(14.25408) - 1.3748656 * jax.random.uniform(key_list[9], (D, D), jnp.float32) ** shard_levels(key_list[9], (D, D), ((0, 4), (1, 8)), -0.2, 0.2)), 3.60448, 14.25408)
    up_weight = scatter_about(key_list[10], (D, FF), D ** -0.5, 0.21875, ((0, 8), (1, 4)), jnp.float32)
    up_first = scatter_about(key_list[11], (D, FF), (0.057 * TOKENS ** 0.5), 40.0, ((0, 8), (1, 4)), jnp.float32)
    up_second = jnp.clip(jnp.exp(math.log(355.5328) - 1.3909133 * jax.random.uniform(key_list[12], (D, FF), jnp.float32) ** shard_levels(key_list[12], (D, FF), ((0, 8), (1, 4)), -0.2, 0.2)), 88.4736, 355.5328)
    down_weight = scatter_about(key_list[13], (FF, D), FF ** -0.5, 0.109375, ((0, 4), (1, 8)), jnp.float32)
    down_first = scatter_about(key_list[14], (FF, D), (0.115 * TOKENS ** 0.5), 80.0, ((0, 4), (1, 8)), jnp.float32)
    down_second = jnp.clip(jnp.exp(math.log(1425.408) - 1.3748656 * jax.random.uniform(key_list[15], (FF, D), jnp.float32) ** shard_levels(key_list[15], (FF, D), ((0, 4), (1, 8)), -0.2, 0.2)), 360.448, 1425.408)
    pool_weight = scatter_about(key_list[16], (D, D), D ** -0.5, 0.21875, ((0, 8),), jnp.float32)
    pool_first = scatter_about(key_list[17], (D, D), (0.0055 * SEQS ** -0.5), 0.0078125, ((0, 8),), jnp.float32)
    pool_second = jnp.clip(jnp.exp(math.log(1.249999968422344e-05) - 1.3862944 * jax.random.uniform(key_list[18], (D, D), jnp.float32) ** shard_levels(key_list[18], (D, D), ((0, 8),), -0.2, 0.2)), 3.12499992105586e-06, 1.249999968422344e-05)
    qv_bias = scatter_about(key_list[19], (2, D), 0.1, 0.6, ((1, 4),), jnp.float32)
    qv_first = scatter_about(key_list[20], (2, D), (0.115 * TOKENS ** 0.5), 80.0, ((1, 4),), jnp.float32)
    qv_second = jnp.clip(jnp.exp(math.log(1425.408) - 1.3748656 * jax.random.uniform(key_list[21], (2, D), jnp.float32) ** shard_levels(key_list[21], (2, D), ((1, 4),), -0.2, 0.2)), 360.448, 1425.408)
    up_bias = scatter_about(key_list[22], (FF,), 0.5, 3.0, ((0, 4),), jnp.float32)
    upb_first = scatter_about(key_list[23], (FF,), (0.057 * TOKENS ** 0.5), 40.0, ((0, 4),), jnp.float32)
    upb_second = jnp.clip(jnp.exp(math.log(355.5328) - 1.3909133 * jax.random.uniform(key_list[24], (FF,), jnp.float32) ** shard_levels(key_list[24], (FF,), ((0, 4),), -0.2, 0.2)), 88.4736, 355.5328)
    layer_vectors = draw_layer_vectors(jax.random.fold_in(key_list[31], 71), 0)
    vector_first = scatter_about(key_list[26], (7, D), (0.18 * TOKENS ** 0.5), 128.0, (), jnp.float32)
    vector_second = jnp.clip(jnp.exp(jax.random.uniform(key_list[27], (7, D), jnp.float32, math.log(901.12), math.log(3604.48))), 901.12, 3604.48)
    class_weight = scatter_about(key_list[28], (D + 1, C), (D // 4) ** -0.5, 0.4375, (), jnp.float32)
    class_first = scatter_about(key_list[29], (D + 1, C), (0.044 * SEQS ** -0.5), 0.0625, (), jnp.float32)
    class_second = jnp.clip(jnp.exp(jax.random.uniform(key_list[30], (D + 1, C), jnp.float32, math.log(0.0002), math.log(0.0008))), 0.0002, 0.0008)
    return {"tokens": tokens, "cotangent": cotangent, "exit_layer": exit_layer, "labels": labels, "qkv_weight": qkv_weight, "qkv_first": qkv_first, "qkv_second": qkv_second, "out_weight": out_weight, "out_first": out_first, "out_second": out_second, "up_weight": up_weight, "up_first": up_first, "up_second": up_second, "down_weight": down_weight, "down_first": down_first, "down_second": down_second, "pool_weight": pool_weight, "pool_first": pool_first, "pool_second": pool_second, "qv_bias": qv_bias, "qv_first": qv_first, "qv_second": qv_second, "up_bias": up_bias, "upb_first": upb_first, "upb_second": upb_second, "layer_vectors": layer_vectors, "vector_first": vector_first, "vector_second": vector_second, "class_weight": class_weight, "class_first": class_first, "class_second": class_second}


@jax.custom_vjp
def low(v):
    return lax.optimization_barrier(v.astype(jnp.bfloat16)).astype(jnp.float32)

@jax.custom_vjp
def low_back(v):
    return v

def low_keep(v):
    return (low(v), None)

def low_pass(kept, grad):
    return (grad,)

def back_keep(v):
    return (v, None)

def back_low(kept, grad):
    return (low(grad),)
low.defvjp(low_keep, low_pass)
low_back.defvjp(back_keep, back_low)
EPS_NORM = 1e-06
BETA_ONE = 0.9
BETA_TWO = 0.98
EPS_ADAM = 1e-08
DECAY = 0.01
RATE = 0.8
VECTOR_RATE = 0.3

def matmul(left, right):
    return jnp.dot(left, right, precision=lax.Precision.HIGHEST, preferred_element_type=jnp.float32)

def normalize(hidden):
    centred = hidden - lax.optimization_barrier(jnp.mean(hidden, axis=-1, keepdims=True))
    return centred * lax.rsqrt(lax.optimization_barrier(jnp.mean(centred * centred, axis=-1, keepdims=True)) + EPS_NORM)

@jax.checkpoint
def attend(queries, key_rows, values):
    raw_scores = jnp.einsum('qhd,khd->hqk', queries, key_rows, precision=lax.Precision.HIGHEST)
    scores = low_back(raw_scores) * HD ** (-0.5)
    weights = low(jax.nn.softmax(scores, axis=-1))
    return jnp.einsum('hqk,khd->qhd', weights, values, precision=lax.Precision.HIGHEST)

def split_sum(left, right, inner):
    row_count = left.shape[0]
    left_parts = left.reshape(row_count, N_MP, inner // N_MP)
    right_parts = right.reshape(N_MP, inner // N_MP, right.shape[1])
    partial_sums = jnp.einsum('tgc,gcd->gtd', left_parts, right_parts, precision=lax.Precision.HIGHEST)
    return lax.optimization_barrier(jnp.sum(low(partial_sums), axis=0))

def group_forward(params, tokens_f, cot_f, live_part, carry_rows, onehot, live_total):
    qkv_w, out_w, up_w, down_w, pool_w, qv_b, up_b, vectors, class_w = params
    row_count = tokens_f.shape[0]
    seqs_here = row_count // LEN
    projected = matmul(tokens_f, low(qkv_w).reshape(D, 3 * D))
    queries = low_back(low(projected[:, :D] + qv_b[0]))
    key_rows = low_back(low(projected[:, D:2 * D]))
    values = low_back(low(projected[:, 2 * D:] + qv_b[1]))
    head_shape = (seqs_here, LEN, H, HD)
    attended = lax.map(lambda triple: attend(triple[0], triple[1], triple[2]), (queries.reshape(head_shape), key_rows.reshape(head_shape), values.reshape(head_shape)))
    attn_rows = low_back(low(attended.reshape(row_count, D)))
    attn_total = low_back(split_sum(attn_rows, low(out_w), D))
    first_in = tokens_f + attn_total + vectors[4]
    middle = normalize(first_in) * vectors[0] + vectors[1]
    ffn_pre = low_back(matmul(low(middle), low(up_w)) + up_b)
    ffn_act = low(jax.nn.gelu(ffn_pre, approximate=False))
    ffn_total = low_back(split_sum(ffn_act, low(down_w), FF))
    second_in = middle + ffn_total + vectors[5]
    result = normalize(second_in) * vectors[2] + vectors[3]
    cls_rows = low(result).reshape(seqs_here, LEN, D)[:, 0]
    pool_pre = low_back(matmul(cls_rows, low(pool_w)) + vectors[6])
    pooled = low(jnp.tanh(pool_pre))
    logits = low_back(matmul(pooled, low(class_w[:D])) + class_w[D])
    log_probs = logits - jax.nn.logsumexp(logits, axis=-1, keepdims=True)
    cross_ent = -lax.optimization_barrier(jnp.sum(onehot * log_probs, axis=-1))
    entropy = -lax.optimization_barrier(jnp.sum(jnp.exp(log_probs) * log_probs, axis=-1))
    total_loss = jnp.sum(live_part * cross_ent) / live_total + jnp.sum(cot_f * result * carry_rows)
    return (total_loss, (result, jnp.sum(live_part * entropy)))

def adamw(weight, first, second, grad, rate, decay):
    first_new = BETA_ONE * first + (1.0 - BETA_ONE) * grad
    second_new = BETA_TWO * second + (1.0 - BETA_TWO) * grad * grad
    first_hat = first_new / (1.0 - BETA_ONE ** STEP)
    second_hat = second_new / (1.0 - BETA_TWO ** STEP)
    weight_new = weight - rate * (first_hat / (jnp.sqrt(second_hat) + EPS_ADAM) + decay * weight)
    return (weight_new, first_new, second_new)

def reference(tokens, cotangent, exit_layer, labels, qkv_weight, qkv_first, qkv_second, out_weight, out_first, out_second, up_weight, up_first, up_second, down_weight, down_first, down_second, pool_weight, pool_first, pool_second, qv_bias, qv_first, qv_second, up_bias, upb_first, upb_second, layer_vectors, vector_first, vector_second, class_weight, class_first, class_second):
    seq_total = exit_layer.shape[0]
    group_seqs = math.gcd(seq_total, max(1, 4096 // LEN))
    group_count = seq_total // group_seqs
    live = (exit_layer >= LAYER).astype(jnp.float32)
    onward = (exit_layer > LAYER).astype(jnp.float32)
    live_total = jnp.sum(live)
    onehot = (labels[:, None] == jnp.arange(C, dtype=jnp.int32)[None, :]).astype(jnp.float32)
    params = (qkv_weight, out_weight, up_weight, down_weight, pool_weight, qv_bias, up_bias, layer_vectors, class_weight)
    token_groups = tokens.astype(jnp.float32).reshape(group_count, group_seqs * LEN, D)
    cot_groups = cotangent.astype(jnp.float32).reshape(group_count, group_seqs * LEN, D)
    carry_groups = jnp.repeat(onward, LEN).reshape(group_count, group_seqs * LEN, 1)
    live_groups = live.reshape(group_count, group_seqs)
    onehot_groups = onehot.reshape(group_count, group_seqs, C)

    def one_group(totals, items):
        token_part, cot_part, carry_part, live_part, onehot_part = items

        def forward(weights, inputs):
            return group_forward(weights, inputs, cot_part, live_part, carry_part, onehot_part, live_total)
        loss_value, pullback, extras = jax.vjp(forward, params, token_part, has_aux=True)
        grad_params, grad_tokens = pullback(jnp.ones((), jnp.float32))
        totals = jax.tree.map(jnp.add, totals, grad_params)
        return (totals, (extras[0], grad_tokens, extras[1]))
    empty_grads = jax.tree.map(jnp.zeros_like, params)
    grads, (results, token_grads, entropies) = lax.scan(one_group, empty_grads, (token_groups, cot_groups, carry_groups, live_groups, onehot_groups))
    qkv_new, qkv_first_new, qkv_second_new = adamw(qkv_weight, qkv_first, qkv_second, grads[0], RATE * D ** (-0.5), DECAY)
    out_new, out_first_new, out_second_new = adamw(out_weight, out_first, out_second, grads[1], RATE * max(1, 2 * D // LEN) ** (-0.5), DECAY)
    up_new, up_first_new, up_second_new = adamw(up_weight, up_first, up_second, grads[2], RATE * D ** (-0.5), DECAY)
    down_new, down_first_new, down_second_new = adamw(down_weight, down_first, down_second, grads[3], RATE * FF ** (-0.5), DECAY)
    pool_new, pool_first_new, pool_second_new = adamw(pool_weight, pool_first, pool_second, grads[4], RATE * D ** (-0.5), DECAY)
    qv_new, qv_first_new, qv_second_new = adamw(qv_bias, qv_first, qv_second, grads[5], VECTOR_RATE, 0.0)
    upb_new, upb_first_new, upb_second_new = adamw(up_bias, upb_first, upb_second, grads[6], VECTOR_RATE, 0.0)
    vector_new, vector_first_new, vector_second_new = adamw(layer_vectors, vector_first, vector_second, grads[7], VECTOR_RATE, 0.0)
    class_new, class_first_new, class_second_new = adamw(class_weight, class_first, class_second, grads[8], RATE * (D // 4) ** (-0.5), DECAY)
    return (results.reshape(tokens.shape).astype(jnp.bfloat16), token_grads.reshape(tokens.shape).astype(jnp.bfloat16), jnp.sum(entropies) / live_total, qkv_new, qkv_first_new, qkv_second_new, qkv_new.astype(jnp.bfloat16), out_new, out_first_new, out_second_new, out_new.astype(jnp.bfloat16), up_new, up_first_new, up_second_new, up_new.astype(jnp.bfloat16), down_new, down_first_new, down_second_new, down_new.astype(jnp.bfloat16), pool_new, pool_first_new, pool_second_new, pool_new.astype(jnp.bfloat16), qv_new, qv_first_new, qv_second_new, upb_new, upb_first_new, upb_second_new, vector_new, vector_first_new, vector_second_new, class_new, class_first_new, class_second_new)
```

```python
import functools

import jax
import jax.numpy as jnp
import numpy as np
from jax import lax
from jax.experimental import pallas as pl
from jax.experimental.pallas import tpu as pltpu
from jax.sharding import PartitionSpec as P

D = 768
HD = 64
FF = 3072
LAYER = 6
STEP = 10
LEN = 1024


EPS_NORM = 1e-06
BETA_ONE = 0.9
BETA_TWO = 0.98
EPS_ADAM = 1e-08
DECAY = 0.01
RATE = 0.8
VECTOR_RATE = 0.3

LOW = jnp.bfloat16
WIDE = jnp.float32
LOG2_E = 1.4426950408889634
MIB = 2**20

CORE, SIDE, X_BIT, Z_LOW, Z_HIGH = 1, 2, 4, 8, 16
BLOCKS = 8
BLOCK_ROWS = D // BLOCKS
ORDERS = {
    "query": (Z_HIGH, Z_LOW, X_BIT, SIDE),
    "key": (SIDE, Z_HIGH, Z_LOW, X_BIT),
    "value": (X_BIT, SIDE, Z_HIGH, Z_LOW),
    "out": (X_BIT, SIDE, Z_HIGH, Z_LOW),
    "up": (Z_HIGH, Z_LOW, X_BIT, SIDE),
    "down": (Z_HIGH, Z_LOW, SIDE, X_BIT),
}
NAMES = tuple(ORDERS)


def dot(left, right):
    return lax.dot_general(
        left, right, (((1,), (0,)), ((), ())), preferred_element_type=WIDE
    )


def dot_nt(left, right):
    return lax.dot_general(
        left, right, (((1,), (1,)), ((), ())), preferred_element_type=WIDE
    )


def dot_tn(left, right):
    return lax.dot_general(
        left, right, (((0,), (0,)), ((), ())), preferred_element_type=WIDE
    )


def adamw(weight, first, second, grad, rate, decay):
    first_new = BETA_ONE * first + (1.0 - BETA_ONE) * grad
    second_new = BETA_TWO * second + (1.0 - BETA_TWO) * grad * grad
    first_hat = first_new / (1.0 - BETA_ONE**STEP)
    second_hat = second_new / (1.0 - BETA_TWO**STEP)
    weight_new = weight - rate * (first_hat / (jnp.sqrt(second_hat) + EPS_ADAM) + decay * weight)
    return (weight_new, first_new, second_new)


class Links:
    def __init__(self, dp_count, mp_count):
        self.dp_count = dp_count
        self.total = dp_count * mp_count
        self.cube = dp_count == BLOCKS
        self.dp = lax.axis_index("dp").astype(jnp.int32)
        mp = lax.axis_index("mp").astype(jnp.int32)
        self.side = mp // 2
        self.core = mp % 2

    def swap(self, value, bit):
        pairs = [(i, i ^ bit) for i in range(self.total)]
        return lax.ppermute(value, ("dp", "mp"), pairs)

    def places(self):
        rows = []
        for name in NAMES:
            for j in range(2 * BLOCKS):
                if self.cube:
                    bits = 0
                    for k, bit in enumerate(ORDERS[name]):
                        bits ^= bit if (j >> k) & 1 else 0
                    rows.append((bits // SIDE & 1, bits // X_BIT))
                else:
                    rows.append((j // BLOCKS, j % BLOCKS))
        flips = np.array(rows, np.int32)
        mine = self.dp if self.cube else 0
        return (self.side ^ flips[:, 0]) * BLOCKS + (mine ^ flips[:, 1])

    def spread(self, share, name):
        if not self.cube:
            near = lax.all_gather(share, "dp", axis=0, tiled=True)
            near = near.reshape(BLOCKS, BLOCK_ROWS, share.shape[1])
            return near, self.swap(near, SIDE)
        near = share[None]
        for bit in ORDERS[name][:-1]:
            near = jnp.concatenate([near, self.swap(near, bit)], axis=0)
        return near, self.swap(near, ORDERS[name][-1])

    def fold(self, near, far, name):
        if not self.cube:
            whole = near.astype(WIDE) + self.swap(far, SIDE).astype(WIDE)
            whole = whole.reshape(D, near.shape[2])
            return lax.psum_scatter(whole, "dp", scatter_dimension=0, tiled=True)
        order = ORDERS[name]
        parts = [near, self.swap(far, order[3])]
        for k in (2, 1, 0):
            half = 2**k
            send = sum(part[half : 2 * half].astype(WIDE) for part in parts)
            parts.append(self.swap(send.astype(LOW), order[k]))
        return sum(part[0].astype(WIDE) for part in parts)

    def total_over(self, value, with_side):
        if self.cube:
            for bit in (X_BIT, Z_LOW, Z_HIGH):
                value = value + self.swap(value, bit)
        else:
            value = lax.psum(value, "dp")
        if with_side:
            value = value + self.swap(value, SIDE)
        return value

    def rows_of(self, share):
        if not self.cube:
            return lax.all_gather(share, "dp", axis=0, tiled=True)
        number = self.dp * 4
        for bit in (X_BIT, Z_LOW, Z_HIGH):
            other = self.swap(share, bit)
            upper = (number & bit) != 0
            share = jnp.where(
                upper,
                jnp.concatenate([other, share], axis=0),
                jnp.concatenate([share, other], axis=0),
            )
        return share

    def both_sides(self, share):
        other = self.swap(share, SIDE)
        return jnp.where(
            self.side == 1,
            jnp.concatenate([other, share], axis=0),
            jnp.concatenate([share, other], axis=0),
        )


def call(kernel, name, grid, in_specs, out_specs, out_shape, scratch, places, args, flops, vmem=56):
    moved = sum(a.size * a.dtype.itemsize for a in args)
    moved += sum(int(np.prod(s.shape)) * np.dtype(s.dtype).itemsize for s in out_shape)
    return pl.pallas_call(
        kernel,
        out_shape=out_shape,
        grid_spec=pltpu.PrefetchScalarGridSpec(
            num_scalar_prefetch=1,
            grid=grid,
            in_specs=in_specs,
            out_specs=out_specs,
            scratch_shapes=scratch,
        ),
        compiler_params=pltpu.CompilerParams(vmem_limit_bytes=vmem * MIB),
        cost_estimate=pl.CostEstimate(
            flops=int(flops), bytes_accessed=int(moved), transcendentals=0
        ),
        name=name,
    )(places, *args)


def whole(array):
    return pl.BlockSpec(array.shape, lambda *_: (0,) * len(array.shape))


def rows(count, width):
    return pl.BlockSpec((count, width), lambda i, *_: (i, 0))


def shape(dims, kind):
    return jax.ShapeDtypeStruct(dims, kind)


def place_at(places, name, j):
    return places[1 + 2 * BLOCKS * NAMES.index(name) + j]


def gather_blocks(places, name, near, far, held):
    for j in range(2 * BLOCKS):
        source = near if j < BLOCKS else far
        held[place_at(places, name, j)] = source[j % BLOCKS]


def scatter_blocks(places, name, held, near, far):
    for j in range(2 * BLOCKS):
        target = near if j < BLOCKS else far
        target[j % BLOCKS] = held[place_at(places, name, j)]


def to_pairs(held):
    left = held[0:BLOCKS].reshape(D, held.shape[2])
    right = held[BLOCKS : 2 * BLOCKS].reshape(D, held.shape[2])
    return jnp.concatenate([left[:, :128], right[:, :128], left[:, 128:], right[:, 128:]], axis=1)


def from_pairs(value, held):
    left = jnp.concatenate([value[:, 0:128], value[:, 256:320]], axis=1)
    right = jnp.concatenate([value[:, 128:256], value[:, 320:384]], axis=1)
    held[0:BLOCKS] = left.reshape(BLOCKS, BLOCK_ROWS, 192)
    held[BLOCKS : 2 * BLOCKS] = right.reshape(BLOCKS, BLOCK_ROWS, 192)


def project_kernel(places, x, bias, qn, qf, kn, kf, vn, vf, q, k, v, w, held):
    @pl.when(pl.program_id(0) == 0)
    def _():
        for i, (name, near, far) in enumerate(
            (("query", qn, qf), ("key", kn, kf), ("value", vn, vf))
        ):
            gather_blocks(places, name, near, far, held)
            w[i] = to_pairs(held)

    left = x[...]
    q[...] = (dot(left, w[0]) + bias[0:1, :]).astype(LOW)
    k[...] = dot(left, w[1]).astype(LOW)
    v[...] = (dot(left, w[2]) + bias[1:2, :]).astype(LOW)


def project(places, tokens, bias, q_parts, k_parts, v_parts):
    step = 256
    args = (tokens, bias, *q_parts, *k_parts, *v_parts)
    return call(
        project_kernel,
        "project",
        (LEN // step,),
        [pl.BlockSpec((step, D), lambda i, places: (places[0] * (LEN // step) + i, 0))]
        + [whole(a) for a in args[1:]],
        [rows(step, 384)] * 3 + [pl.BlockSpec((3, D, 384), lambda *_: (0, 0, 0))],
        [shape((LEN, 384), LOW)] * 3 + [shape((3, D, 384), LOW)],
        [pltpu.VMEM((2 * BLOCKS, BLOCK_ROWS, 192), LOW)],
        places,
        args,
        2 * LEN * D * 1152,
    )


def first_of_pair():
    return lax.broadcasted_iota(jnp.int32, (1, 128), 1) < HD


def attend_kernel(places, q_ref, k_ref, v_ref, o_ref, inv_ref, p_ref, vx):
    first = first_of_pair()
    zero, one = jnp.zeros((), LOW), jnp.ones((), LOW)
    k = k_ref[...]
    v = v_ref[...]
    n = k.shape[0]
    vx[0:n, 0:128] = jnp.where(first, v, zero)
    vx[n : 2 * n, 0:128] = jnp.where(first, zero, v)
    vx[0:n, 128:256] = jnp.broadcast_to(jnp.where(first, one, zero), (n, 128))
    vx[n : 2 * n, 128:256] = jnp.broadcast_to(jnp.where(first, zero, one), (n, 128))
    step = 256
    for i in range(n // step):
        at = pl.ds(i * step, step)
        q = q_ref[at, :]
        result = None
        for head in range(2):
            mine = jnp.where(first, q, zero) if head == 0 else jnp.where(first, zero, q)
            score = dot_nt(mine, k)
            top = jnp.max(score, axis=1, keepdims=True)
            weight = jnp.exp2((score - top) * (HD**-0.5 * LOG2_E)).astype(LOW)
            p_ref[head, at, :] = weight
            part = dot(weight, vx[head * n : (head + 1) * n, :])
            result = part if result is None else result + part
        inv = 1.0 / result[:, 128:256]
        inv_ref[at, :] = inv
        o_ref[at, :] = (result[:, 0:128] * inv).astype(LOW)


def attend(places, q, k, v):
    pair = pl.BlockSpec((LEN, 128), lambda i, *_: (0, i))
    return call(
        attend_kernel,
        "attend_forward",
        (3,),
        [pair] * 3,
        [pair, pair, pl.BlockSpec((2, LEN, LEN), lambda i, *_: (i, 0, 0))],
        [shape((LEN, 384), LOW), shape((LEN, 384), WIDE), shape((6, LEN, LEN), LOW)],
        [pltpu.VMEM((2 * LEN, 256), LOW)],
        places,
        (q, k, v),
        4 * 6 * LEN * LEN * 256,
    )


def out_kernel(places, o, near, far, z, w, held):
    @pl.when(pl.program_id(0) == 0)
    def _():
        gather_blocks(places, "out", near, far, held)
        w[...] = to_pairs(held)

    z[...] = dot_nt(o[...], w[...]).astype(LOW)


def project_out(places, o, parts):
    step = 256
    return call(
        out_kernel,
        "project_out",
        (LEN // step,),
        [rows(step, 384)] + [whole(a) for a in parts],
        [rows(step, D), pl.BlockSpec((D, 384), lambda *_: (0, 0))],
        [shape((LEN, D), LOW), shape((D, 384), LOW)],
        [pltpu.VMEM((2 * BLOCKS, BLOCK_ROWS, 192), LOW)],
        places,
        (o, *parts),
        2 * LEN * D * 384,
    )


def normalize(hidden):
    centred = hidden - jnp.mean(hidden, axis=-1, keepdims=True)
    spread = lax.rsqrt(jnp.mean(centred * centred, axis=-1, keepdims=True) + EPS_NORM)
    return centred * spread, spread


def norm_back(grad_normed, normed, spread):
    return spread * (
        grad_normed
        - jnp.mean(grad_normed, axis=-1, keepdims=True)
        - normed * jnp.mean(grad_normed * normed, axis=-1, keepdims=True)
    )


def up_kernel(places, x, z, zp, vec, bias, near, far, m, slope, n1, rs1, low, w, held):
    @pl.when(pl.program_id(0) == 0)
    def _():
        gather_blocks(places, "up", near, far, held)
        w[:, 0:D] = held[0:BLOCKS].reshape(D, D)
        w[:, D : 2 * D] = held[BLOCKS : 2 * BLOCKS].reshape(D, D)

    total = z[...].astype(WIDE) + zp[...].astype(WIDE)
    normed, spread = normalize(x[...].astype(WIDE) + total + vec[4:5, :])
    n1[...] = normed
    rs1[...] = jnp.broadcast_to(spread, rs1.shape)
    middle = (normed * vec[0:1, :] + vec[1:2, :]).astype(LOW)
    low[...] = middle
    for c in range(4):
        at = pl.ds(c * 384, 384)
        u = dot(middle, w[:, at]) + bias[0:1, at]
        half = 0.5 * (1.0 + lax.erf(u * 0.7071067811865476))
        m[:, at] = (u * half).astype(LOW)
        slope[:, at] = (half + u * (jnp.exp(-0.5 * u * u) * 0.3989422804014327)).astype(LOW)


def feed_up(places, tokens, z, zp, vec, bias, parts):
    step = 256
    args = (tokens, z, zp, vec, bias, *parts)
    return call(
        up_kernel,
        "feed_up",
        (LEN // step,),
        [pl.BlockSpec((step, D), lambda i, places: (places[0] * (LEN // step) + i, 0))]
        + [rows(step, D)] * 2
        + [whole(a) for a in args[3:]],
        [rows(step, 2 * D)] * 2
        + [rows(step, D), rows(step, 128), rows(step, D)]
        + [pl.BlockSpec((D, 2 * D), lambda *_: (0, 0))],
        [shape((LEN, 2 * D), LOW)] * 2
        + [shape((LEN, D), WIDE), shape((LEN, 128), WIDE), shape((LEN, D), LOW)]
        + [shape((D, 2 * D), LOW)],
        [pltpu.VMEM((2 * BLOCKS, BLOCK_ROWS, D), LOW)],
        places,
        args,
        2 * LEN * D * 2 * D,
    )


def down_kernel(places, m, near, far, f, w, held):
    @pl.when(pl.program_id(0) == 0)
    def _():
        gather_blocks(places, "down", near, far, held)
        w[:, 0:D] = held[0:BLOCKS].reshape(D, D)
        w[:, D : 2 * D] = held[BLOCKS : 2 * BLOCKS].reshape(D, D)

    f[...] = dot_nt(m[...], w[...]).astype(LOW)


def feed_down(places, m, parts):
    step = 256
    return call(
        down_kernel,
        "feed_down",
        (LEN // step,),
        [rows(step, 2 * D)] + [whole(a) for a in parts],
        [rows(step, D), pl.BlockSpec((D, 2 * D), lambda *_: (0, 0))],
        [shape((LEN, D), LOW), shape((D, 2 * D), LOW)],
        [pltpu.VMEM((2 * BLOCKS, BLOCK_ROWS, D), LOW)],
        places,
        (m, *parts),
        2 * LEN * D * 2 * D,
    )


def turn_kernel(
    places, facts, n1, f, fp, cot, vec, pool_a, pool_b, classes, bias, y, dh2, low, sums, ramp, pool
):
    step = pl.program_id(0)
    middle = n1[...] * vec[0:1, :] + vec[1:2, :]
    total = f[...].astype(WIDE) + fp[...].astype(WIDE)
    normed, spread = normalize(middle + total + vec[5:6, :])
    result = normed * vec[2:3, :] + vec[3:4, :]
    y[...] = result.astype(LOW)
    grad = cot[...].astype(WIDE) * facts[2]
    dh2[...] = grad

    @pl.when(step == 0)
    def _():
        sums[...] = jnp.zeros_like(sums)
        half = D // 2
        own = places[0 + 1 + 2 * BLOCKS * len(NAMES)]

        @pl.when(own == 0)
        def _():
            pool[:, 0:half] = pool_a[...]
            pool[:, half:D] = pool_b[...]

        @pl.when(own == 1)
        def _():
            pool[:, 0:half] = pool_b[...]
            pool[:, half:D] = pool_a[...]

        count = 16
        head = result[0:count, :].astype(LOW)
        pooled = jnp.tanh(dot(head, pool[...]) + vec[6:7, :])
        pooled_low = pooled.astype(LOW)
        lane = lax.broadcasted_iota(jnp.int32, (count, 128), 1)
        row = lax.broadcasted_iota(jnp.int32, (count, 128), 0)
        valid = lane < 3
        logits = dot(pooled_low, classes[...]) + bias[0:1, :]
        top = jnp.max(jnp.where(valid, logits, -jnp.inf), axis=1, keepdims=True)
        shifted = logits - top
        log_sum = jnp.log(
            jnp.sum(jnp.where(valid, jnp.exp(shifted), 0.0), axis=1, keepdims=True)
        )
        log_probs = jnp.where(valid, shifted - log_sum, 0.0)
        probs = jnp.where(valid, jnp.exp(log_probs), 0.0)
        live = facts[1]
        entropy = -live * jnp.sum(probs * log_probs, axis=1, keepdims=True)
        label = facts[0].astype(jnp.int32)
        onehot = jnp.where(lane == label, 1.0, 0.0)
        grad_logits = live * (probs - onehot) / facts[3]
        grad_logits = jnp.where(valid & (row == 0), grad_logits, 0.0).astype(LOW)
        grad_pre = (dot_nt(grad_logits, classes[...]) * (1.0 - pooled * pooled)).astype(LOW)
        grad_head = dot_nt(grad_pre, pool[...])
        dh2[0:count, :] = dh2[0:count, :] + grad_head
        sums[3:4, :] = grad_pre[0:1, :].astype(WIDE)
        of_class = dot_tn(grad_logits, pooled_low)
        sums[4:7, :] = of_class[0:3, :]
        last = jnp.where(lane == 3, entropy, grad_logits.astype(WIDE))
        sums[7:8, 0:128] = last[0:1, :]
        wide_row = lax.broadcasted_iota(jnp.int32, (count, D), 0)
        second = jnp.broadcast_to(grad_pre[0:1, :].astype(WIDE), (count, D))
        kept = jnp.where(wide_row == 0, head.astype(WIDE), 0.0)
        ramp[...] = jnp.where(wide_row == 1, second, kept).astype(LOW)

    grad = dh2[...]
    sums[0:1, :] += jnp.sum(grad * normed, axis=0, keepdims=True)
    sums[1:2, :] += jnp.sum(grad, axis=0, keepdims=True)
    back = norm_back(grad * vec[2:3, :], normed, spread)
    sums[2:3, :] += jnp.sum(back, axis=0, keepdims=True)
    dh2[...] = back
    low[...] = back.astype(LOW)


def turn(places, facts, n1, f, fp, cotangent, vec, pool_a, pool_b, classes, bias):
    step = 256
    args = (facts, n1, f, fp, cotangent, vec, pool_a, pool_b, classes, bias)
    return call(
        turn_kernel,
        "turn",
        (LEN // step,),
        [pl.BlockSpec(memory_space=pltpu.SMEM)]
        + [rows(step, D)] * 3
        + [pl.BlockSpec((step, D), lambda i, places: (places[0] * (LEN // step) + i, 0))]
        + [whole(a) for a in args[5:]],
        [rows(step, D)] * 3
        + [pl.BlockSpec((8, D), lambda *_: (0, 0)), pl.BlockSpec((16, D), lambda *_: (0, 0))],
        [shape((LEN, D), LOW), shape((LEN, D), WIDE), shape((LEN, D), LOW)]
        + [shape((8, D), WIDE), shape((16, D), LOW)],
        [pltpu.VMEM((D, D), LOW)],
        places,
        args,
        LEN * D * 60,
    )


def feed_back_kernel(places, dh2, slope, w_down, w_up, du, dx, sums):
    grad = dot(dh2[...], w_down[...]) * slope[...].astype(WIDE)
    grad = grad.astype(LOW)
    du[...] = grad
    dx[...] = dot_nt(grad, w_up[...]).astype(LOW)

    @pl.when(pl.program_id(0) == 0)
    def _():
        sums[...] = jnp.zeros_like(sums)

    sums[0:1, :] += jnp.sum(grad.astype(WIDE), axis=0, keepdims=True)


def feed_back(places, dh2, slope, w_down, w_up):
    step = 256
    args = (dh2, slope, w_down, w_up)
    return call(
        feed_back_kernel,
        "feed_back",
        (LEN // step,),
        [rows(step, D), rows(step, 2 * D), whole(w_down), whole(w_up)],
        [rows(step, 2 * D), rows(step, D), pl.BlockSpec((8, 2 * D), lambda *_: (0, 0))],
        [shape((LEN, 2 * D), LOW), shape((LEN, D), LOW), shape((8, 2 * D), WIDE)],
        [],
        places,
        args,
        4 * LEN * D * 2 * D,
    )


def feed_grad_kernel(name, places, left, right, near, far, held, turned):
    @pl.when(pl.program_id(0) == 0)
    def _():
        turned[...] = left[...].T

    side = pl.program_id(0)
    for c in range(3):
        at = pl.ds(c * 256, 256)
        part = dot(turned[...], right[:, at]).astype(LOW)
        held[pl.ds(pl.multiple_of(side * BLOCKS, BLOCKS), BLOCKS), :, at] = part.reshape(
            BLOCKS, BLOCK_ROWS, 256
        )

    @pl.when(side == 1)
    def _():
        scatter_blocks(places, name, held, near, far)


def feed_grad(places, name, left, right):
    return call(
        functools.partial(feed_grad_kernel, name),
        "feed_grad_" + name,
        (2,),
        [whole(left), pl.BlockSpec((LEN, D), lambda i, *_: (0, i))],
        [pl.BlockSpec((BLOCKS, BLOCK_ROWS, D), lambda *_: (0, 0, 0))] * 2,
        [shape((BLOCKS, BLOCK_ROWS, D), LOW)] * 2,
        [pltpu.VMEM((2 * BLOCKS, BLOCK_ROWS, D), LOW), pltpu.VMEM((D, LEN), LOW)],
        places,
        (left, right),
        2 * LEN * D * 2 * D,
    )


def mid_kernel(places, dh2, dx, dxp, n1, rs1, vec, w_out, dh1, low, do, sums):
    @pl.when(pl.program_id(0) == 0)
    def _():
        sums[...] = jnp.zeros_like(sums)

    total = dx[...].astype(WIDE) + dxp[...].astype(WIDE)
    grad = dh2[...] + total
    normed = n1[...]
    sums[0:1, :] += jnp.sum(grad * normed, axis=0, keepdims=True)
    sums[1:2, :] += jnp.sum(grad, axis=0, keepdims=True)
    back = norm_back(grad * vec[0:1, :], normed, rs1[:, 0:1])
    sums[2:3, :] += jnp.sum(back, axis=0, keepdims=True)
    dh1[...] = back
    back_low = back.astype(LOW)
    low[...] = back_low
    do[...] = dot(back_low, w_out[...]).astype(LOW)


def mid(places, dh2, dx, dxp, n1, rs1, vec, w_out):
    step = 256
    args = (dh2, dx, dxp, n1, rs1, vec, w_out)
    return call(
        mid_kernel,
        "middle_back",
        (LEN // step,),
        [rows(step, D)] * 4 + [rows(step, 128), whole(vec), whole(w_out)],
        [rows(step, D)] * 2 + [rows(step, 384), pl.BlockSpec((8, D), lambda *_: (0, 0))],
        [shape((LEN, D), WIDE), shape((LEN, D), LOW), shape((LEN, 384), LOW), shape((8, D), WIDE)],
        [],
        places,
        args,
        2 * LEN * D * 384,
    )


def attend_back_kernel(
    places, q_ref, k_ref, v_ref, do_ref, inv_ref, p_ref, dq_ref, dk_ref, dv_ref, ds_ref, held
):
    first = first_of_pair()
    zero = jnp.zeros((), LOW)
    n = k_ref.shape[0]
    k = k_ref[...]
    v = v_ref[...]
    k_own = [jnp.where(first, k, zero), jnp.where(first, zero, k)]
    scaled = (do_ref[...].astype(WIDE) * inv_ref[...]).astype(LOW)
    held[...] = scaled
    step = 256
    for i in range(n // step):
        at = pl.ds(i * step, step)
        d = held[at, :]
        total = None
        for head in range(2):
            mine = jnp.where(first, d, zero) if head == 0 else jnp.where(first, zero, d)
            grad_weight = dot_nt(mine, v)
            weight = p_ref[head, at, :].astype(WIDE)
            product = weight * grad_weight
            inner = jnp.sum(product, axis=1, keepdims=True)
            inner = inner * inv_ref[at, pl.ds(HD * head, 1)]
            grad_score = (product - weight * inner).astype(LOW)
            ds_ref[head, at, :] = grad_score
            part = dot(grad_score, k_own[head])
            total = part if total is None else total + part
        dq_ref[at, :] = (total * HD**-0.5).astype(LOW)
    scaled_t = scaled.T
    q_t = q_ref[...].T
    grad_v = jnp.concatenate(
        [dot(scaled_t[0:HD], p_ref[0]), dot(scaled_t[HD : 2 * HD], p_ref[1])], axis=0
    )
    dv_ref[...] = grad_v.T.astype(LOW)
    grad_k = jnp.concatenate(
        [dot(q_t[0:HD], ds_ref[0]), dot(q_t[HD : 2 * HD], ds_ref[1])], axis=0
    )
    dk_ref[...] = (grad_k * HD**-0.5).T.astype(LOW)


def attend_back(places, q, k, v, do, inv, p):
    pair = pl.BlockSpec((LEN, 128), lambda i, *_: (0, i))
    return call(
        attend_back_kernel,
        "attend_backward",
        (3,),
        [pair] * 5 + [pl.BlockSpec((2, LEN, LEN), lambda i, *_: (i, 0, 0))],
        [pair] * 3,
        [shape((LEN, 384), LOW)] * 3,
        [pltpu.VMEM((2, LEN, LEN), LOW), pltpu.VMEM((LEN, 128), LOW)],
        places,
        (q, k, v, do, inv, p),
        8 * 6 * LEN * LEN * 256,
    )


def narrow_grad_kernel(names, places, left, *refs):
    count = len(names)
    rights, outs, sums = refs[:count], refs[count : 3 * count], refs[3 * count]
    held, turned = refs[3 * count + 1 :]
    turned[...] = left[...].T
    for i, name in enumerate(names):
        from_pairs(dot(turned[...], rights[i][...]).astype(LOW), held)
        scatter_blocks(places, name, held, outs[2 * i], outs[2 * i + 1])
        sums[i : i + 1, :] = jnp.sum(rights[i][...].astype(WIDE), axis=0, keepdims=True)


def narrow_grad(places, names, left, rights, from_side):
    count = len(names)
    own = pl.BlockSpec((LEN, D), (lambda i, places: (places[0], 0)) if from_side else (lambda *_: (0, 0)))
    half = pl.BlockSpec((BLOCKS, BLOCK_ROWS, 192), lambda *_: (0, 0, 0))
    return call(
        functools.partial(narrow_grad_kernel, names),
        "narrow_grad_" + names[0],
        (1,),
        [own] + [whole(a) for a in rights],
        [half] * (2 * count) + [pl.BlockSpec((8, 384), lambda *_: (0, 0))],
        [shape((BLOCKS, BLOCK_ROWS, 192), LOW)] * (2 * count) + [shape((8, 384), WIDE)],
        [pltpu.VMEM((2 * BLOCKS, BLOCK_ROWS, 192), LOW), pltpu.VMEM((D, LEN), LOW)],
        places,
        (left, *rights),
        2 * LEN * D * 384 * count,
    )


def input_kernel(places, dq, dk, dv, w, out):
    total = dot_nt(dq[...], w[0]) + dot_nt(dk[...], w[1]) + dot_nt(dv[...], w[2])
    out[...] = total.astype(LOW)


def input_grad(places, dq, dk, dv, w):
    step = 256
    return call(
        input_kernel,
        "input_grad",
        (LEN // step,),
        [rows(step, 384)] * 3 + [whole(w)],
        [rows(step, D)],
        [shape((LEN, D), LOW)],
        [],
        places,
        (dq, dk, dv, w),
        2 * LEN * D * 1152,
    )[0]


def both_sequences(links, mine):
    half = LEN // 2
    own_half = lax.dynamic_slice_in_dim(mine, links.core * half, half, 0)
    other_half = links.swap(own_half, SIDE)
    last_half = links.swap(other_half, CORE)
    other = jnp.where(
        links.core == 0,
        jnp.concatenate([other_half, last_half], axis=0),
        jnp.concatenate([last_half, other_half], axis=0),
    )
    return jnp.where(
        links.side == 0,
        jnp.concatenate([mine, other], axis=0),
        jnp.concatenate([other, mine], axis=0),
    )


def per_device(
    dp_count,
    mp_count,
    tokens,
    cotangent,
    exit_layer,
    labels,
    qkv_weight,
    qkv_first,
    qkv_second,
    out_weight,
    out_first,
    out_second,
    up_weight,
    up_first,
    up_second,
    down_weight,
    down_first,
    down_second,
    pool_weight,
    pool_first,
    pool_second,
    qv_bias,
    qv_first,
    qv_second,
    up_bias,
    upb_first,
    upb_second,
    layer_vectors,
    vector_first,
    vector_second,
    class_weight,
    class_first,
    class_second,
):
    links = Links(dp_count, mp_count)
    side, core = links.side, links.core

    places = jnp.concatenate([side[None], links.places(), core[None]]).astype(jnp.int32)

    qkv_low = qkv_weight.astype(LOW)
    q_parts = links.spread(qkv_low[:, 0], "query")
    k_parts = links.spread(qkv_low[:, 1], "key")
    v_parts = links.spread(qkv_low[:, 2], "value")
    biases = links.both_sides(
        jnp.concatenate([qv_bias.reshape(1, 384), up_bias.reshape(1, D)], axis=1)
    )
    qv_pairs = jnp.stack(
        [
            jnp.concatenate(
                [
                    biases[0, 192 * i : 192 * i + 128],
                    biases[1, 192 * i : 192 * i + 128],
                    biases[0, 192 * i + 128 : 192 * i + 192],
                    biases[1, 192 * i + 128 : 192 * i + 192],
                ]
            )
            for i in range(2)
        ]
    )
    up_bias_both = biases[:, 384:].reshape(1, 2 * D)
    live_mask = (exit_layer >= LAYER).astype(WIDE)
    carry_mask = (exit_layer > LAYER).astype(WIDE)
    live_total = links.total_over(
        jnp.broadcast_to(jnp.sum(live_mask), (8, 128)), with_side=False
    )[0, 0]
    out_parts = links.spread(out_weight.T.astype(LOW), "out")
    up_parts = links.spread(up_weight.astype(LOW), "up")
    down_parts = links.spread(down_weight.T.astype(LOW), "down")
    pool_low = lax.dynamic_slice_in_dim(pool_weight.astype(LOW), core * (D // 2), D // 2, 1)
    pool_mine = links.rows_of(pool_low)
    pool_other = links.swap(pool_mine, CORE)

    q, k, v, w_qkv = project(places, tokens, qv_pairs, q_parts, k_parts, v_parts)
    o, inv, p = attend(places, q, k, v)
    z, w_out = project_out(places, o, out_parts)
    zp = links.swap(z, CORE)
    m, slope, n1, rs1, middle_low, w_up = feed_up(
        places, tokens, z, zp, layer_vectors, up_bias_both, up_parts
    )
    f, w_down = feed_down(places, m, down_parts)
    fp = links.swap(f, CORE)
    classes = jnp.pad(class_weight[:D].astype(LOW), ((0, 0), (0, 125)))
    class_bias = jnp.pad(class_weight[D:], ((0, 0), (0, 125)))
    facts = jnp.stack(
        [
            labels.astype(WIDE)[side],
            live_mask[side],
            carry_mask[side],
            live_total,
        ]
    )
    y, dh2, dh2_low, turn_sums, ramp = turn(
        places, facts, n1, f, fp, cotangent, layer_vectors, pool_mine, pool_other, classes, class_bias
    )
    result = both_sequences(links, y)

    du, dx, up_sums = feed_back(places, dh2_low, slope, w_down, w_up)
    dxp = links.swap(dx, CORE)
    down_near, down_far = feed_grad(places, "down", dh2_low, m)
    grad_down = links.fold(down_near, down_far, "down")
    up_near, up_far = feed_grad(places, "up", middle_low, du)
    grad_up = links.fold(up_near, up_far, "up")
    dh1, dh1_low, do, mid_sums = mid(places, dh2, dx, dxp, n1, rs1, layer_vectors, w_out)
    out_near, out_far, _ = narrow_grad(places, ("out",), dh1_low, (o,), False)
    grad_out = links.fold(out_near, out_far, "out")
    sums = links.total_over(
        jnp.concatenate([turn_sums, mid_sums[0:3], up_sums[0].reshape(2, D)], axis=0),
        with_side=True,
    )
    ramps = links.rows_of(links.both_sides(ramp[None]))
    dq, dk, dv = attend_back(places, q, k, v, do, inv, p)
    token_part = input_grad(places, dq, dk, dv, w_qkv)
    token_other = links.swap(token_part, CORE)
    qn, qf, kn, kf, vn, vf, pair_sums = narrow_grad(
        places, ("query", "key", "value"), tokens, (dq, dk, dv), True
    )
    grad_q = links.fold(qn, qf, "query")
    grad_k = links.fold(kn, kf, "key")
    grad_v = links.fold(vn, vf, "value")
    pair_total = links.total_over(pair_sums, with_side=True)
    token_sum = token_part.astype(WIDE) + token_other.astype(WIDE)
    tokens_grad = both_sequences(links, (dh1 + token_sum).astype(LOW))

    own_rows = lax.dynamic_slice_in_dim(
        ramps[:, 0, :], links.dp * (D // dp_count), D // dp_count, 1
    )
    grad_pool = lax.dot_general(
        own_rows, ramps[:, 1, :], (((0,), (0,)), ((), ())), preferred_element_type=WIDE
    )
    vector_sum = jnp.stack([sums[8], sums[9], sums[0], sums[1], sums[10], sums[2], sums[3]])
    class_sum = jnp.concatenate([sums[4:7].T, sums[7:8, 0:3]], axis=0)
    upb_sum = lax.dynamic_slice_in_dim(sums, 11 + side, 1, 0)[0]
    pair_rows = jnp.stack([pair_total[0], pair_total[2]])
    bias_sum = jnp.concatenate(
        [
            lax.dynamic_slice_in_dim(pair_rows, side * 128, 128, 1),
            lax.dynamic_slice_in_dim(pair_rows, 256 + side * 64, 64, 1),
        ],
        axis=1,
    )
    grad_qkv = jnp.stack([grad_q, grad_k, grad_v], axis=1)

    qkv_new, qkv_first_new, qkv_second_new = adamw(
        qkv_weight, qkv_first, qkv_second, grad_qkv, RATE * D ** (-0.5), DECAY
    )
    out_new, out_first_new, out_second_new = adamw(
        out_weight, out_first, out_second, grad_out.T, RATE * max(1, 2 * D // LEN) ** (-0.5), DECAY
    )
    up_new, up_first_new, up_second_new = adamw(
        up_weight, up_first, up_second, grad_up, RATE * D ** (-0.5), DECAY
    )
    down_new, down_first_new, down_second_new = adamw(
        down_weight, down_first, down_second, grad_down.T, RATE * FF ** (-0.5), DECAY
    )
    pool_new, pool_first_new, pool_second_new = adamw(
        pool_weight, pool_first, pool_second, grad_pool, RATE * D ** (-0.5), DECAY
    )
    qv_new, qv_first_new, qv_second_new = adamw(
        qv_bias, qv_first, qv_second, bias_sum, VECTOR_RATE, 0.0
    )
    upb_new, upb_first_new, upb_second_new = adamw(
        up_bias, upb_first, upb_second, upb_sum, VECTOR_RATE, 0.0
    )
    vector_new, vector_first_new, vector_second_new = adamw(
        layer_vectors, vector_first, vector_second, vector_sum, VECTOR_RATE, 0.0
    )
    class_new, class_first_new, class_second_new = adamw(
        class_weight, class_first, class_second, class_sum, RATE * (D // 4) ** (-0.5), DECAY
    )
    return (
        result,
        tokens_grad,
        sums[7, 3] / live_total,
        qkv_new,
        qkv_first_new,
        qkv_second_new,
        qkv_new.astype(LOW),
        out_new,
        out_first_new,
        out_second_new,
        out_new.astype(LOW),
        up_new,
        up_first_new,
        up_second_new,
        up_new.astype(LOW),
        down_new,
        down_first_new,
        down_second_new,
        down_new.astype(LOW),
        pool_new,
        pool_first_new,
        pool_second_new,
        pool_new.astype(LOW),
        qv_new,
        qv_first_new,
        qv_second_new,
        upb_new,
        upb_first_new,
        upb_second_new,
        vector_new,
        vector_first_new,
        vector_second_new,
        class_new,
        class_first_new,
        class_second_new,
    )


def solution(mesh):
    in_specs = (
        P("dp", None),
        P("dp", None),
        P("dp"),
        P("dp"),
        P("dp", None, "mp"),
        P("dp", None, "mp"),
        P("dp", None, "mp"),
        P("mp", "dp"),
        P("mp", "dp"),
        P("mp", "dp"),
        P("dp", "mp"),
        P("dp", "mp"),
        P("dp", "mp"),
        P("mp", "dp"),
        P("mp", "dp"),
        P("mp", "dp"),
        P("dp", None),
        P("dp", None),
        P("dp", None),
        P(None, "mp"),
        P(None, "mp"),
        P(None, "mp"),
        P("mp"),
        P("mp"),
        P("mp"),
        P(),
        P(),
        P(),
        P(),
        P(),
        P(),
    )
    out_specs = (
        P("dp", None),
        P("dp", None),
        P(),
        P("dp", None, "mp"),
        P("dp", None, "mp"),
        P("dp", None, "mp"),
        P("dp", None, "mp"),
        P("mp", "dp"),
        P("mp", "dp"),
        P("mp", "dp"),
        P("mp", "dp"),
        P("dp", "mp"),
        P("dp", "mp"),
        P("dp", "mp"),
        P("dp", "mp"),
        P("mp", "dp"),
        P("mp", "dp"),
        P("mp", "dp"),
        P("mp", "dp"),
        P("dp", None),
        P("dp", None),
        P("dp", None),
        P("dp", None),
        P(None, "mp"),
        P(None, "mp"),
        P(None, "mp"),
        P("mp"),
        P("mp"),
        P("mp"),
        P(),
        P(),
        P(),
        P(),
        P(),
        P(),
    )
    one_device = functools.partial(per_device, mesh.shape["dp"], mesh.shape["mp"])
    return jax.shard_map(
        one_device, mesh=mesh, in_specs=in_specs, out_specs=out_specs, check_vma=False
    )
```

```python
import functools

import jax
import jax.numpy as jnp
import numpy as np
from jax import lax
from jax.experimental import pallas as pl
from jax.experimental.pallas import tpu as pltpu
from jax.sharding import PartitionSpec as P

D = 768
HD = 64
FF = 3072
LAYER = 6
STEP = 10
LEN = 1024


EPS_NORM = 1e-06
BETA_ONE = 0.9
BETA_TWO = 0.98
EPS_ADAM = 1e-08
DECAY = 0.01
RATE = 0.8
VECTOR_RATE = 0.3

LOW = jnp.bfloat16
WIDE = jnp.float32
LOG2_E = 1.4426950408889634
MIB = 2**20
COST_SCALE = 16

CORE, SIDE, X_BIT, Z_LOW, Z_HIGH = 1, 2, 4, 8, 16
BLOCKS = 8
BLOCK_ROWS = D // BLOCKS
PART_ROWS = BLOCK_ROWS // 2
MARKS_AT, MARKED_WIDTH = 768, 896
ACROSS = ((Z_HIGH, Z_LOW, X_BIT, SIDE), (Z_HIGH, Z_LOW, SIDE, X_BIT))
ALONG = ((Z_HIGH, Z_LOW, SIDE, X_BIT), (Z_HIGH, SIDE, X_BIT, Z_LOW))
Z_LINE = (Z_HIGH, Z_LOW, Z_HIGH | Z_LOW)
ROUTES = (ACROSS, ALONG)


def dot(left, right):
    return lax.dot_general(
        left, right, (((1,), (0,)), ((), ())), preferred_element_type=WIDE
    )


def dot_nt(left, right):
    return lax.dot_general(
        left, right, (((1,), (1,)), ((), ())), preferred_element_type=WIDE
    )


def dot_tn(left, right):
    return lax.dot_general(
        left, right, (((0,), (0,)), ((), ())), preferred_element_type=WIDE
    )


def adamw(weight, first, second, grad, rate, decay):
    first_new = BETA_ONE * first + (1.0 - BETA_ONE) * grad
    second_new = BETA_TWO * second + (1.0 - BETA_TWO) * grad * grad
    first_hat = first_new / (1.0 - BETA_ONE**STEP)
    second_hat = second_new / (1.0 - BETA_TWO**STEP)
    weight_new = weight - rate * (first_hat / (jnp.sqrt(second_hat) + EPS_ADAM) + decay * weight)
    return (weight_new, first_new, second_new)


class Links:
    def __init__(self, dp_count, mp_count):
        self.dp_count = dp_count
        self.total = dp_count * mp_count
        self.cube = dp_count == BLOCKS
        self.dp = lax.axis_index("dp").astype(jnp.int32)
        mp = lax.axis_index("mp").astype(jnp.int32)
        self.side = mp // 2
        self.core = mp % 2

    def swap(self, value, bit):
        pairs = [(i, i ^ bit) for i in range(self.total)]
        return lax.ppermute(value, ("dp", "mp"), pairs)

    def places(self):
        flips = []
        for order in sum(ROUTES, ()):
            for j in range(2 * BLOCKS):
                if self.cube:
                    bits = 0
                    for k, bit in enumerate(order):
                        bits ^= bit if (j >> k) & 1 else 0
                    flips.append((bits // SIDE & 1, bits // X_BIT))
                else:
                    flips.append((j // BLOCKS, j % BLOCKS))
        flips = np.array(flips, np.int32)
        mine = self.dp if self.cube else 0
        return (self.side ^ flips[:, 0]) * BLOCKS + (mine ^ flips[:, 1])

    def spread(self, share):
        return (Spread if self.cube else WholeSpread)(self, share)

    def fold(self, halves, route):
        return (Fold if self.cube else WholeFold)(self, halves, route)


class Spread:
    def __init__(self, links, share):
        self.links = links
        self.held = [share[None]]
        self.last = None
        self.round = 0

    def step(self, *others):
        links = self.links
        if others:
            (self.held, self.last), *_ = lax.optimization_barrier(((self.held, self.last), *others))
        if self.round == 0:
            self.last = [links.swap(self.held[0], bits) for bits in Z_LINE]
        elif self.round == 1:
            line = [self.held[0], *self.last]
            at = (slice(0, PART_ROWS), slice(PART_ROWS, BLOCK_ROWS))
            self.held = [jnp.concatenate([a[:, i] for a in line], axis=0) for i in at]
        else:
            self.held = [
                jnp.concatenate([mine, other], axis=0)
                for mine, other in zip(self.held, self.last, strict=True)
            ]
        if self.round:
            self.last = [
                links.swap(part, ACROSS[i][self.round + 1]) for i, part in enumerate(self.held)
            ]
        self.round += 1
        return tuple(self.held)

    def halves(self):
        return (self.held[0], self.last[0], self.held[1], self.last[1])


class WholeSpread:
    def __init__(self, links, share):
        self.last = ()
        near = lax.all_gather(share, "dp", axis=0, tiled=True)
        near = near.reshape(BLOCKS, BLOCK_ROWS, share.shape[1])
        far = links.swap(near, SIDE)
        self.parts = (
            near[:, :PART_ROWS],
            far[:, :PART_ROWS],
            near[:, PART_ROWS:],
            far[:, PART_ROWS:],
        )

    def step(self, *others):
        return ()

    def halves(self):
        return self.parts


class Fold:
    def __init__(self, links, halves, route):
        self.links = links
        self.route = route
        self.parts = [[halves[0]], [halves[2]]]
        self.far = [halves[1], halves[3]]
        self.joined = []
        self.round = 0

    def step(self, *others, vmem=60):
        links, k = self.links, 3 - self.round
        if others:
            (self.parts, self.joined, self.far), *_ = lax.optimization_barrier(
                ((self.parts, self.joined, self.far), *others)
            )
        if self.route is ACROSS and self.round == 2:
            sent = fold_add(self.parts, [], (1, 2, 3), False, vmem)
            self.joined = [links.swap(a, bits) for a, bits in zip(sent, Z_LINE, strict=True)]
        else:
            if self.round == 0:
                sent = self.far
            else:
                sent = fold_add(self.parts, [], range(2**k, 2 ** (k + 1)), True, vmem)
            for i, order in enumerate(self.route):
                self.parts[i].append(links.swap(sent[i], order[k]))
        self.round += 1
        return tuple(sent)

    def pieces(self):
        return (self.parts[0], self.parts[1], self.joined)


class WholeFold:
    def __init__(self, links, halves, route):
        near, far = (
            jnp.concatenate([halves[i], halves[i + 2]], axis=1).reshape(D, -1) for i in range(2)
        )
        total = near.astype(WIDE) + links.swap(far, SIDE).astype(WIDE)
        self.share = lax.psum_scatter(total, "dp", scatter_dimension=0, tiled=True)
        if self.share.shape[1] == MARKED_WIDTH:
            marks = lax.psum(total[0:8, MARKS_AT:], "dp")
            self.share = self.share.at[0:8, MARKS_AT:].set(marks)

    def step(self, *others, vmem=60):
        return ()

    def pieces(self):
        return ([], [], [self.share])


def sum_pieces(refs, counts):
    def add(group):
        return sum(ref[0].astype(WIDE) for ref in group)

    first, second, joined = counts
    if first:
        total = jnp.concatenate(
            [add_marked(refs[:first]), add_marked(refs[first : first + second])], axis=0
        )
        if joined:
            total = total + add(refs[first + second :])
        return total
    return refs[0][...]


def add_marked(refs):
    total = sum(ref[0].astype(WIDE) for ref in refs)
    if total.shape[1] != MARKED_WIDTH:
        return total
    marks = refs[0][0][:, MARKS_AT:].astype(WIDE)
    for ref in refs[1:]:
        marks = marks.astype(LOW).astype(WIDE) + ref[0][:, MARKS_AT:].astype(WIDE)
    return jnp.concatenate([total[:, :MARKS_AT], marks], axis=1)


def fold_add_kernel(counts, apart, *refs):
    first = counts[0]
    total = sum(counts)
    ins, outs = refs[:total], refs[total:]
    if apart:
        outs[0][0] = add_marked(ins[:first]).astype(LOW)
        outs[1][0] = add_marked(ins[first:]).astype(LOW)
    else:
        block = sum_pieces(ins, counts).astype(LOW)
        for i, out in enumerate(outs):

            @pl.when(pl.program_id(0) == i)
            def _(out=out):
                out[0] = block


def fold_add(parts, joined, blocks, apart, vmem):
    counts = (len(parts[0]), len(parts[1]), len(joined))
    args = [*parts[0], *parts[1], *joined]
    width = args[0].shape[2]
    low, count = blocks[0], len(blocks)
    if apart:
        outs = [shape((count, PART_ROWS, width), LOW)] * 2
        out_specs = [pl.BlockSpec((1, PART_ROWS, width), lambda i: (i, 0, 0))] * 2
    else:
        outs = [shape((1, BLOCK_ROWS, width), LOW)] * count
        out_specs = [pl.BlockSpec((1, BLOCK_ROWS, width), lambda i: (0, 0, 0))] * count
    return pl.pallas_call(
        functools.partial(fold_add_kernel, counts, apart),
        grid=(count,),
        in_specs=[pl.BlockSpec((1, a.shape[1], width), lambda i: (low + i, 0, 0)) for a in args],
        out_specs=out_specs,
        out_shape=outs,
        compiler_params=pltpu.CompilerParams(vmem_limit_bytes=vmem * MIB),
        cost_estimate=pl.CostEstimate(
            flops=count * BLOCK_ROWS * width, bytes_accessed=count * width, transcendentals=0
        ),
        name="fold_add",
    )(*args)


class Total:
    def __init__(self, links, value):
        self.links = links
        self.value = value
        self.bits = [Z_LOW, Z_HIGH, X_BIT, SIDE]
        self.last = None

    def step(self, *others):
        links = self.links
        if others:
            (self.value, self.last), *_ = lax.optimization_barrier(
                ((self.value, self.last), *others)
            )
        self.value = self.result()
        if not links.cube and len(self.bits) == 4:
            self.bits = [SIDE]
            self.value = lax.psum(self.value, "dp")
        if not self.bits:
            return ()
        self.last = links.swap(self.value, self.bits.pop(0))
        return (self.value,)

    def result(self):
        return self.value if self.last is None else self.value + self.last


def after(value, *others):
    return lax.optimization_barrier((value, *others))[0]


def call(kernel, name, grid, in_specs, out_specs, out_shape, scratch, places, args, flops, vmem=24, aliases=None):
    moved = sum(a.size * a.dtype.itemsize for a in args)
    moved += sum(int(np.prod(s.shape)) * np.dtype(s.dtype).itemsize for s in out_shape)
    return pl.pallas_call(
        kernel,
        out_shape=out_shape,
        grid_spec=pltpu.PrefetchScalarGridSpec(
            num_scalar_prefetch=1,
            grid=grid,
            in_specs=in_specs,
            out_specs=out_specs,
            scratch_shapes=scratch,
        ),
        input_output_aliases=aliases or {},
        compiler_params=pltpu.CompilerParams(vmem_limit_bytes=vmem * MIB),
        cost_estimate=pl.CostEstimate(
            flops=int(flops) // COST_SCALE, bytes_accessed=int(moved) // COST_SCALE, transcendentals=0
        ),
        name=name,
    )(places, *args)


def whole(array):
    return pl.BlockSpec(array.shape, lambda *_: (0,) * len(array.shape))


def rows(count, width):
    return pl.BlockSpec((count, width), lambda i, *_: (i, 0))


def shape(dims, kind):
    return jax.ShapeDtypeStruct(dims, kind)


def gather_blocks(places, halves, held, route=ACROSS):
    for i in range(2):
        for j in range(2 * BLOCKS):
            source = halves[2 * i + j // BLOCKS]
            target = places[1 + 2 * BLOCKS * (2 * ROUTES.index(route) + i) + j]
            held[target, i * PART_ROWS : (i + 1) * PART_ROWS, :] = source[j % BLOCKS]


def scatter_blocks(places, held, halves, route=ACROSS):
    for i in range(2):
        for j in range(2 * BLOCKS):
            target = halves[2 * i + j // BLOCKS]
            source = places[1 + 2 * BLOCKS * (2 * ROUTES.index(route) + i) + j]
            target[j % BLOCKS] = held[source, i * PART_ROWS : (i + 1) * PART_ROWS, :]


CORE_AT = 1 + 4 * BLOCKS * len(ROUTES)
SLOT_AT = CORE_AT + 1


def side_of(held, side, at, width):
    return held[side * BLOCKS : (side + 1) * BLOCKS, :, at : at + width].reshape(D, width)


def to_pairs(held, wide_at, narrow_at):
    return jnp.concatenate(
        [side_of(held, side, wide_at, 128) for side in range(2)]
        + [side_of(held, side, narrow_at, 64) for side in range(2)],
        axis=1,
    )


def from_pairs(value, held, wide_at, narrow_at):
    for side in range(2):
        at = slice(side * BLOCKS, (side + 1) * BLOCKS)
        wide = value[:, 128 * side : 128 * (side + 1)]
        held[at, :, wide_at : wide_at + 128] = wide.reshape(BLOCKS, BLOCK_ROWS, 128)
        narrow = value[:, 256 + 64 * side : 320 + 64 * side]
        held[at, :, narrow_at : narrow_at + 64] = narrow.reshape(BLOCKS, BLOCK_ROWS, 64)


def half_shapes(width):
    return [shape((BLOCKS, PART_ROWS, width), LOW)] * 4


def half_specs(width):
    return [pl.BlockSpec((BLOCKS, PART_ROWS, width), lambda *_: (0, 0, 0))] * 4


def held_blocks(width):
    return pltpu.VMEM((2 * BLOCKS, BLOCK_ROWS, width), LOW)


def pack_first_kernel(w, out):
    wide = [w[i][:, :128] for i in range(3)]
    narrow = [w[i][:, 128:] for i in range(3)]
    out[...] = jnp.concatenate(wide + narrow, axis=1).astype(LOW)


def pack_first(qkv):
    return pl.pallas_call(
        pack_first_kernel,
        out_shape=shape((qkv.shape[1], 576), LOW),
        name="pack_first",
    )(qkv)


def pack_kernel(places, exit_layer, up, out, down, pool, qv, upb, up_out, down_pool, biases):
    up_out[:, 0:D] = up[...].astype(LOW)
    up_out[:, D : D + 192] = out[...].T.astype(LOW)
    down_pool[:, 0:D] = down[...].astype(LOW)
    quarter = 2 * places[CORE_AT] + places[0]
    mine = jnp.zeros((pool.shape[0], 192), WIDE)
    for i in range(4):
        mine = jnp.where(quarter == i, pool[:, 192 * i : 192 * (i + 1)], mine)
    live = jnp.float32(0.0)
    for i in range(exit_layer.shape[0]):
        live += jnp.where(exit_layer[i] >= LAYER, 1.0, 0.0)
    row = lax.broadcasted_iota(jnp.int32, (pool.shape[0], 64), 0)
    marks = jnp.where(row == 0, live, 0.0)
    down_pool[:, D : D + 256] = jnp.concatenate([mine, marks], axis=1).astype(LOW)
    biases[...] = jnp.zeros_like(biases)
    biases[0:1, :] = upb[...].reshape(1, D)
    biases[1:2, 0:192] = qv[0:1, :]
    biases[2:3, 0:192] = qv[1:2, :]


def pack(places, exit_layer, up, out, down, pool, qv, upb):
    share = up.shape[0]
    args = (exit_layer, up, out, down, pool, qv, upb)
    return call(
        pack_kernel,
        "pack",
        (1,),
        [pl.BlockSpec(memory_space=pltpu.SMEM)] + [whole(a) for a in args[1:]],
        [pl.BlockSpec((share, 960), lambda *_: (0, 0)), pl.BlockSpec((share, 1024), lambda *_: (0, 0))]
        + [pl.BlockSpec((8, D), lambda *_: (0, 0))],
        [shape((share, 960), LOW), shape((share, 1024), LOW), shape((8, D), WIDE)],
        [],
        places,
        args,
        1,
        vmem=60,
    )


def by_side(places, mine, other):
    upper = places[0] == 1
    return jnp.where(upper, other, mine), jnp.where(upper, mine, other)


def project_kernel(places, x, bias, bias_other, h0, h1, h2, h3, q, k, v, w, held, pairs):
    @pl.when(pl.program_id(0) == 0)
    def _():
        gather_blocks(places, (h0, h1, h2, h3), held)
        for i in range(3):
            w[i] = to_pairs(held, 128 * i, 512 + 64 * i - 128)
        left, right = by_side(places, bias[...], bias_other[...])
        pairs[...] = jnp.concatenate(
            [left[:, :128], right[:, :128], left[:, 128:192], right[:, 128:192]], axis=1
        )

    left = x[...]
    q[...] = (dot(left, w[0]) + pairs[1:2, :]).astype(LOW)
    k[...] = dot(left, w[1]).astype(LOW)
    v[...] = (dot(left, w[2]) + pairs[2:3, :]).astype(LOW)


def project(places, tokens, bias, bias_other, halves):
    step = 256
    args = (tokens, bias, bias_other, *halves)
    return call(
        project_kernel,
        "project",
        (LEN // step,),
        [pl.BlockSpec((step, D), lambda i, places: (places[0] * (LEN // step) + i, 0))]
        + [whole(a) for a in args[1:]],
        [rows(step, 384)] * 3 + [pl.BlockSpec((3, D, 384), lambda *_: (0, 0, 0))],
        [shape((LEN, 384), LOW)] * 3 + [shape((3, D, 384), LOW)],
        [held_blocks(576), pltpu.VMEM((8, 384), WIDE)],
        places,
        args,
        2 * LEN * D * 1152,
    )


def first_of_pair():
    return lax.broadcasted_iota(jnp.int32, (1, 128), 1) < HD


def attend_kernel(places, q_ref, k_ref, v_ref, o_ref, inv_ref, p_ref, vx):
    first = first_of_pair()
    zero, one = jnp.zeros((), LOW), jnp.ones((), LOW)
    k = k_ref[...]
    v = v_ref[...]
    n = k.shape[0]
    vx[0:n, 0:128] = jnp.where(first, v, zero)
    vx[n : 2 * n, 0:128] = jnp.where(first, zero, v)
    vx[0:n, 128:256] = jnp.broadcast_to(jnp.where(first, one, zero), (n, 128))
    vx[n : 2 * n, 128:256] = jnp.broadcast_to(jnp.where(first, zero, one), (n, 128))
    step = 256
    for i in range(n // step):
        at = pl.ds(i * step, step)
        q = q_ref[at, :]
        result = None
        for head in range(2):
            mine = jnp.where(first, q, zero) if head == 0 else jnp.where(first, zero, q)
            score = dot_nt(mine, k)
            top = jnp.max(score, axis=1, keepdims=True)
            weight = jnp.exp2((score - top) * (HD**-0.5 * LOG2_E)).astype(LOW)
            p_ref[head, at, :] = weight
            part = dot(weight, vx[head * n : (head + 1) * n, :])
            result = part if result is None else result + part
        inv = 1.0 / result[:, 128:256]
        inv_ref[at, :] = inv
        o_ref[at, :] = (result[:, 0:128] * inv).astype(LOW)


def attend(places, q, k, v):
    pair = pl.BlockSpec((LEN, 128), lambda i, *_: (0, i))
    return call(
        attend_kernel,
        "attend_forward",
        (3,),
        [pair] * 3,
        [pair, pair, pl.BlockSpec((2, LEN, LEN), lambda i, *_: (i, 0, 0))],
        [shape((LEN, 384), LOW), shape((LEN, 384), WIDE), shape((6, LEN, LEN), LOW)],
        [pltpu.VMEM((2 * LEN, 256), LOW)],
        places,
        (q, k, v),
        4 * 6 * LEN * LEN * 256,
        vmem=50,
    )


def out_kernel(places, o, h0, h1, h2, h3, z, w_out, w_up, held):
    @pl.when(pl.program_id(0) == 0)
    def _():
        gather_blocks(places, (h0, h1, h2, h3), held)
        w_out[...] = to_pairs(held, D, D + 128)
        w_up[:, 0:D] = side_of(held, 0, 0, D)
        w_up[:, D : 2 * D] = side_of(held, 1, 0, D)

    z[...] = dot_nt(o[...], w_out[...]).astype(LOW)


def project_out(places, o, halves):
    step = 256
    return call(
        out_kernel,
        "project_out",
        (LEN // step,),
        [rows(step, 384)] + [whole(a) for a in halves],
        [rows(step, D), pl.BlockSpec((D, 384), lambda *_: (0, 0))]
        + [pl.BlockSpec((D, 2 * D), lambda *_: (0, 0))],
        [shape((LEN, D), LOW), shape((D, 384), LOW), shape((D, 2 * D), LOW)],
        [held_blocks(960)],
        places,
        (o, *halves),
        2 * LEN * D * 384,
    )


def normalize(hidden):
    centred = hidden - jnp.mean(hidden, axis=-1, keepdims=True)
    spread = lax.rsqrt(jnp.mean(centred * centred, axis=-1, keepdims=True) + EPS_NORM)
    return centred * spread, spread


def norm_back(grad_normed, normed, spread):
    return spread * (
        grad_normed
        - jnp.mean(grad_normed, axis=-1, keepdims=True)
        - normed * jnp.mean(grad_normed * normed, axis=-1, keepdims=True)
    )


def up_kernel(places, x, z, zp, vec, bias_mine, bias_other, w, m, slope, n1, rs1, low, bias):
    @pl.when(pl.program_id(0) == 0)
    def _():
        left, right = by_side(places, bias_mine[0:1, :], bias_other[0:1, :])
        bias[:, 0:D] = left
        bias[:, D : 2 * D] = right

    total = z[...].astype(WIDE) + zp[...].astype(WIDE)
    normed, spread = normalize(x[...].astype(WIDE) + total + vec[4:5, :])
    n1[...] = normed
    rs1[...] = jnp.broadcast_to(spread, rs1.shape)
    middle = (normed * vec[0:1, :] + vec[1:2, :]).astype(LOW)
    low[...] = middle
    for c in range(4):
        at = pl.ds(c * 384, 384)
        u = dot(middle, w[:, at]) + bias[0:1, at]
        half = 0.5 * (1.0 + lax.erf(u * 0.7071067811865476))
        m[:, at] = (u * half).astype(LOW)
        slope[:, at] = (half + u * (jnp.exp(-0.5 * u * u) * 0.3989422804014327)).astype(LOW)


def feed_up(places, tokens, z, zp, vec, bias, bias_other, w_up):
    step = 256
    args = (tokens, z, zp, vec, bias, bias_other, w_up)
    return call(
        up_kernel,
        "feed_up",
        (LEN // step,),
        [pl.BlockSpec((step, D), lambda i, places: (places[0] * (LEN // step) + i, 0))]
        + [rows(step, D)] * 2
        + [whole(a) for a in args[3:]],
        [rows(step, 2 * D)] * 2
        + [rows(step, D), rows(step, 128), rows(step, D)],
        [shape((LEN, 2 * D), LOW)] * 2
        + [shape((LEN, D), WIDE), shape((LEN, 128), WIDE), shape((LEN, D), LOW)],
        [pltpu.VMEM((1, 2 * D), WIDE)],
        places,
        args,
        2 * LEN * D * 2 * D,
    )


def down_kernel(places, m, h0, h1, h2, h3, f, w, pool, count, held):
    @pl.when(pl.program_id(0) == 0)
    def _():
        gather_blocks(places, (h0, h1, h2, h3), held)
        for side in range(2):
            w[:, D * side : D * (side + 1)] = side_of(held, side, 0, D)
        pool[...] = jnp.concatenate([side_of(held, side, D, 192) for side in range(2)], axis=1)
        live = jnp.sum(side_of(held, 0, D + 192, 64).astype(WIDE), axis=0, keepdims=True)
        count[...] = jnp.broadcast_to(live[:, 0:1], count.shape)

    f[...] = dot_nt(m[...], w[...]).astype(LOW)


def feed_down(places, m, halves):
    step = 256
    return call(
        down_kernel,
        "feed_down",
        (LEN // step,),
        [rows(step, 2 * D)] + [whole(a) for a in halves],
        [rows(step, D), pl.BlockSpec((D, 2 * D), lambda *_: (0, 0))]
        + [pl.BlockSpec((D, 384), lambda *_: (0, 0)), pl.BlockSpec((8, 128), lambda *_: (0, 0))],
        [shape((LEN, D), LOW), shape((D, 2 * D), LOW), shape((D, 384), LOW), shape((8, 128), WIDE)],
        [held_blocks(1024)],
        places,
        (m, *halves),
        2 * LEN * D * 2 * D,
    )


def turn_kernel(
    places, exit_layer, labels, n1, f, fp, cot, vec, pool_a, pool_b, classes, bias, live_count,
    y, half, dh2, low, sums, ramp, pool
):
    step = pl.program_id(0)
    middle = n1[...] * vec[0:1, :] + vec[1:2, :]
    total = f[...].astype(WIDE) + fp[...].astype(WIDE)
    normed, spread = normalize(middle + total + vec[5:6, :])
    result = normed * vec[2:3, :] + vec[3:4, :]
    low_result = result.astype(LOW)
    y[...] = low_result

    @pl.when(step // 2 == places[CORE_AT])
    def _():
        half[...] = low_result

    leaves = exit_layer[places[0]]
    grad = cot[...].astype(WIDE) * jnp.where(leaves > LAYER, 1.0, 0.0)
    dh2[...] = grad

    @pl.when(step == 0)
    def _():
        sums[...] = jnp.zeros_like(sums)
        own = places[CORE_AT]

        @pl.when(own == 0)
        def _():
            pool[:, 0:384] = pool_a[...]
            pool[:, 384:D] = pool_b[...]

        @pl.when(own == 1)
        def _():
            pool[:, 0:384] = pool_b[...]
            pool[:, 384:D] = pool_a[...]

        count = 16
        head = result[0:count, :].astype(LOW)
        pooled = jnp.tanh(dot(head, pool[...]) + vec[6:7, :])
        pooled_low = pooled.astype(LOW)
        lane = lax.broadcasted_iota(jnp.int32, (count, 128), 1)
        row = lax.broadcasted_iota(jnp.int32, (count, 128), 0)
        valid = lane < 3
        logits = dot(pooled_low, classes[...]) + bias[0:1, :]
        top = jnp.max(jnp.where(valid, logits, -jnp.inf), axis=1, keepdims=True)
        shifted = logits - top
        log_sum = jnp.log(
            jnp.sum(jnp.where(valid, jnp.exp(shifted), 0.0), axis=1, keepdims=True)
        )
        log_probs = jnp.where(valid, shifted - log_sum, 0.0)
        probs = jnp.where(valid, jnp.exp(log_probs), 0.0)
        live = jnp.where(leaves >= LAYER, 1.0, 0.0)
        entropy = -live * jnp.sum(probs * log_probs, axis=1, keepdims=True)
        onehot = jnp.where(lane == labels[places[0]], 1.0, 0.0)
        grad_logits = live * (probs - onehot) / live_count[0:1, 0:1]
        grad_logits = jnp.where(valid & (row == 0), grad_logits, 0.0).astype(LOW)
        grad_pre = (dot_nt(grad_logits, classes[...]) * (1.0 - pooled * pooled)).astype(LOW)
        grad_head = dot_nt(grad_pre, pool[...])
        dh2[0:count, :] = dh2[0:count, :] + grad_head
        sums[3:4, :] = grad_pre[0:1, :].astype(WIDE)
        of_class = dot_tn(grad_logits, pooled_low)
        sums[4:7, :] = of_class[0:3, :]
        last = jnp.where(lane == 3, entropy, grad_logits.astype(WIDE))
        sums[7:8, 0:128] = last[0:1, :]
        ramp[0:1, :] = head[0:1, :].astype(WIDE)
        ramp[1:2, :] = grad_pre[0:1, :].astype(WIDE)

    grad = dh2[...]
    sums[0:1, :] += jnp.sum(grad * normed, axis=0, keepdims=True)
    sums[1:2, :] += jnp.sum(grad, axis=0, keepdims=True)
    back = norm_back(grad * vec[2:3, :], normed, spread)
    sums[2:3, :] += jnp.sum(back, axis=0, keepdims=True)
    dh2[...] = back
    low[...] = back.astype(LOW)


def own_rows(step):
    return pl.BlockSpec((step, D), lambda i, places: (places[0] * (LEN // step) + i, 0))


def half_rows(step, sibling=False):
    count = LEN // step // 2

    def at(i, places):
        core = 1 - places[CORE_AT] if sibling else places[CORE_AT]
        return jnp.clip(i - count * core, 0, count - 1), 0

    return pl.BlockSpec((step, D), at)


def turn(places, exit_layer, labels, n1, f, fp, cotangent, vec, pool_a, pool_b, classes, bias, live_count):
    step = 256
    args = (exit_layer, labels, n1, f, fp, cotangent, vec, pool_a, pool_b, classes, bias, live_count)
    return call(
        turn_kernel,
        "turn",
        (LEN // step,),
        [pl.BlockSpec(memory_space=pltpu.SMEM)] * 2
        + [rows(step, D)] * 3
        + [own_rows(step)]
        + [whole(a) for a in args[6:]],
        [own_rows(step), half_rows(step)]
        + [rows(step, D)] * 2
        + [pl.BlockSpec((8, D), lambda *_: (0, 0))] * 2,
        [shape((2 * LEN, D), LOW), shape((LEN // 2, D), LOW)]
        + [shape((LEN, D), WIDE), shape((LEN, D), LOW)]
        + [shape((8, D), WIDE)] * 2,
        [pltpu.VMEM((D, D), LOW)],
        places,
        args,
        LEN * D * 60,
    )


def feed_back_kernel(places, dh2, slope, w_down, w_up, du, dx, sums):
    grad = dot(dh2[...], w_down[...]) * slope[...].astype(WIDE)
    grad = grad.astype(LOW)
    du[...] = grad
    dx[...] = dot_nt(grad, w_up[...]).astype(LOW)

    @pl.when(pl.program_id(0) == 0)
    def _():
        sums[...] = jnp.zeros_like(sums)

    sums[0:1, :] += jnp.sum(grad.astype(WIDE), axis=0, keepdims=True)


def feed_back(places, dh2, slope, w_down, w_up):
    step = 256
    args = (dh2, slope, w_down, w_up)
    return call(
        feed_back_kernel,
        "feed_back",
        (LEN // step,),
        [rows(step, D), rows(step, 2 * D), whole(w_down), whole(w_up)],
        [rows(step, 2 * D), rows(step, D), pl.BlockSpec((8, 2 * D), lambda *_: (0, 0))],
        [shape((LEN, 2 * D), LOW), shape((LEN, D), LOW), shape((8, 2 * D), WIDE)],
        [],
        places,
        args,
        4 * LEN * D * 2 * D,
    )


def feed_grad_kernel(places, dh2, m, middle, du, h0, h1, h2, h3, held, turned):
    for at, left, right in ((0, dh2, m), (D, middle, du)):
        turned[...] = left[...].T
        for side in range(2):
            for c in range(0, D, 256):
                part = dot(turned[...], right[:, D * side + c : D * side + c + 256]).astype(LOW)
                held[side * BLOCKS : (side + 1) * BLOCKS, :, at + c : at + c + 256] = part.reshape(
                    BLOCKS, BLOCK_ROWS, 256
                )
    scatter_blocks(places, held, (h0, h1, h2, h3))


def feed_grad(places, dh2, m, middle, du):
    args = (dh2, m, middle, du)
    return call(
        feed_grad_kernel,
        "feed_grad",
        (1,),
        [whole(a) for a in args],
        half_specs(2 * D),
        half_shapes(2 * D),
        [held_blocks(2 * D), pltpu.VMEM((D, LEN), LOW)],
        places,
        args,
        4 * LEN * D * 2 * D,
        vmem=40,
    )


def mid_kernel(
    places, dh2, dx, dxp, n1, rs1, vec, w_out, turn_sums, up_sums, ramp, dh1, low, do, sums
):
    @pl.when(pl.program_id(0) == 0)
    def _():
        row = lax.broadcasted_iota(jnp.int32, sums.shape, 0)
        at = 16 + 2 * places[SLOT_AT]
        slots = jnp.where(row == at, ramp[0:1, :], jnp.where(row == at + 1, ramp[1:2, :], 0.0))
        sums[...] = slots
        sums[0:8, :] = turn_sums[...]
        sums[11:12, :] = up_sums[0:1, 0:D]
        sums[12:13, :] = up_sums[0:1, D : 2 * D]

    total = dx[...].astype(WIDE) + dxp[...].astype(WIDE)
    grad = dh2[...] + total
    normed = n1[...]
    sums[8:9, :] += jnp.sum(grad * normed, axis=0, keepdims=True)
    sums[9:10, :] += jnp.sum(grad, axis=0, keepdims=True)
    back = norm_back(grad * vec[0:1, :], normed, rs1[:, 0:1])
    sums[10:11, :] += jnp.sum(back, axis=0, keepdims=True)
    dh1[...] = back
    back_low = back.astype(LOW)
    low[...] = back_low
    do[...] = dot(back_low, w_out[...]).astype(LOW)


def mid(places, dh2, dx, dxp, n1, rs1, vec, w_out, turn_sums, up_sums, ramp, slots):
    step = 256
    args = (dh2, dx, dxp, n1, rs1, vec, w_out, turn_sums, up_sums, ramp)
    count = 16 + 2 * slots
    return call(
        mid_kernel,
        "middle_back",
        (LEN // step,),
        [rows(step, D)] * 4 + [rows(step, 128)] + [whole(a) for a in args[5:]],
        [rows(step, D)] * 2 + [rows(step, 384), pl.BlockSpec((count, D), lambda *_: (0, 0))],
        [shape((LEN, D), WIDE), shape((LEN, D), LOW), shape((LEN, 384), LOW), shape((count, D), WIDE)],
        [],
        places,
        args,
        2 * LEN * D * 384,
    )


def attend_back_kernel(
    places, q_ref, k_ref, v_ref, do_ref, inv_ref, p_ref, dq_ref, dk_ref, dv_ref, ds_ref, held
):
    first = first_of_pair()
    zero = jnp.zeros((), LOW)
    n = k_ref.shape[0]
    k = k_ref[...]
    v = v_ref[...]
    k_own = [jnp.where(first, k, zero), jnp.where(first, zero, k)]
    scaled = (do_ref[...].astype(WIDE) * inv_ref[...]).astype(LOW)
    held[...] = scaled
    step = 256
    for i in range(n // step):
        at = pl.ds(i * step, step)
        d = held[at, :]
        total = None
        for head in range(2):
            mine = jnp.where(first, d, zero) if head == 0 else jnp.where(first, zero, d)
            grad_weight = dot_nt(mine, v)
            weight = p_ref[head, at, :].astype(WIDE)
            product = weight * grad_weight
            inner = jnp.sum(product, axis=1, keepdims=True)
            inner = inner * inv_ref[at, pl.ds(HD * head, 1)]
            grad_score = (product - weight * inner).astype(LOW)
            ds_ref[head, at, :] = grad_score
            part = dot(grad_score, k_own[head])
            total = part if total is None else total + part
        dq_ref[at, :] = (total * HD**-0.5).astype(LOW)
    scaled_t = scaled.T
    q_t = q_ref[...].T
    grad_v = jnp.concatenate(
        [dot(scaled_t[0:HD], p_ref[0]), dot(scaled_t[HD : 2 * HD], p_ref[1])], axis=0
    )
    dv_ref[...] = grad_v.T.astype(LOW)
    grad_k = jnp.concatenate(
        [dot(q_t[0:HD], ds_ref[0]), dot(q_t[HD : 2 * HD], ds_ref[1])], axis=0
    )
    dk_ref[...] = (grad_k * HD**-0.5).T.astype(LOW)


def attend_back(places, q, k, v, do, inv, p):
    at = pl.BlockSpec((LEN, 128), lambda i, *_: (0, i))
    return call(
        attend_back_kernel,
        "attend_backward",
        (3,),
        [at] * 5 + [pl.BlockSpec((2, LEN, LEN), lambda i, *_: (i, 0, 0))],
        [at] * 3,
        [shape((LEN, 384), LOW)] * 3,
        [pltpu.VMEM((2, LEN, LEN), LOW), pltpu.VMEM((LEN, 128), LOW)],
        places,
        (q, k, v, do, inv, p),
        8 * 6 * LEN * LEN * 256,
        vmem=36,
    )


def narrow_grad_kernel(share, places, left, dh1, o, *refs):
    grads, halves, (held, turned) = refs[:3], refs[3:7], refs[7:]
    turned[...] = left[...].T
    marks = []
    for i in range(3):
        right = grads[i][...]
        from_pairs(dot(turned[...], right).astype(LOW), held, 128 * i, 512 + 64 * i)
        if i != 1:
            marks.append(jnp.sum(right.astype(WIDE), axis=0, keepdims=True))
    turned[...] = dh1[...].T
    from_pairs(dot(turned[...], o[...]).astype(LOW), held, 384, 704)
    row = lax.rem(lax.broadcasted_iota(jnp.int32, (BLOCK_ROWS, 128), 0), share)
    for side in range(2):
        block = jnp.zeros((BLOCK_ROWS, 128), WIDE)
        for i, mark in enumerate(marks):
            narrow = mark[:, 256 + 64 * side : 320 + 64 * side]
            pieces = (mark[:, 128 * side : 128 * (side + 1)], jnp.concatenate([narrow, narrow], axis=1))
            for j, piece in enumerate(pieces):
                block = jnp.where(row == 2 * i + j, piece, block)
        for p in range(BLOCKS):
            held[side * BLOCKS + p, :, MARKS_AT:MARKED_WIDTH] = block.astype(LOW)
    scatter_blocks(places, held, halves, ALONG)


def narrow_grad(places, share, tokens, dh1, o, grads):
    args = (tokens, dh1, o, *grads)
    return call(
        functools.partial(narrow_grad_kernel, share),
        "narrow_grad",
        (1,),
        [own_rows(LEN)] + [whole(a) for a in args[1:]],
        half_specs(MARKED_WIDTH),
        half_shapes(MARKED_WIDTH),
        [held_blocks(MARKED_WIDTH), pltpu.VMEM((D, LEN), LOW)],
        places,
        args,
        2 * LEN * D * 1536,
    )


def input_kernel(places, *refs):
    grads, w, (keep, send) = refs[:3], refs[3], refs[4:]
    total = None
    for i in range(3):
        part = dot_nt(grads[i][...], w[i])
        total = part if total is None else total + part
    total = total.astype(LOW)
    mine = pl.program_id(0) // 2 == places[CORE_AT]

    @pl.when(mine)
    def _():
        keep[...] = total

    @pl.when(jnp.logical_not(mine))
    def _():
        send[...] = total


def input_grad(places, grads, w):
    step = 256
    return call(
        input_kernel,
        "input_grad",
        (LEN // step,),
        [rows(step, 384)] * 3 + [whole(w)],
        [half_rows(step), half_rows(step, True)],
        [shape((LEN // 2, D), LOW)] * 2,
        [],
        places,
        (*grads, w),
        2 * LEN * D * 1152,
    )


def finish_kernel(places, dh1, keep, other, half):
    total = keep[...].astype(WIDE) + other[...].astype(WIDE)
    half[...] = (dh1[...] + total).astype(LOW)


def finish(places, dh1, keep, other):
    step = 128
    count = LEN // 2 // step
    return call(
        finish_kernel,
        "finish",
        (count,),
        [pl.BlockSpec((step, D), lambda i, places: (count * places[CORE_AT] + i, 0))]
        + [rows(step, D)] * 2,
        [rows(step, D)],
        [shape((LEN // 2, D), LOW)],
        [],
        places,
        (dh1, keep, other),
        LEN * D * 3,
    )[0]


def place_kernel(count, places, *refs):
    half = LEN // 2
    ins, out, sems = refs[-2 - count : -2], refs[-2], refs[-1]
    side, core = places[0], places[CORE_AT]
    at = [(1 - side, core), (1 - side, 1 - core), (side, core), (side, 1 - core)]
    copies = []
    for i, ref in enumerate(ins):
        first = pl.multiple_of((2 * at[i][0] + at[i][1]) * half, half)
        copies.append(pltpu.make_async_copy(ref, out.at[pl.ds(first, half)], sems.at[i]))
        copies[-1].start()
    for copy in copies:
        copy.wait()


def place(places, kept, quarters):
    first = [] if kept is None else [kept]
    return call(
        functools.partial(place_kernel, len(quarters)),
        "place",
        (1,),
        [pl.BlockSpec(memory_space=pl.ANY)] * len(first) + [whole(a) for a in quarters],
        [pl.BlockSpec(memory_space=pl.ANY)],
        [shape((2 * LEN, D), LOW)],
        [pltpu.SemaphoreType.DMA((len(quarters),))],
        places,
        (*first, *quarters),
        1,
        vmem=12,
        aliases={} if kept is None else {1: 0},
    )[0]


def update(places, name, pieces, width, masters, kernel, extra):
    counts = tuple(len(group) for group in pieces)
    args = [a for group in pieces for a in group]
    specs = [
        pl.BlockSpec((1, a.shape[1], width), lambda *_: (0, 0, 0))
        if a.ndim == 3
        else pl.BlockSpec(a.shape, lambda *_: (0, 0))
        for a in args
    ]
    flat = [a for triple in masters for a in triple]
    outs = []
    for weight, first, second in masters:
        outs += [shape(weight.shape, WIDE)] * 3 + [shape(weight.shape, LOW)]
    outs += extra
    return call(
        functools.partial(kernel, counts),
        name,
        (1,),
        specs + [whole(a) for a in flat],
        [whole(o) for o in outs],
        outs,
        [],
        places,
        (*args, *flat),
        1,
        vmem=60,
    )


def step_matrix(ins, outs, at, grad, rate):
    new, first, second = adamw(ins[0][at], ins[1][at], ins[2][at], grad, rate, DECAY)
    outs[0][at] = new
    outs[1][at] = first
    outs[2][at] = second
    outs[3][at] = new.astype(LOW)


def update_feed_kernel(counts, places, *refs):
    total = sum(counts)
    grad = sum_pieces(refs[:total], counts)
    ins, outs = refs[total : total + 6], refs[total + 6 :]
    step_matrix(ins[0:3], outs[0:4], ..., grad[:, 0:D], RATE * FF ** (-0.5))
    step_matrix(ins[3:6], outs[4:8], ..., grad[:, D : 2 * D], RATE * D ** (-0.5))


def update_narrow_kernel(counts, places, *refs):
    total = sum(counts)
    grad = sum_pieces(refs[:total], counts)
    ins, outs = refs[total : total + 6], refs[total + 6 :]

    def columns(i):
        return jnp.concatenate(
            [grad[:, 128 * i : 128 * (i + 1)], grad[:, 512 + 64 * i : 576 + 64 * i]], axis=1
        )

    for i in range(3):
        step_matrix(ins[0:3], outs[0:4], i, columns(i), RATE * D ** (-0.5))
    step_matrix(ins[3:6], outs[4:8], ..., columns(3).T, RATE * max(1, 2 * D // LEN) ** (-0.5))
    outs[8][...] = grad[0:8, MARKS_AT:MARKED_WIDTH]


def per_device(
    dp_count,
    mp_count,
    tokens,
    cotangent,
    exit_layer,
    labels,
    qkv_weight,
    qkv_first,
    qkv_second,
    out_weight,
    out_first,
    out_second,
    up_weight,
    up_first,
    up_second,
    down_weight,
    down_first,
    down_second,
    pool_weight,
    pool_first,
    pool_second,
    qv_bias,
    qv_first,
    qv_second,
    up_bias,
    upb_first,
    upb_second,
    layer_vectors,
    vector_first,
    vector_second,
    class_weight,
    class_first,
    class_second,
):
    links = Links(dp_count, mp_count)
    side, core = links.side, links.core

    slot = 2 * links.dp + side
    places = jnp.concatenate([side[None], links.places(), core[None], slot[None]]).astype(jnp.int32)
    share = D // dp_count

    by_kind = [a.transpose(1, 0, 2) for a in (qkv_weight, qkv_first, qkv_second)]
    down_turned = [a.T for a in (down_weight, down_first, down_second)]
    qkv_spread = links.spread(pack_first(by_kind[0]))
    sent = qkv_spread.step()
    up_out, down_pool, biases = pack(
        places,
        exit_layer,
        after(up_weight, *sent),
        out_weight,
        down_turned[0],
        pool_weight,
        qv_bias,
        up_bias,
    )
    other_biases = links.swap(biases, SIDE)
    qkv_z = tuple(qkv_spread.last)
    sent = qkv_spread.step(up_out, other_biases)
    up_out_spread = links.spread(up_out)
    up_out_spread.step(*qkv_z)
    class_low = after(class_weight, *sent)
    classes = jnp.pad(class_low[:D].astype(LOW), ((0, 0), (0, 125)))
    class_bias = jnp.pad(class_low[D:], ((0, 0), (0, 125)))
    sent = qkv_spread.step(classes, class_bias)
    sent = up_out_spread.step(*sent)
    down_spread = links.spread(down_pool)
    sent = down_spread.step(*sent)

    biases = after(biases, *sent)
    q, k, v, w_qkv = project(places, tokens, biases, other_biases, qkv_spread.halves())
    sent = up_out_spread.step(q)
    q = after(q, *sent)
    o, inv, p = attend(places, q, k, v)
    sent = down_spread.step(o)
    o = after(o, *sent)
    z, w_out, w_up = project_out(places, o, up_out_spread.halves())
    zp = links.swap(z, CORE)
    sent = down_spread.step(z)
    z = after(z, *sent)
    m, slope, n1, rs1, middle_low = feed_up(
        places, tokens, z, zp, layer_vectors, biases, other_biases, w_up
    )
    f, w_down, pool_mine, live_count = feed_down(places, m, down_spread.halves())
    fp = links.swap(f, CORE)
    pool_other = links.swap(pool_mine, CORE)
    y, y_half, dh2, dh2_low, turn_sums, ramp = turn(
        places, exit_layer, labels, n1, f, fp, cotangent, layer_vectors, pool_mine, pool_other,
        classes, class_bias, live_count,
    )

    y_first = links.swap(y_half, SIDE)
    du, dx, up_sums = feed_back(places, dh2_low, slope, w_down, w_up)
    dxp = links.swap(dx, CORE)
    m, dh2_low = after((m, dh2_low), dx)
    feed_halves = feed_grad(places, dh2_low, m, middle_low, du)
    feed_fold = links.fold(feed_halves, ACROSS)
    feed_fold.step(y_first)
    dx = after(dx, *feed_halves)
    slots = 2 * dp_count
    dh1, dh1_low, do, sums = mid(
        places, dh2, dx, dxp, n1, rs1, layer_vectors, w_out, turn_sums, up_sums, ramp, slots
    )
    total = Total(links, sums)
    total.step()
    grads = attend_back(places, q, k, v, do, inv, p)
    sent = feed_fold.step(grads[0], vmem=12)
    grads = after(grads, *sent)
    token_keep, token_send = input_grad(places, grads, w_qkv)
    token_other = links.swap(token_send, CORE)
    grads = after(grads, token_keep)
    narrow_halves = narrow_grad(places, share, tokens, dh1_low, o, grads)
    narrow_fold = links.fold(narrow_halves, ALONG)
    narrow_fold.step()
    token_keep = after(token_keep, *narrow_halves)
    grad_half = finish(places, dh1, token_keep, token_other)
    first = links.swap(grad_half, SIDE)
    second_own = links.swap(grad_half, CORE)
    sent = total.step(grad_half)
    sent = feed_fold.step(*sent)
    y_second = links.swap(after(y_first, *sent), CORE)
    sent = narrow_fold.step(*sent)
    first = after(first, *sent)
    second = links.swap(first, CORE)
    sent = total.step(*sent)
    y = after(y, *sent)
    result = place(places, y, [y_first, y_second])
    feed_pieces = after(feed_fold.pieces(), result)
    feed_new = update(
        places,
        "update_feed",
        feed_pieces,
        2 * D,
        [down_turned, (up_weight, up_first, up_second)],
        update_feed_kernel,
        [],
    )
    sent = narrow_fold.step(feed_new[0])
    sent = total.step(*sent)
    tokens_grad = place(
        places, None, [first, after(second, *sent), grad_half, second_own]
    )
    sent = narrow_fold.step(tokens_grad)
    total.value, total.last = after((total.value, total.last), *sent)
    sums = total.result()
    down_new, down_first_new, down_second_new, down_copy = (a.T for a in feed_new[0:4])
    up_new, up_first_new, up_second_new, up_copy = feed_new[4:8]
    *narrow_new, marks = update(
        places,
        "update_narrow",
        narrow_fold.pieces(),
        MARKED_WIDTH,
        [by_kind, (out_weight, out_first, out_second)],
        update_narrow_kernel,
        [shape((8, 128), WIDE)],
    )
    qkv_new, qkv_first_new, qkv_second_new, qkv_copy = (
        a.transpose(1, 0, 2) for a in narrow_new[0:4]
    )
    out_new, out_first_new, out_second_new, out_copy = narrow_new[4:8]

    ramps = sums[16:].reshape(slots, 2, D)

    head_rows = lax.dynamic_slice_in_dim(ramps[:, 0], links.dp * share, share, 1)
    grad_pool = lax.dot_general(
        head_rows.astype(LOW),
        ramps[:, 1].astype(LOW),
        (((0,), (0,)), ((), ())),
        preferred_element_type=WIDE,
    )
    vector_sum = jnp.concatenate([sums[8:10], sums[0:2], sums[10:11], sums[2:4]], axis=0)
    class_sum = jnp.concatenate([sums[4:7].T, sums[7:8, 0:3]], axis=0)
    upb_sum = lax.dynamic_slice_in_dim(sums, 11 + side, 1, 0)[0]
    bias_sum = jnp.concatenate([marks[0:4:2], marks[1:4:2, 0:64]], axis=1)

    pool_new, pool_first_new, pool_second_new = adamw(
        pool_weight, pool_first, pool_second, grad_pool, RATE * D ** (-0.5), DECAY
    )
    qv_new, qv_first_new, qv_second_new = adamw(
        qv_bias, qv_first, qv_second, bias_sum, VECTOR_RATE, 0.0
    )
    upb_new, upb_first_new, upb_second_new = adamw(
        up_bias, upb_first, upb_second, upb_sum, VECTOR_RATE, 0.0
    )
    vector_new, vector_first_new, vector_second_new = adamw(
        layer_vectors, vector_first, vector_second, vector_sum, VECTOR_RATE, 0.0
    )
    class_new, class_first_new, class_second_new = adamw(
        class_weight, class_first, class_second, class_sum, RATE * (D // 4) ** (-0.5), DECAY
    )
    return (
        result,
        tokens_grad,
        sums[7, 3] / live_count[0, 0],
        qkv_new,
        qkv_first_new,
        qkv_second_new,
        qkv_copy,
        out_new,
        out_first_new,
        out_second_new,
        out_copy,
        up_new,
        up_first_new,
        up_second_new,
        up_copy,
        down_new,
        down_first_new,
        down_second_new,
        down_copy,
        pool_new,
        pool_first_new,
        pool_second_new,
        pool_new.astype(LOW),
        qv_new,
        qv_first_new,
        qv_second_new,
        upb_new,
        upb_first_new,
        upb_second_new,
        vector_new,
        vector_first_new,
        vector_second_new,
        class_new,
        class_first_new,
        class_second_new,
    )


def solution(mesh):
    in_specs = (
        P("dp", None),
        P("dp", None),
        P("dp"),
        P("dp"),
        P("dp", None, "mp"),
        P("dp", None, "mp"),
        P("dp", None, "mp"),
        P("mp", "dp"),
        P("mp", "dp"),
        P("mp", "dp"),
        P("dp", "mp"),
        P("dp", "mp"),
        P("dp", "mp"),
        P("mp", "dp"),
        P("mp", "dp"),
        P("mp", "dp"),
        P("dp", None),
        P("dp", None),
        P("dp", None),
        P(None, "mp"),
        P(None, "mp"),
        P(None, "mp"),
        P("mp"),
        P("mp"),
        P("mp"),
        P(),
        P(),
        P(),
        P(),
        P(),
        P(),
    )
    out_specs = (
        P("dp", None),
        P("dp", None),
        P(),
        P("dp", None, "mp"),
        P("dp", None, "mp"),
        P("dp", None, "mp"),
        P("dp", None, "mp"),
        P("mp", "dp"),
        P("mp", "dp"),
        P("mp", "dp"),
        P("mp", "dp"),
        P("dp", "mp"),
        P("dp", "mp"),
        P("dp", "mp"),
        P("dp", "mp"),
        P("mp", "dp"),
        P("mp", "dp"),
        P("mp", "dp"),
        P("mp", "dp"),
        P("dp", None),
        P("dp", None),
        P("dp", None),
        P("dp", None),
        P(None, "mp"),
        P(None, "mp"),
        P(None, "mp"),
        P("mp"),
        P("mp"),
        P("mp"),
        P(),
        P(),
        P(),
        P(),
        P(),
        P(),
    )
    one_device = functools.partial(per_device, mesh.shape["dp"], mesh.shape["mp"])
    return jax.shard_map(
        one_device, mesh=mesh, in_specs=in_specs, out_specs=out_specs, check_vma=False
    )
```

```python
import functools

import jax
import jax.numpy as jnp
import numpy as np
from jax import lax
from jax.experimental import pallas as pl
from jax.experimental.pallas import tpu as pltpu
from jax.sharding import PartitionSpec as P

D = 768
HD = 64
FF = 3072
LAYER = 6
STEP = 10
LEN = 1024


EPS_NORM = 1e-06
BETA_ONE = 0.9
BETA_TWO = 0.98
EPS_ADAM = 1e-08
DECAY = 0.01
RATE = 0.8
VECTOR_RATE = 0.3

LOW = jnp.bfloat16
WIDE = jnp.float32
LOG2_E = 1.4426950408889634
MIB = 2**20
COST_SCALE = 16

CORE, SIDE, X_BIT, Z_LOW, Z_HIGH = 1, 2, 4, 8, 16
BLOCKS = 8
BLOCK_ROWS = D // BLOCKS
PART_ROWS = BLOCK_ROWS // 2
ACROSS = ((Z_HIGH, Z_LOW, X_BIT, SIDE), (Z_HIGH, Z_LOW, SIDE, X_BIT))
ALONG = ((Z_HIGH, Z_LOW, SIDE, X_BIT), (SIDE, Z_HIGH, X_BIT, Z_LOW))
Z_LINE = (Z_HIGH, Z_LOW, Z_HIGH | Z_LOW)
ROUTES = (ACROSS, ALONG)


def dot(left, right):
    return lax.dot_general(
        left, right, (((1,), (0,)), ((), ())), preferred_element_type=WIDE
    )


def dot_nt(left, right):
    return lax.dot_general(
        left, right, (((1,), (1,)), ((), ())), preferred_element_type=WIDE
    )


def dot_tn(left, right):
    return lax.dot_general(
        left, right, (((0,), (0,)), ((), ())), preferred_element_type=WIDE
    )


def adamw(weight, first, second, grad, rate, decay):
    first_new = BETA_ONE * first + (1.0 - BETA_ONE) * grad
    second_new = BETA_TWO * second + (1.0 - BETA_TWO) * grad * grad
    first_hat = first_new / (1.0 - BETA_ONE**STEP)
    second_hat = second_new / (1.0 - BETA_TWO**STEP)
    weight_new = weight - rate * (first_hat / (jnp.sqrt(second_hat) + EPS_ADAM) + decay * weight)
    return (weight_new, first_new, second_new)


class Links:
    def __init__(self, dp_count, mp_count):
        self.dp_count = dp_count
        self.total = dp_count * mp_count
        self.cube = dp_count == BLOCKS
        self.dp = lax.axis_index("dp").astype(jnp.int32)
        mp = lax.axis_index("mp").astype(jnp.int32)
        self.side = mp // 2
        self.core = mp % 2

    def swap(self, value, bit):
        pairs = [(i, i ^ bit) for i in range(self.total)]
        return lax.ppermute(value, ("dp", "mp"), pairs)

    def places(self):
        flips = []
        for order in sum(ROUTES, ()):
            for j in range(2 * BLOCKS):
                if self.cube:
                    bits = 0
                    for k, bit in enumerate(order):
                        bits ^= bit if (j >> k) & 1 else 0
                    flips.append((bits // SIDE & 1, bits // X_BIT))
                else:
                    flips.append((j // BLOCKS, j % BLOCKS))
        flips = np.array(flips, np.int32)
        mine = self.dp if self.cube else 0
        return (self.side ^ flips[:, 0]) * BLOCKS + (mine ^ flips[:, 1])

    def spread(self, share):
        return (Spread if self.cube else WholeSpread)(self, share)

    def fold(self, halves, route, base):
        return (Fold if self.cube else WholeFold)(self, halves, route, base)


class Spread:
    def __init__(self, links, share):
        self.links = links
        self.held = [share[None]]
        self.last = None
        self.round = 0

    def step(self, *others):
        links = self.links
        if others:
            (self.held, self.last), *_ = lax.optimization_barrier(((self.held, self.last), *others))
        if self.round == 0:
            self.last = [links.swap(self.held[0], bits) for bits in Z_LINE]
        elif self.round == 1:
            line = [self.held[0], *self.last]
            at = (slice(0, PART_ROWS), slice(PART_ROWS, BLOCK_ROWS))
            self.held = [jnp.concatenate([a[:, i] for a in line], axis=0) for i in at]
        else:
            self.held = [
                jnp.concatenate([mine, other], axis=0)
                for mine, other in zip(self.held, self.last, strict=True)
            ]
        if self.round:
            self.last = [
                links.swap(part, ACROSS[i][self.round + 1]) for i, part in enumerate(self.held)
            ]
        self.round += 1
        return tuple(self.held)

    def halves(self):
        return (self.held[0], self.last[0], self.held[1], self.last[1])


class WholeSpread:
    def __init__(self, links, share):
        self.last = ()
        near = lax.all_gather(share, "dp", axis=0, tiled=True)
        near = near.reshape(BLOCKS, BLOCK_ROWS, share.shape[1])
        far = links.swap(near, SIDE)
        self.parts = (
            near[:, :PART_ROWS],
            far[:, :PART_ROWS],
            near[:, PART_ROWS:],
            far[:, PART_ROWS:],
        )

    def step(self, *others):
        return ()

    def halves(self):
        return self.parts


class Fold:
    def __init__(self, links, halves, route, base):
        self.links = links
        self.route = route
        self.base = base
        self.parts = [[halves[0]], [halves[2]]]
        self.far = [halves[1], halves[3]]
        self.joined = []
        self.round = 0

    def step(self, *others, vmem=16):
        links, k = self.links, 3 - self.round
        if others:
            (self.parts, self.joined, self.far), *_ = lax.optimization_barrier(
                ((self.parts, self.joined, self.far), *others)
            )
        if self.route is ACROSS and self.round == 2:
            sent = fold_add(self.parts, 2, False, self.base, vmem)
            self.joined = [links.swap(a, bits) for a, bits in zip(sent, Z_LINE, strict=True)]
        else:
            if self.round == 0:
                sent = self.far
            else:
                sent = fold_add(self.parts, 2**k, True, self.base, vmem)
            for i, order in enumerate(self.route):
                self.parts[i].append(links.swap(sent[i], order[k]))
        self.round += 1
        return tuple(sent)

    def pieces(self):
        return (self.parts[0], self.parts[1], self.joined)


class WholeFold:
    def __init__(self, links, halves, route, base):
        near, far = (
            jnp.concatenate([halves[i], halves[i + 2]], axis=1).reshape(D, -1) for i in range(2)
        )
        total = near.astype(WIDE) + links.swap(far, SIDE).astype(WIDE)
        share = lax.psum_scatter(total[:, :base], "dp", scatter_dimension=0, tiled=True)
        self.parts = [share, lax.psum(total[:BLOCK_ROWS, base:], "dp")]

    def step(self, *others, vmem=16):
        return ()

    def pieces(self):
        return ([], [], self.parts)


def add_marked(refs, at, base):
    total = sum(ref[at, :, 0:base].astype(WIDE) for ref in refs)
    marks = refs[0][at, :, base:].astype(WIDE)
    for ref in refs[1:]:
        marks = marks.astype(LOW).astype(WIDE) + ref[at, :, base:].astype(WIDE)
    return total, marks


def sum_pieces(refs, counts, base, at=0):
    first, second, joined = counts
    if not first:
        return refs[0][...], refs[1][...]
    tops = add_marked(refs[:first], at, base)
    ends = add_marked(refs[first : first + second], at, base)
    total, marks = (jnp.concatenate(pair, axis=0) for pair in zip(tops, ends, strict=True))
    joints = refs[first + second :]
    for ref in joints:
        total = total + ref[at, :, 0:base].astype(WIDE)
    if joints:
        high, low, both = (ref[at, :, base:].astype(WIDE) for ref in joints)
        marks = (marks.astype(LOW).astype(WIDE) + high) + (low + both)
    return total, marks


def fold_add_kernel(count, half, apart, base, *refs):
    ins, outs = refs[: 2 * count], refs[2 * count :]
    if apart:
        for i in range(half):
            for j in range(2):
                total, marks = add_marked(ins[j * count : (j + 1) * count], i, base)
                outs[j][i, :, 0:base] = total.astype(LOW)
                outs[j][i, :, base:] = marks.astype(LOW)
    else:
        for i, out in enumerate(outs):
            total, marks = sum_pieces(ins, (count, count, 0), base, i + 1)
            out[0, :, 0:base] = total.astype(LOW)
            out[0, :, base:] = marks.astype(LOW)


def fold_add(parts, half, apart, base, vmem):
    args = [*parts[0], *parts[1]]
    width = args[0].shape[2]
    if apart:
        outs = [shape((half, PART_ROWS, width), LOW)] * 2
        specs = [pl.BlockSpec((half, PART_ROWS, width), lambda i: (1, 0, 0))] * len(args)
    else:
        outs = [shape((1, BLOCK_ROWS, width), LOW)] * 3
        specs = [pl.BlockSpec((4, PART_ROWS, width), lambda i: (0, 0, 0))] * len(args)
    return pl.pallas_call(
        functools.partial(fold_add_kernel, len(parts[0]), half, apart, base),
        grid=(1,),
        in_specs=specs,
        out_specs=[pl.BlockSpec(o.shape, lambda i: (0, 0, 0)) for o in outs],
        out_shape=outs,
        compiler_params=pltpu.CompilerParams(vmem_limit_bytes=vmem * MIB),
        cost_estimate=pl.CostEstimate(
            flops=half * BLOCK_ROWS * width, bytes_accessed=half * width, transcendentals=0
        ),
        name="fold_add",
    )(*args)


def after(value, *others):
    return lax.optimization_barrier((value, *others))[0]


def call(kernel, name, grid, in_specs, out_specs, out_shape, scratch, places, args, flops, vmem=6, aliases=None):
    moved = sum(a.size * a.dtype.itemsize for a in args)
    moved += sum(int(np.prod(s.shape)) * np.dtype(s.dtype).itemsize for s in out_shape)
    return pl.pallas_call(
        kernel,
        out_shape=out_shape,
        grid_spec=pltpu.PrefetchScalarGridSpec(
            num_scalar_prefetch=1,
            grid=grid,
            in_specs=in_specs,
            out_specs=out_specs,
            scratch_shapes=scratch,
        ),
        input_output_aliases=aliases or {},
        compiler_params=pltpu.CompilerParams(vmem_limit_bytes=vmem * MIB),
        cost_estimate=pl.CostEstimate(
            flops=int(flops) // COST_SCALE, bytes_accessed=int(moved) // COST_SCALE, transcendentals=0
        ),
        name=name,
    )(places, *args)


def whole(array):
    return pl.BlockSpec(array.shape, lambda *_: (0,) * len(array.shape))


def rows(count, width):
    return pl.BlockSpec((count, width), lambda i, *_: (i, 0))


def shape(dims, kind):
    return jax.ShapeDtypeStruct(dims, kind)


def gather_blocks(places, halves, held, route=ACROSS):
    for i in range(2):
        for j in range(2 * BLOCKS):
            source = halves[2 * i + j // BLOCKS]
            target = places[1 + 2 * BLOCKS * (2 * ROUTES.index(route) + i) + j]
            held[target, i * PART_ROWS : (i + 1) * PART_ROWS, :] = source[j % BLOCKS]


def scatter_blocks(places, held, halves, route=ACROSS):
    for i in range(2):
        for j in range(2 * BLOCKS):
            target = halves[2 * i + j // BLOCKS]
            source = places[1 + 2 * BLOCKS * (2 * ROUTES.index(route) + i) + j]
            target[j % BLOCKS] = held[source, i * PART_ROWS : (i + 1) * PART_ROWS, :]


CORE_AT = 1 + 4 * BLOCKS * len(ROUTES)
SLOT_AT = CORE_AT + 1
DP_AT = CORE_AT + 2


def side_of(held, side, at, width):
    return held[side * BLOCKS : (side + 1) * BLOCKS, :, at : at + width].reshape(D, width)


def to_pairs(held, wide_at, narrow_at):
    return jnp.concatenate(
        [side_of(held, side, wide_at, 128) for side in range(2)]
        + [side_of(held, side, narrow_at, 64) for side in range(2)],
        axis=1,
    )


def from_pairs(value, held, wide_at, narrow_at):
    for side in range(2):
        at = slice(side * BLOCKS, (side + 1) * BLOCKS)
        wide = value[:, 128 * side : 128 * (side + 1)]
        held[at, :, wide_at : wide_at + 128] = wide.reshape(BLOCKS, BLOCK_ROWS, 128)
        narrow = value[:, 256 + 64 * side : 320 + 64 * side]
        held[at, :, narrow_at : narrow_at + 64] = narrow.reshape(BLOCKS, BLOCK_ROWS, 64)


def half_shapes(width):
    return [shape((BLOCKS, PART_ROWS, width), LOW)] * 4


def half_specs(width):
    return [pl.BlockSpec((BLOCKS, PART_ROWS, width), lambda *_: (0, 0, 0))] * 4


def held_blocks(width):
    return pltpu.VMEM((2 * BLOCKS, BLOCK_ROWS, width), LOW)


def pack_first_kernel(w, out):
    wide = [w[i][:, :128] for i in range(3)]
    narrow = [w[i][:, 128:] for i in range(3)]
    out[...] = jnp.concatenate(wide + narrow, axis=1).astype(LOW)


def pack_first(qkv):
    return pl.pallas_call(
        pack_first_kernel,
        out_shape=shape((qkv.shape[1], 576), LOW),
        name="pack_first",
    )(qkv)


def pack_kernel(places, exit_layer, up, out, down, pool, qv, upb, up_out, down_pool, biases):
    up_out[:, 0:D] = up[...].astype(LOW)
    up_out[:, D : D + 192] = out[...].T.astype(LOW)
    down_pool[:, 0:D] = down[...].astype(LOW)
    quarter = 2 * places[CORE_AT] + places[0]
    mine = jnp.zeros((pool.shape[0], 192), WIDE)
    for i in range(4):
        mine = jnp.where(quarter == i, pool[:, 192 * i : 192 * (i + 1)], mine)
    live = jnp.float32(0.0)
    for i in range(exit_layer.shape[0]):
        live += jnp.where(exit_layer[i] >= LAYER, 1.0, 0.0)
    row = lax.broadcasted_iota(jnp.int32, (pool.shape[0], 64), 0)
    marks = jnp.where(row == 0, live, 0.0)
    down_pool[:, D : D + 256] = jnp.concatenate([mine, marks], axis=1).astype(LOW)
    biases[...] = jnp.zeros_like(biases)
    biases[0:1, :] = upb[...].reshape(1, D)
    biases[1:2, 0:192] = qv[0:1, :]
    biases[2:3, 0:192] = qv[1:2, :]


def pack(places, exit_layer, up, out, down, pool, qv, upb):
    share = up.shape[0]
    args = (exit_layer, up, out, down, pool, qv, upb)
    return call(
        pack_kernel,
        "pack",
        (1,),
        [pl.BlockSpec(memory_space=pltpu.SMEM)] + [whole(a) for a in args[1:]],
        [pl.BlockSpec((share, 960), lambda *_: (0, 0)), pl.BlockSpec((share, 1024), lambda *_: (0, 0))]
        + [pl.BlockSpec((8, D), lambda *_: (0, 0))],
        [shape((share, 960), LOW), shape((share, 1024), LOW), shape((8, D), WIDE)],
        [],
        places,
        args,
        1,
        vmem=60,
    )


def by_side(places, mine, other):
    upper = places[0] == 1
    return jnp.where(upper, other, mine), jnp.where(upper, mine, other)


def project_kernel(places, x, bias, bias_other, h0, h1, h2, h3, q, k, v, w, held, pairs):
    @pl.when(pl.program_id(0) == 0)
    def _():
        gather_blocks(places, (h0, h1, h2, h3), held)
        for i in range(3):
            w[i] = to_pairs(held, 128 * i, 512 + 64 * i - 128)
        left, right = by_side(places, bias[...], bias_other[...])
        pairs[...] = jnp.concatenate(
            [left[:, :128], right[:, :128], left[:, 128:192], right[:, 128:192]], axis=1
        )

    left = x[...]
    q[...] = (dot(left, w[0]) + pairs[1:2, :]).astype(LOW)
    k[...] = dot(left, w[1]).astype(LOW)
    v[...] = (dot(left, w[2]) + pairs[2:3, :]).astype(LOW)


def project(places, tokens, bias, bias_other, halves):
    step = 256
    args = (tokens, bias, bias_other, *halves)
    return call(
        project_kernel,
        "project",
        (LEN // step,),
        [pl.BlockSpec((step, D), lambda i, places: (places[0] * (LEN // step) + i, 0))]
        + [whole(a) for a in args[1:]],
        [rows(step, 384)] * 3 + [pl.BlockSpec((3, D, 384), lambda *_: (0, 0, 0))],
        [shape((LEN, 384), LOW)] * 3 + [shape((3, D, 384), LOW)],
        [held_blocks(576), pltpu.VMEM((8, 384), WIDE)],
        places,
        args,
        2 * LEN * D * 1152,
    )


def first_of_pair():
    return lax.broadcasted_iota(jnp.int32, (1, 128), 1) < HD


def attend_kernel(places, q_ref, k_ref, v_ref, o_ref, inv_ref, p_ref, vx):
    first = first_of_pair()
    zero, one = jnp.zeros((), LOW), jnp.ones((), LOW)
    k = k_ref[...]
    v = v_ref[...]
    n = k.shape[0]
    vx[0:n, 0:128] = jnp.where(first, v, zero)
    vx[n : 2 * n, 0:128] = jnp.where(first, zero, v)
    vx[0:n, 128:256] = jnp.broadcast_to(jnp.where(first, one, zero), (n, 128))
    vx[n : 2 * n, 128:256] = jnp.broadcast_to(jnp.where(first, zero, one), (n, 128))
    step = 256
    for i in range(n // step):
        at = pl.ds(i * step, step)
        q = q_ref[at, :]
        result = None
        for head in range(2):
            mine = jnp.where(first, q, zero) if head == 0 else jnp.where(first, zero, q)
            score = dot_nt(mine, k)
            top = jnp.max(score, axis=1, keepdims=True)
            weight = jnp.exp2((score - top) * (HD**-0.5 * LOG2_E)).astype(LOW)
            p_ref[head, at, :] = weight
            part = dot(weight, vx[head * n : (head + 1) * n, :])
            result = part if result is None else result + part
        inv = 1.0 / result[:, 128:256]
        inv_ref[at, :] = inv
        o_ref[at, :] = (result[:, 0:128] * inv).astype(LOW)


def attend(places, q, k, v):
    pair = pl.BlockSpec((LEN, 128), lambda i, *_: (0, i))
    return call(
        attend_kernel,
        "attend_forward",
        (3,),
        [pair] * 3,
        [pair, pair, pl.BlockSpec((2, LEN, LEN), lambda i, *_: (i, 0, 0))],
        [shape((LEN, 384), LOW), shape((LEN, 384), WIDE), shape((6, LEN, LEN), LOW)],
        [pltpu.VMEM((2 * LEN, 256), LOW)],
        places,
        (q, k, v),
        4 * 6 * LEN * LEN * 256,
        vmem=12,
    )


def out_kernel(places, o, h0, h1, h2, h3, z, w_out, w_up, held):
    @pl.when(pl.program_id(0) == 0)
    def _():
        gather_blocks(places, (h0, h1, h2, h3), held)
        w_out[...] = to_pairs(held, D, D + 128)
        w_up[:, 0:D] = side_of(held, 0, 0, D)
        w_up[:, D : 2 * D] = side_of(held, 1, 0, D)

    z[...] = dot_nt(o[...], w_out[...]).astype(LOW)


def project_out(places, o, halves):
    step = 256
    return call(
        out_kernel,
        "project_out",
        (LEN // step,),
        [rows(step, 384)] + [whole(a) for a in halves],
        [rows(step, D), pl.BlockSpec((D, 384), lambda *_: (0, 0))]
        + [pl.BlockSpec((D, 2 * D), lambda *_: (0, 0))],
        [shape((LEN, D), LOW), shape((D, 384), LOW), shape((D, 2 * D), LOW)],
        [held_blocks(960)],
        places,
        (o, *halves),
        2 * LEN * D * 384,
    )


def normalize(hidden):
    centred = hidden - jnp.mean(hidden, axis=-1, keepdims=True)
    spread = lax.rsqrt(jnp.mean(centred * centred, axis=-1, keepdims=True) + EPS_NORM)
    return centred * spread, spread


def norm_back(grad_normed, normed, spread):
    return spread * (
        grad_normed
        - jnp.mean(grad_normed, axis=-1, keepdims=True)
        - normed * jnp.mean(grad_normed * normed, axis=-1, keepdims=True)
    )


def up_kernel(places, x, z, zp, vec, bias_mine, bias_other, w, m, slope, n1, rs1, low, bias):
    @pl.when(pl.program_id(0) == 0)
    def _():
        left, right = by_side(places, bias_mine[0:1, :], bias_other[0:1, :])
        bias[:, 0:D] = left
        bias[:, D : 2 * D] = right

    total = z[...].astype(WIDE) + zp[...].astype(WIDE)
    normed, spread = normalize(x[...].astype(WIDE) + total + vec[4:5, :])
    n1[...] = normed
    rs1[...] = jnp.broadcast_to(spread, rs1.shape)
    middle = (normed * vec[0:1, :] + vec[1:2, :]).astype(LOW)
    low[...] = middle
    for c in range(4):
        at = pl.ds(c * 384, 384)
        u = dot(middle, w[:, at]) + bias[0:1, at]
        half = 0.5 * (1.0 + lax.erf(u * 0.7071067811865476))
        m[:, at] = (u * half).astype(LOW)
        slope[:, at] = (half + u * (jnp.exp(-0.5 * u * u) * 0.3989422804014327)).astype(LOW)


def feed_up(places, tokens, z, zp, vec, bias, bias_other, w_up):
    step = 256
    args = (tokens, z, zp, vec, bias, bias_other, w_up)
    return call(
        up_kernel,
        "feed_up",
        (LEN // step,),
        [pl.BlockSpec((step, D), lambda i, places: (places[0] * (LEN // step) + i, 0))]
        + [rows(step, D)] * 2
        + [whole(a) for a in args[3:]],
        [rows(step, 2 * D)] * 2
        + [rows(step, D), rows(step, 128), rows(step, D)],
        [shape((LEN, 2 * D), LOW)] * 2
        + [shape((LEN, D), WIDE), shape((LEN, 128), WIDE), shape((LEN, D), LOW)],
        [pltpu.VMEM((1, 2 * D), WIDE)],
        places,
        args,
        2 * LEN * D * 2 * D,
    )


def down_kernel(places, m, h0, h1, h2, h3, f, w, pool, count, held):
    @pl.when(pl.program_id(0) == 0)
    def _():
        gather_blocks(places, (h0, h1, h2, h3), held)
        for side in range(2):
            w[:, D * side : D * (side + 1)] = side_of(held, side, 0, D)
        pool[...] = jnp.concatenate([side_of(held, side, D, 192) for side in range(2)], axis=1)
        live = jnp.sum(side_of(held, 0, D + 192, 64).astype(WIDE), axis=0, keepdims=True)
        count[...] = jnp.broadcast_to(live[:, 0:1], count.shape)

    f[...] = dot_nt(m[...], w[...]).astype(LOW)


def feed_down(places, m, halves):
    step = 256
    return call(
        down_kernel,
        "feed_down",
        (LEN // step,),
        [rows(step, 2 * D)] + [whole(a) for a in halves],
        [rows(step, D), pl.BlockSpec((D, 2 * D), lambda *_: (0, 0))]
        + [pl.BlockSpec((D, 384), lambda *_: (0, 0)), pl.BlockSpec((8, 128), lambda *_: (0, 0))],
        [shape((LEN, D), LOW), shape((D, 2 * D), LOW), shape((D, 384), LOW), shape((8, 128), WIDE)],
        [held_blocks(1024)],
        places,
        (m, *halves),
        2 * LEN * D * 2 * D,
    )


def turn_kernel(
    places, exit_layer, labels, n1, f, fp, cot, vec, pool_a, pool_b, classes, bias, live_count,
    y, half, dh2, low, sums, ramp, pool
):
    step = pl.program_id(0)
    middle = n1[...] * vec[0:1, :] + vec[1:2, :]
    total = f[...].astype(WIDE) + fp[...].astype(WIDE)
    normed, spread = normalize(middle + total + vec[5:6, :])
    result = normed * vec[2:3, :] + vec[3:4, :]
    low_result = result.astype(LOW)
    y[...] = low_result

    @pl.when(step // 2 == places[CORE_AT])
    def _():
        half[...] = low_result

    leaves = exit_layer[places[0]]
    grad = cot[...].astype(WIDE) * jnp.where(leaves > LAYER, 1.0, 0.0)
    dh2[...] = grad

    @pl.when(step == 0)
    def _():
        sums[...] = jnp.zeros_like(sums)
        own = places[CORE_AT]

        @pl.when(own == 0)
        def _():
            pool[:, 0:384] = pool_a[...]
            pool[:, 384:D] = pool_b[...]

        @pl.when(own == 1)
        def _():
            pool[:, 0:384] = pool_b[...]
            pool[:, 384:D] = pool_a[...]

        count = 16
        head = result[0:count, :].astype(LOW)
        pooled = jnp.tanh(dot(head, pool[...]) + vec[6:7, :])
        pooled_low = pooled.astype(LOW)
        lane = lax.broadcasted_iota(jnp.int32, (count, 128), 1)
        row = lax.broadcasted_iota(jnp.int32, (count, 128), 0)
        valid = lane < 3
        logits = dot(pooled_low, classes[...]) + bias[0:1, :]
        top = jnp.max(jnp.where(valid, logits, -jnp.inf), axis=1, keepdims=True)
        shifted = logits - top
        log_sum = jnp.log(
            jnp.sum(jnp.where(valid, jnp.exp(shifted), 0.0), axis=1, keepdims=True)
        )
        log_probs = jnp.where(valid, shifted - log_sum, 0.0)
        probs = jnp.where(valid, jnp.exp(log_probs), 0.0)
        live = jnp.where(leaves >= LAYER, 1.0, 0.0)
        entropy = -live * jnp.sum(probs * log_probs, axis=1, keepdims=True)
        onehot = jnp.where(lane == labels[places[0]], 1.0, 0.0)
        grad_logits = live * (probs - onehot) / live_count[0:1, 0:1]
        grad_logits = jnp.where(valid & (row == 0), grad_logits, 0.0).astype(LOW)
        grad_pre = (dot_nt(grad_logits, classes[...]) * (1.0 - pooled * pooled)).astype(LOW)
        grad_head = dot_nt(grad_pre, pool[...])
        dh2[0:count, :] = dh2[0:count, :] + grad_head
        sums[3:4, :] = grad_pre[0:1, :].astype(WIDE)
        of_class = dot_tn(grad_logits, pooled_low)
        sums[4:7, :] = of_class[0:3, :]
        last = jnp.where(lane == 3, entropy, grad_logits.astype(WIDE))
        sums[7:8, 0:128] = last[0:1, :]
        ramp[0:1, :] = head[0:1, :].astype(WIDE)
        ramp[1:2, :] = grad_pre[0:1, :].astype(WIDE)

    grad = dh2[...]
    sums[0:1, :] += jnp.sum(grad * normed, axis=0, keepdims=True)
    sums[1:2, :] += jnp.sum(grad, axis=0, keepdims=True)
    back = norm_back(grad * vec[2:3, :], normed, spread)
    sums[2:3, :] += jnp.sum(back, axis=0, keepdims=True)
    dh2[...] = back
    low[...] = back.astype(LOW)


def own_rows(step):
    return pl.BlockSpec((step, D), lambda i, places: (places[0] * (LEN // step) + i, 0))


def half_rows(step, sibling=False):
    count = LEN // step // 2

    def at(i, places):
        core = 1 - places[CORE_AT] if sibling else places[CORE_AT]
        return jnp.clip(i - count * core, 0, count - 1), 0

    return pl.BlockSpec((step, D), at)


def turn(places, exit_layer, labels, n1, f, fp, cotangent, vec, pool_a, pool_b, classes, bias, live_count):
    step = 256
    args = (exit_layer, labels, n1, f, fp, cotangent, vec, pool_a, pool_b, classes, bias, live_count)
    return call(
        turn_kernel,
        "turn",
        (LEN // step,),
        [pl.BlockSpec(memory_space=pltpu.SMEM)] * 2
        + [rows(step, D)] * 3
        + [own_rows(step)]
        + [whole(a) for a in args[6:]],
        [own_rows(step), half_rows(step)]
        + [rows(step, D)] * 2
        + [pl.BlockSpec((8, D), lambda *_: (0, 0))] * 2,
        [shape((2 * LEN, D), LOW), shape((LEN // 2, D), LOW)]
        + [shape((LEN, D), WIDE), shape((LEN, D), LOW)]
        + [shape((8, D), WIDE)] * 2,
        [pltpu.VMEM((D, D), LOW)],
        places,
        args,
        LEN * D * 60,
    )


def feed_back_kernel(places, dh2, slope, w_down, w_up, du, dx, sums):
    grad = dot(dh2[...], w_down[...]) * slope[...].astype(WIDE)
    grad = grad.astype(LOW)
    du[...] = grad
    dx[...] = dot_nt(grad, w_up[...]).astype(LOW)

    @pl.when(pl.program_id(0) == 0)
    def _():
        sums[...] = jnp.zeros_like(sums)

    sums[0:1, :] += jnp.sum(grad.astype(WIDE), axis=0, keepdims=True)


def feed_back(places, dh2, slope, w_down, w_up):
    step = 256
    args = (dh2, slope, w_down, w_up)
    return call(
        feed_back_kernel,
        "feed_back",
        (LEN // step,),
        [rows(step, D), rows(step, 2 * D), whole(w_down), whole(w_up)],
        [rows(step, 2 * D), rows(step, D), pl.BlockSpec((8, 2 * D), lambda *_: (0, 0))],
        [shape((LEN, 2 * D), LOW), shape((LEN, D), LOW), shape((8, 2 * D), WIDE)],
        [],
        places,
        args,
        4 * LEN * D * 2 * D,
    )


def feed_grad_kernel(places, dh2, m, middle, du, ramp, h0, h1, h2, h3, held, turned):
    for at, left, right in ((0, dh2, m), (D, middle, du)):
        turned[...] = left[...].T
        for side in range(2):
            for c in range(0, D, 256):
                part = dot(turned[...], right[:, D * side + c : D * side + c + 256]).astype(LOW)
                held[side * BLOCKS : (side + 1) * BLOCKS, :, at + c : at + c + 256] = part.reshape(
                    BLOCKS, BLOCK_ROWS, 256
                )
    row = lax.broadcasted_iota(jnp.int32, (BLOCK_ROWS, 256), 0)
    for group in range((held.shape[2] - 2 * D) // 256):
        slot = places[SLOT_AT] - 16 * group
        block = jnp.zeros((BLOCK_ROWS, 256), WIDE)
        for i in range(6):
            values = ramp[i // 3 : i // 3 + 1, 256 * (i % 3) : 256 * (i % 3 + 1)]
            mine = (row == 6 * slot + i) & (slot >= 0) & (slot < 16)
            block = jnp.where(mine, values, block)
        block = block.astype(LOW)
        at = 2 * D + 256 * group
        for p in range(2 * BLOCKS):
            held[p, :, at : at + 256] = block
    scatter_blocks(places, held, (h0, h1, h2, h3), ALONG)


def feed_grad(places, slots, dh2, m, middle, du, ramp):
    args = (dh2, m, middle, du, ramp)
    width = 2 * D + 16 * slots
    return call(
        feed_grad_kernel,
        "feed_grad",
        (1,),
        [whole(a) for a in args],
        half_specs(width),
        half_shapes(width),
        [held_blocks(width), pltpu.VMEM((D, LEN), LOW)],
        places,
        args,
        4 * LEN * D * 2 * D,
        vmem=12 if slots == 16 else 56,
    )


def mid_kernel(places, dh2, dx, dxp, n1, rs1, vec, w_out, turn_sums, up_sums, dh1, low, do, sums):
    @pl.when(pl.program_id(0) == 0)
    def _():
        sums[...] = jnp.zeros_like(sums)
        sums[0:8, :] = turn_sums[...]
        sums[11:12, :] = up_sums[0:1, 0:D]
        sums[12:13, :] = up_sums[0:1, D : 2 * D]

    total = dx[...].astype(WIDE) + dxp[...].astype(WIDE)
    grad = dh2[...] + total
    normed = n1[...]
    sums[8:9, :] += jnp.sum(grad * normed, axis=0, keepdims=True)
    sums[9:10, :] += jnp.sum(grad, axis=0, keepdims=True)
    back = norm_back(grad * vec[0:1, :], normed, rs1[:, 0:1])
    sums[10:11, :] += jnp.sum(back, axis=0, keepdims=True)
    dh1[...] = back
    back_low = back.astype(LOW)
    low[...] = back_low
    do[...] = dot(back_low, w_out[...]).astype(LOW)


def mid(places, dh2, dx, dxp, n1, rs1, vec, w_out, turn_sums, up_sums):
    step = 256
    args = (dh2, dx, dxp, n1, rs1, vec, w_out, turn_sums, up_sums)
    count = 16
    return call(
        mid_kernel,
        "middle_back",
        (LEN // step,),
        [rows(step, D)] * 4 + [rows(step, 128)] + [whole(a) for a in args[5:]],
        [rows(step, D)] * 2 + [rows(step, 384), pl.BlockSpec((count, D), lambda *_: (0, 0))],
        [shape((LEN, D), WIDE), shape((LEN, D), LOW), shape((LEN, 384), LOW), shape((count, D), WIDE)],
        [],
        places,
        args,
        2 * LEN * D * 384,
    )


def attend_back_kernel(
    places, q_ref, k_ref, v_ref, do_ref, inv_ref, p_ref, dq_ref, dk_ref, dv_ref, ds_ref, held
):
    first = first_of_pair()
    zero = jnp.zeros((), LOW)
    n = k_ref.shape[0]
    k = k_ref[...]
    v = v_ref[...]
    k_own = [jnp.where(first, k, zero), jnp.where(first, zero, k)]
    scaled = (do_ref[...].astype(WIDE) * inv_ref[...]).astype(LOW)
    held[...] = scaled
    step = 256
    for i in range(n // step):
        at = pl.ds(i * step, step)
        d = held[at, :]
        total = None
        for head in range(2):
            mine = jnp.where(first, d, zero) if head == 0 else jnp.where(first, zero, d)
            grad_weight = dot_nt(mine, v)
            weight = p_ref[head, at, :].astype(WIDE)
            product = weight * grad_weight
            inner = jnp.sum(product, axis=1, keepdims=True)
            inner = inner * inv_ref[at, pl.ds(HD * head, 1)]
            grad_score = (product - weight * inner).astype(LOW)
            ds_ref[head, at, :] = grad_score
            part = dot(grad_score, k_own[head])
            total = part if total is None else total + part
        dq_ref[at, :] = (total * HD**-0.5).astype(LOW)
    scaled_t = scaled.T
    q_t = q_ref[...].T
    grad_v = jnp.concatenate(
        [dot(scaled_t[0:HD], p_ref[0]), dot(scaled_t[HD : 2 * HD], p_ref[1])], axis=0
    )
    dv_ref[...] = grad_v.T.astype(LOW)
    grad_k = jnp.concatenate(
        [dot(q_t[0:HD], ds_ref[0]), dot(q_t[HD : 2 * HD], ds_ref[1])], axis=0
    )
    dk_ref[...] = (grad_k * HD**-0.5).T.astype(LOW)


def attend_back(places, q, k, v, do, inv, p):
    at = pl.BlockSpec((LEN, 128), lambda i, *_: (0, i))
    return call(
        attend_back_kernel,
        "attend_backward",
        (3,),
        [at] * 5 + [pl.BlockSpec((2, LEN, LEN), lambda i, *_: (i, 0, 0))],
        [at] * 3,
        [shape((LEN, 384), LOW)] * 3,
        [pltpu.VMEM((2, LEN, LEN), LOW), pltpu.VMEM((LEN, 128), LOW)],
        places,
        (q, k, v, do, inv, p),
        8 * 6 * LEN * LEN * 256,
        vmem=18,
    )


MARK_ROWS = 6


def narrow_grad_kernel(places, left, dh1, o, dq, dk, dv, sums, h0, h1, h2, h3, held, turned, marks):
    turned[...] = left[...].T
    marks[...] = jnp.zeros_like(marks)
    for i, right in enumerate((dq, dk, dv)):
        value = right[...]
        from_pairs(dot(turned[...], value).astype(LOW), held, 128 * i, 512 + 64 * i)
        if i != 1:
            total = jnp.sum(value.astype(WIDE), axis=0, keepdims=True)
            for k in range(3):
                at = 13 * MARK_ROWS + 3 * (i // 2) + k
                marks[at : at + 1, :] = total[:, 128 * k : 128 * (k + 1)]
    turned[...] = dh1[...].T
    from_pairs(dot(turned[...], o[...]).astype(LOW), held, 384, 704)
    for i in range(13):
        for k in range(MARK_ROWS):
            at = i * MARK_ROWS + k
            marks[at : at + 1, :] = sums[i : i + 1, 128 * k : 128 * (k + 1)]
    block = marks[...].astype(LOW)
    for p in range(2 * BLOCKS):
        held[p, :, D : D + 128] = block
    scatter_blocks(places, held, (h0, h1, h2, h3), ALONG)


def narrow_grad(places, tokens, dh1, o, grads, sums):
    args = (tokens, dh1, o, *grads, sums)
    width = D + 128
    return call(
        narrow_grad_kernel,
        "narrow_grad",
        (1,),
        [own_rows(LEN)] + [whole(a) for a in args[1:]],
        half_specs(width),
        half_shapes(width),
        [held_blocks(width), pltpu.VMEM((D, LEN), LOW), pltpu.VMEM((BLOCK_ROWS, 128), WIDE)],
        places,
        args,
        2 * LEN * D * 1536,
        vmem=9,
    )


def input_kernel(places, *refs):
    grads, w, (keep, send) = refs[:3], refs[3], refs[4:]
    total = None
    for i in range(3):
        part = dot_nt(grads[i][...], w[i])
        total = part if total is None else total + part
    total = total.astype(LOW)
    mine = pl.program_id(0) // 2 == places[CORE_AT]

    @pl.when(mine)
    def _():
        keep[...] = total

    @pl.when(jnp.logical_not(mine))
    def _():
        send[...] = total


def input_grad(places, grads, w):
    step = 256
    return call(
        input_kernel,
        "input_grad",
        (LEN // step,),
        [rows(step, 384)] * 3 + [whole(w)],
        [half_rows(step), half_rows(step, True)],
        [shape((LEN // 2, D), LOW)] * 2,
        [],
        places,
        (*grads, w),
        2 * LEN * D * 1152,
    )


def finish_kernel(places, dh1, keep, other, half):
    total = keep[...].astype(WIDE) + other[...].astype(WIDE)
    half[...] = (dh1[...] + total).astype(LOW)


def finish(places, dh1, keep, other):
    step = 128
    count = LEN // 2 // step
    return call(
        finish_kernel,
        "finish",
        (count,),
        [pl.BlockSpec((step, D), lambda i, places: (count * places[CORE_AT] + i, 0))]
        + [rows(step, D)] * 2,
        [rows(step, D)],
        [shape((LEN // 2, D), LOW)],
        [],
        places,
        (dh1, keep, other),
        LEN * D * 3,
    )[0]


def place_kernel(count, places, *refs):
    half = LEN // 2
    ins, out, sems = refs[-2 - count : -2], refs[-2], refs[-1]
    side, core = places[0], places[CORE_AT]
    at = [(1 - side, core), (1 - side, 1 - core), (side, core), (side, 1 - core)]
    copies = []
    for i, ref in enumerate(ins):
        first = pl.multiple_of((2 * at[i][0] + at[i][1]) * half, half)
        copies.append(pltpu.make_async_copy(ref, out.at[pl.ds(first, half)], sems.at[i]))
        copies[-1].start()
    for copy in copies:
        copy.wait()


def place(places, kept, quarters):
    first = [] if kept is None else [kept]
    return call(
        functools.partial(place_kernel, len(quarters)),
        "place",
        (1,),
        [pl.BlockSpec(memory_space=pl.ANY)] * len(first) + [whole(a) for a in quarters],
        [pl.BlockSpec(memory_space=pl.ANY)],
        [shape((2 * LEN, D), LOW)],
        [pltpu.SemaphoreType.DMA((len(quarters),))],
        places,
        (*first, *quarters),
        1,
        vmem=12,
        aliases={} if kept is None else {1: 0},
    )[0]


def update(places, name, pieces, width, ins, kernel, outs, scratch):
    counts = tuple(len(group) for group in pieces)
    args = [a for group in pieces for a in group]
    specs = [
        pl.BlockSpec((1, a.shape[1], width), lambda *_: (0, 0, 0)) if a.ndim == 3 else whole(a)
        for a in args
    ]
    return call(
        functools.partial(kernel, counts),
        name,
        (1,),
        specs + [whole(a) for a in ins],
        [whole(o) for o in outs],
        outs,
        scratch,
        places,
        (*args, *ins),
        1,
        vmem=60,
    )


def matrix_outs(weight):
    return [shape(weight.shape, WIDE)] * 3 + [shape(weight.shape, LOW)]


def step_matrix(ins, outs, at, grad, rate):
    new, first, second = adamw(ins[0][at], ins[1][at], ins[2][at], grad, rate, DECAY)
    outs[0][at] = new
    outs[1][at] = first
    outs[2][at] = second
    outs[3][at] = new.astype(LOW)


def step_vector(ins, outs, at, grad, rate=VECTOR_RATE, decay=0.0):
    results = adamw(ins[0][at], ins[1][at], ins[2][at], grad, rate, decay)
    for out, result in zip(outs, results, strict=True):
        out[at] = result


def update_feed_kernel(counts, places, *refs):
    total = sum(counts)
    grad, marks = sum_pieces(refs[:total], counts, 2 * D)
    ins, outs = refs[total : total + 9], refs[total + 9 : total + 21]
    heads, slopes = refs[total + 21 :]
    step_matrix(ins[0:3], outs[0:4], ..., grad[:, 0:D], RATE * FF ** (-0.5))
    step_matrix(ins[3:6], outs[4:8], ..., grad[:, D : 2 * D], RATE * D ** (-0.5))
    for s in range(heads.shape[0]):
        at = 256 * (s // 16)
        for i, target in enumerate((heads, slopes)):
            for k in range(3):
                row = 6 * (s % 16) + 3 * i + k
                target[s : s + 1, 256 * k : 256 * (k + 1)] = marks[row : row + 1, at : at + 256]
    share = ins[6].shape[0]
    column = lax.broadcasted_iota(jnp.int32, (D, share), 0)
    own = column == lax.broadcasted_iota(jnp.int32, (D, share), 1) + places[DP_AT] * share
    picked = dot(heads[...].astype(LOW), jnp.where(own, 1.0, 0.0).astype(LOW)).astype(LOW)
    pool = dot_tn(picked, slopes[...].astype(LOW))
    step_matrix(ins[6:9], outs[8:12], ..., pool, RATE * D ** (-0.5))


def update_narrow_kernel(counts, places, *refs):
    total = sum(counts)
    grad, marks = sum_pieces(refs[:total], counts, D)
    ins, outs = refs[total : total + 19], refs[total + 19 : total + 40]
    rows_of = refs[total + 40]

    def columns(i):
        return jnp.concatenate(
            [grad[:, 128 * i : 128 * (i + 1)], grad[:, 512 + 64 * i : 576 + 64 * i]], axis=1
        )

    for i in range(3):
        step_matrix(ins[0:3], outs[0:4], i, columns(i), RATE * D ** (-0.5))
    step_matrix(ins[3:6], outs[4:8], ..., columns(3).T, RATE * max(1, 2 * D // LEN) ** (-0.5))
    for i in range(14):
        for k in range(MARK_ROWS):
            at = i * MARK_ROWS + k
            rows_of[i : i + 1, 128 * k : 128 * (k + 1)] = marks[at : at + 1, :]
    side = places[0]
    pairs = rows_of[13:14, :]
    for i in range(2):
        pair = pairs[:, 384 * i : 384 * (i + 1)]
        wide = jnp.where(side == 0, pair[:, 0:128], pair[:, 128:256])
        narrow = jnp.where(side == 0, pair[:, 256:320], pair[:, 320:384])
        own = jnp.concatenate([wide, narrow], axis=1)
        step_vector(ins[6:9], outs[8:11], pl.ds(i, 1), own)
    hidden = jnp.where(side == 0, rows_of[11:12, :], rows_of[12:13, :])
    step_vector(ins[9:12], outs[11:14], ..., hidden.reshape(D))
    for i, at in enumerate((8, 9, 0, 1, 10, 2, 3)):
        step_vector(ins[12:15], outs[14:17], pl.ds(i, 1), rows_of[at : at + 1, :])
    for i in range(3):
        one = jnp.concatenate([rows_of[4 + i : 5 + i, :], rows_of[7:8, i : i + 1]], axis=1)
        step_vector(
            ins[15:18], outs[17:20], pl.ds(i, 1), one, RATE * (D // 4) ** (-0.5), DECAY
        )
    outs[20][...] = rows_of[7:8, 3:4] / ins[18][0:1, 0:1]


def per_device(
    dp_count,
    mp_count,
    tokens,
    cotangent,
    exit_layer,
    labels,
    qkv_weight,
    qkv_first,
    qkv_second,
    out_weight,
    out_first,
    out_second,
    up_weight,
    up_first,
    up_second,
    down_weight,
    down_first,
    down_second,
    pool_weight,
    pool_first,
    pool_second,
    qv_bias,
    qv_first,
    qv_second,
    up_bias,
    upb_first,
    upb_second,
    layer_vectors,
    vector_first,
    vector_second,
    class_weight,
    class_first,
    class_second,
):
    links = Links(dp_count, mp_count)
    side, core = links.side, links.core

    slot = 2 * links.dp + side
    places = jnp.concatenate(
        [side[None], links.places(), core[None], slot[None], links.dp[None]]
    ).astype(jnp.int32)
    share = D // dp_count

    by_kind = [a.transpose(1, 0, 2) for a in (qkv_weight, qkv_first, qkv_second)]
    down_turned = [a.T for a in (down_weight, down_first, down_second)]
    qkv_spread = links.spread(pack_first(by_kind[0]))
    sent = qkv_spread.step()
    up_out, down_pool, biases = pack(
        places,
        exit_layer,
        after(up_weight, *sent),
        out_weight,
        down_turned[0],
        pool_weight,
        qv_bias,
        up_bias,
    )
    other_biases = links.swap(biases, SIDE)
    qkv_z = tuple(qkv_spread.last)
    sent = qkv_spread.step(up_out, other_biases)
    up_out_spread = links.spread(up_out)
    up_out_spread.step(*qkv_z)
    class_low = after(class_weight, *sent)
    classes = jnp.pad(class_low[:D].astype(LOW), ((0, 0), (0, 125)))
    class_bias = jnp.pad(class_low[D:], ((0, 0), (0, 125)))
    sent = qkv_spread.step(classes, class_bias)
    sent = up_out_spread.step(*sent)
    down_spread = links.spread(down_pool)
    sent = down_spread.step(*sent)

    biases = after(biases, *sent)
    q, k, v, w_qkv = project(places, tokens, biases, other_biases, qkv_spread.halves())
    sent = up_out_spread.step(q)
    q = after(q, *sent)
    o, inv, p = attend(places, q, k, v)
    sent = down_spread.step(o)
    o = after(o, *sent)
    z, w_out, w_up = project_out(places, o, up_out_spread.halves())
    zp = links.swap(z, CORE)
    sent = down_spread.step(z)
    z = after(z, *sent)
    m, slope, n1, rs1, middle_low = feed_up(
        places, tokens, z, zp, layer_vectors, biases, other_biases, w_up
    )
    f, w_down, pool_mine, live_count = feed_down(places, m, down_spread.halves())
    fp = links.swap(f, CORE)
    pool_other = links.swap(pool_mine, CORE)
    y, y_half, dh2, dh2_low, turn_sums, ramp = turn(
        places, exit_layer, labels, n1, f, fp, cotangent, layer_vectors, pool_mine, pool_other,
        classes, class_bias, live_count,
    )

    y_first = links.swap(y_half, SIDE)
    du, dx, up_sums = feed_back(places, dh2_low, slope, w_down, w_up)
    dxp = links.swap(dx, CORE)
    m, dh2_low = after((m, dh2_low), dx)
    slots = 2 * dp_count
    feed_halves = feed_grad(places, slots, dh2_low, m, middle_low, du, ramp)
    feed_fold = links.fold(feed_halves, ALONG, 2 * D)
    feed_fold.step()
    dx = after(dx, *feed_halves)
    dh1, dh1_low, do, sums = mid(
        places, dh2, dx, dxp, n1, rs1, layer_vectors, w_out, turn_sums, up_sums
    )
    grads = attend_back(places, q, k, v, do, inv, p)
    token_keep, token_send = input_grad(places, grads, w_qkv)
    token_other = links.swap(token_send, CORE)
    sent = feed_fold.step(token_keep, y_first)
    grads = after(grads, *sent)
    narrow_halves = narrow_grad(places, tokens, dh1_low, o, grads, sums)
    narrow_fold = links.fold(narrow_halves, ALONG, D)
    narrow_fold.step()
    token_keep = after(token_keep, *narrow_halves)
    grad_half = finish(places, dh1, token_keep, token_other)
    first = links.swap(grad_half, SIDE)
    second_own = links.swap(grad_half, CORE)
    sent = feed_fold.step(grad_half)
    sent = narrow_fold.step(*sent)
    sent = feed_fold.step(*sent)
    sent = narrow_fold.step(*sent)
    first, y_first = after((first, y_first), *sent)
    second, y_second = links.swap(first, CORE), links.swap(y_first, CORE)
    tokens_grad = place(places, None, [first, second, grad_half, second_own])
    result = place(places, y, [y_first, after(y_second, tokens_grad)])
    sent = narrow_fold.step(result)
    by_class = [a.T for a in (class_weight, class_first, class_second)]
    masters = [*by_kind, out_weight, out_first, out_second]
    vectors = [qv_bias, qv_first, qv_second, up_bias, upb_first, upb_second]
    vectors += [layer_vectors, vector_first, vector_second, *by_class]
    narrow_new = update(
        places,
        "update_narrow",
        narrow_fold.pieces(),
        D + 128,
        [*masters, *vectors, live_count],
        update_narrow_kernel,
        [o for a in masters[0::3] for o in matrix_outs(a)]
        + [shape(a.shape, WIDE) for a in vectors]
        + [shape((1, 1), WIDE)],
        [pltpu.VMEM((16, D), WIDE)],
    )
    masters = [*down_turned, up_weight, up_first, up_second, pool_weight, pool_first, pool_second]
    feed_new = update(
        places,
        "update_feed",
        after(feed_fold.pieces(), narrow_new[0]),
        2 * D + 16 * slots,
        masters,
        update_feed_kernel,
        [o for a in masters[0::3] for o in matrix_outs(a)],
        [pltpu.VMEM((slots, D), WIDE)] * 2,
    )
    down_new, down_first_new, down_second_new, down_copy = (a.T for a in feed_new[0:4])
    up_new, up_first_new, up_second_new, up_copy = feed_new[4:8]
    pool_new, pool_first_new, pool_second_new, pool_copy = feed_new[8:12]
    qkv_new, qkv_first_new, qkv_second_new, qkv_copy = (
        a.transpose(1, 0, 2) for a in narrow_new[0:4]
    )
    out_new, out_first_new, out_second_new, out_copy = narrow_new[4:8]
    qv_new, qv_first_new, qv_second_new = narrow_new[8:11]
    upb_new, upb_first_new, upb_second_new = narrow_new[11:14]
    vector_new, vector_first_new, vector_second_new = narrow_new[14:17]
    class_new, class_first_new, class_second_new = (a.T for a in narrow_new[17:20])
    entropy = narrow_new[20].reshape(())
    return (
        result,
        tokens_grad,
        entropy,
        qkv_new,
        qkv_first_new,
        qkv_second_new,
        qkv_copy,
        out_new,
        out_first_new,
        out_second_new,
        out_copy,
        up_new,
        up_first_new,
        up_second_new,
        up_copy,
        down_new,
        down_first_new,
        down_second_new,
        down_copy,
        pool_new,
        pool_first_new,
        pool_second_new,
        pool_copy,
        qv_new,
        qv_first_new,
        qv_second_new,
        upb_new,
        upb_first_new,
        upb_second_new,
        vector_new,
        vector_first_new,
        vector_second_new,
        class_new,
        class_first_new,
        class_second_new,
    )


def solution(mesh):
    in_specs = (
        P("dp", None),
        P("dp", None),
        P("dp"),
        P("dp"),
        P("dp", None, "mp"),
        P("dp", None, "mp"),
        P("dp", None, "mp"),
        P("mp", "dp"),
        P("mp", "dp"),
        P("mp", "dp"),
        P("dp", "mp"),
        P("dp", "mp"),
        P("dp", "mp"),
        P("mp", "dp"),
        P("mp", "dp"),
        P("mp", "dp"),
        P("dp", None),
        P("dp", None),
        P("dp", None),
        P(None, "mp"),
        P(None, "mp"),
        P(None, "mp"),
        P("mp"),
        P("mp"),
        P("mp"),
        P(),
        P(),
        P(),
        P(),
        P(),
        P(),
    )
    out_specs = (
        P("dp", None),
        P("dp", None),
        P(),
        P("dp", None, "mp"),
        P("dp", None, "mp"),
        P("dp", None, "mp"),
        P("dp", None, "mp"),
        P("mp", "dp"),
        P("mp", "dp"),
        P("mp", "dp"),
        P("mp", "dp"),
        P("dp", "mp"),
        P("dp", "mp"),
        P("dp", "mp"),
        P("dp", "mp"),
        P("mp", "dp"),
        P("mp", "dp"),
        P("mp", "dp"),
        P("mp", "dp"),
        P("dp", None),
        P("dp", None),
        P("dp", None),
        P("dp", None),
        P(None, "mp"),
        P(None, "mp"),
        P(None, "mp"),
        P("mp"),
        P("mp"),
        P("mp"),
        P(),
        P(),
        P(),
        P(),
        P(),
        P(),
    )
    one_device = functools.partial(per_device, mesh.shape["dp"], mesh.shape["mp"])
    return jax.shard_map(
        one_device, mesh=mesh, in_specs=in_specs, out_specs=out_specs, check_vma=False
    )
```

```python
import functools

import jax
import jax.numpy as jnp
import numpy as np
from jax import lax
from jax.experimental import pallas as pl
from jax.experimental.pallas import tpu as pltpu
from jax.sharding import PartitionSpec as P

D = 768
HD = 64
FF = 3072
LAYER = 6
STEP = 10
LEN = 1024


EPS_NORM = 1e-06
BETA_ONE = 0.9
BETA_TWO = 0.98
EPS_ADAM = 1e-08
DECAY = 0.01
RATE = 0.8
VECTOR_RATE = 0.3

LOW = jnp.bfloat16
WIDE = jnp.float32
LOG2_E = 1.4426950408889634
MIB = 2**20
COST_SCALE = 16

CORE, SIDE, X_BIT, Z_LOW, Z_HIGH = 1, 2, 4, 8, 16
BLOCKS = 8
BLOCK_ROWS = D // BLOCKS
PART_ROWS = BLOCK_ROWS // 2
ACROSS = ((Z_HIGH, Z_LOW, X_BIT, SIDE), (Z_HIGH, Z_LOW, SIDE, X_BIT))
ALONG = ((Z_HIGH, Z_LOW, SIDE, X_BIT), (SIDE, Z_HIGH, X_BIT, Z_LOW))
Z_LINE = (Z_HIGH, Z_LOW, Z_HIGH | Z_LOW)
BESIDE = ((Z_HIGH, Z_LOW, SIDE, X_BIT), (Z_HIGH, SIDE, X_BIT, Z_LOW))
ROUTES = (ACROSS, ALONG, BESIDE)


def dot(left, right):
    return lax.dot_general(
        left, right, (((1,), (0,)), ((), ())), preferred_element_type=WIDE
    )


def dot_nt(left, right):
    return lax.dot_general(
        left, right, (((1,), (1,)), ((), ())), preferred_element_type=WIDE
    )


def dot_tn(left, right):
    return lax.dot_general(
        left, right, (((0,), (0,)), ((), ())), preferred_element_type=WIDE
    )


def adamw(weight, first, second, grad, rate, decay):
    first_new = BETA_ONE * first + (1.0 - BETA_ONE) * grad
    second_new = BETA_TWO * second + (1.0 - BETA_TWO) * grad * grad
    first_hat = first_new / (1.0 - BETA_ONE**STEP)
    second_hat = second_new / (1.0 - BETA_TWO**STEP)
    weight_new = weight - rate * (first_hat / (jnp.sqrt(second_hat) + EPS_ADAM) + decay * weight)
    return (weight_new, first_new, second_new)


class Links:
    def __init__(self, dp_count, mp_count):
        self.dp_count = dp_count
        self.total = dp_count * mp_count
        self.cube = dp_count == BLOCKS
        self.dp = lax.axis_index("dp").astype(jnp.int32)
        mp = lax.axis_index("mp").astype(jnp.int32)
        self.side = mp // 2
        self.core = mp % 2

    def swap(self, value, bit):
        pairs = [(i, i ^ bit) for i in range(self.total)]
        return lax.ppermute(value, ("dp", "mp"), pairs)

    def places(self):
        flips = []
        for order in sum(ROUTES, ()):
            for j in range(2 * BLOCKS):
                if self.cube:
                    bits = 0
                    for k, bit in enumerate(order):
                        bits ^= bit if (j >> k) & 1 else 0
                    flips.append((bits // SIDE & 1, bits // X_BIT))
                else:
                    flips.append((j // BLOCKS, j % BLOCKS))
        flips = np.array(flips, np.int32)
        mine = self.dp if self.cube else 0
        return (self.side ^ flips[:, 0]) * BLOCKS + (mine ^ flips[:, 1])

    def spread(self, share):
        return (Spread if self.cube else WholeSpread)(self, share)

    def fold(self, halves, route, base):
        return (Fold if self.cube else WholeFold)(self, halves, route, base)


class Spread:
    def __init__(self, links, share):
        self.links = links
        self.held = [share[None]]
        self.last = None
        self.round = 0

    def step(self, *others):
        links = self.links
        if others:
            (self.held, self.last), *_ = lax.optimization_barrier(((self.held, self.last), *others))
        if self.round == 0:
            self.last = [links.swap(self.held[0], bits) for bits in Z_LINE]
        elif self.round == 1:
            line = [self.held[0], *self.last]
            at = (slice(0, PART_ROWS), slice(PART_ROWS, BLOCK_ROWS))
            self.held = [jnp.concatenate([a[:, i] for a in line], axis=0) for i in at]
        else:
            self.held = [
                jnp.concatenate([mine, other], axis=0)
                for mine, other in zip(self.held, self.last, strict=True)
            ]
        if self.round:
            self.last = [
                links.swap(part, ACROSS[i][self.round + 1]) for i, part in enumerate(self.held)
            ]
        self.round += 1
        return tuple(self.held)

    def halves(self):
        return (self.held[0], self.last[0], self.held[1], self.last[1])


class WholeSpread:
    def __init__(self, links, share):
        self.last = ()
        near = lax.all_gather(share, "dp", axis=0, tiled=True)
        near = near.reshape(BLOCKS, BLOCK_ROWS, share.shape[1])
        far = links.swap(near, SIDE)
        self.parts = (
            near[:, :PART_ROWS],
            far[:, :PART_ROWS],
            near[:, PART_ROWS:],
            far[:, PART_ROWS:],
        )

    def step(self, *others):
        return ()

    def halves(self):
        return self.parts


class Fold:
    def __init__(self, links, halves, route, base):
        self.links = links
        self.route = route
        self.base = base
        self.parts = [[halves[0]], [halves[2]]]
        self.far = [halves[1], halves[3]]
        self.joined = []
        self.round = 0

    def step(self, *others, vmem=16):
        links, k = self.links, 3 - self.round
        if others:
            (self.parts, self.joined, self.far), *_ = lax.optimization_barrier(
                ((self.parts, self.joined, self.far), *others)
            )
        if self.route is ACROSS and self.round == 2:
            sent = fold_add(self.parts, 2, False, self.base, vmem)
            self.joined = [links.swap(a, bits) for a, bits in zip(sent, Z_LINE, strict=True)]
        else:
            if self.round == 0:
                sent = self.far
            else:
                sent = fold_add(self.parts, 2**k, True, self.base, vmem)
            for i, order in enumerate(self.route):
                self.parts[i].append(links.swap(sent[i], order[k]))
        self.round += 1
        return tuple(sent)

    def pieces(self):
        return (self.parts[0], self.parts[1], self.joined)


class WholeFold:
    def __init__(self, links, halves, route, base):
        near, far = (
            jnp.concatenate([halves[i], halves[i + 2]], axis=1).reshape(D, -1) for i in range(2)
        )
        total = near.astype(WIDE) + links.swap(far, SIDE).astype(WIDE)
        share = lax.psum_scatter(total[:, :base], "dp", scatter_dimension=0, tiled=True)
        self.parts = [share, lax.psum(total[:BLOCK_ROWS, base:], "dp")]

    def step(self, *others, vmem=16):
        return ()

    def pieces(self):
        return ([], [], self.parts)


def add_marked(refs, at, base):
    total = sum(ref[at, :, 0:base].astype(WIDE) for ref in refs)
    marks = refs[0][at, :, base:].astype(WIDE)
    for ref in refs[1:]:
        marks = marks.astype(LOW).astype(WIDE) + ref[at, :, base:].astype(WIDE)
    return total, marks


def sum_pieces(refs, counts, base, at=0):
    first, second, joined = counts
    if not first:
        return refs[0][...], refs[1][...]
    tops = add_marked(refs[:first], at, base)
    ends = add_marked(refs[first : first + second], at, base)
    total, marks = (jnp.concatenate(pair, axis=0) for pair in zip(tops, ends, strict=True))
    joints = refs[first + second :]
    for ref in joints:
        total = total + ref[at, :, 0:base].astype(WIDE)
    if joints:
        high, low, both = (ref[at, :, base:].astype(WIDE) for ref in joints)
        marks = (marks.astype(LOW).astype(WIDE) + high) + (low + both)
    return total, marks


def fold_add_kernel(count, half, apart, base, *refs):
    ins, outs = refs[: 2 * count], refs[2 * count :]
    if apart:
        for i in range(half):
            for j in range(2):
                total, marks = add_marked(ins[j * count : (j + 1) * count], i, base)
                outs[j][i, :, 0:base] = total.astype(LOW)
                outs[j][i, :, base:] = marks.astype(LOW)
    else:
        for i, out in enumerate(outs):
            total, marks = sum_pieces(ins, (count, count, 0), base, i + 1)
            out[0, :, 0:base] = total.astype(LOW)
            out[0, :, base:] = marks.astype(LOW)


def fold_add(parts, half, apart, base, vmem):
    args = [*parts[0], *parts[1]]
    width = args[0].shape[2]
    if apart:
        outs = [shape((half, PART_ROWS, width), LOW)] * 2
        specs = [pl.BlockSpec((half, PART_ROWS, width), lambda i: (1, 0, 0))] * len(args)
    else:
        outs = [shape((1, BLOCK_ROWS, width), LOW)] * 3
        specs = [pl.BlockSpec((4, PART_ROWS, width), lambda i: (0, 0, 0))] * len(args)
    return pl.pallas_call(
        functools.partial(fold_add_kernel, len(parts[0]), half, apart, base),
        grid=(1,),
        in_specs=specs,
        out_specs=[pl.BlockSpec(o.shape, lambda i: (0, 0, 0)) for o in outs],
        out_shape=outs,
        compiler_params=pltpu.CompilerParams(vmem_limit_bytes=vmem * MIB),
        cost_estimate=pl.CostEstimate(
            flops=half * BLOCK_ROWS * width, bytes_accessed=half * width, transcendentals=0
        ),
        name="fold_add",
    )(*args)


def after(value, *others):
    return lax.optimization_barrier((value, *others))[0]


def call(kernel, name, grid, in_specs, out_specs, out_shape, scratch, places, args, flops, vmem=10, aliases=None):
    moved = sum(a.size * a.dtype.itemsize for a in args)
    moved += sum(int(np.prod(s.shape)) * np.dtype(s.dtype).itemsize for s in out_shape)
    return pl.pallas_call(
        kernel,
        out_shape=out_shape,
        grid_spec=pltpu.PrefetchScalarGridSpec(
            num_scalar_prefetch=1,
            grid=grid,
            in_specs=in_specs,
            out_specs=out_specs,
            scratch_shapes=scratch,
        ),
        input_output_aliases=aliases or {},
        compiler_params=pltpu.CompilerParams(vmem_limit_bytes=vmem * MIB),
        cost_estimate=pl.CostEstimate(
            flops=int(flops) // COST_SCALE, bytes_accessed=int(moved) // COST_SCALE, transcendentals=0
        ),
        name=name,
    )(places, *args)


def whole(array):
    return pl.BlockSpec(array.shape, lambda *_: (0,) * len(array.shape))


def rows(count, width):
    return pl.BlockSpec((count, width), lambda i, *_: (i, 0))


def shape(dims, kind):
    return jax.ShapeDtypeStruct(dims, kind)


def gather_blocks(places, halves, held, route=ACROSS):
    for i in range(2):
        for j in range(2 * BLOCKS):
            source = halves[2 * i + j // BLOCKS]
            target = places[1 + 2 * BLOCKS * (2 * ROUTES.index(route) + i) + j]
            held[target, i * PART_ROWS : (i + 1) * PART_ROWS, :] = source[j % BLOCKS]


def scatter_blocks(places, held, halves, route=ACROSS):
    for i in range(2):
        for j in range(2 * BLOCKS):
            target = halves[2 * i + j // BLOCKS]
            source = places[1 + 2 * BLOCKS * (2 * ROUTES.index(route) + i) + j]
            target[j % BLOCKS] = held[source, i * PART_ROWS : (i + 1) * PART_ROWS, :]


CORE_AT = 1 + 4 * BLOCKS * len(ROUTES)
SLOT_AT = CORE_AT + 1
DP_AT = CORE_AT + 2


def side_of(held, side, at, width):
    return held[side * BLOCKS : (side + 1) * BLOCKS, :, at : at + width].reshape(D, width)


def to_pairs(held, wide_at, narrow_at):
    return jnp.concatenate(
        [side_of(held, side, wide_at, 128) for side in range(2)]
        + [side_of(held, side, narrow_at, 64) for side in range(2)],
        axis=1,
    )


def from_pairs(value, held, wide_at, narrow_at):
    for side in range(2):
        at = slice(side * BLOCKS, (side + 1) * BLOCKS)
        wide = value[:, 128 * side : 128 * (side + 1)]
        held[at, :, wide_at : wide_at + 128] = wide.reshape(BLOCKS, BLOCK_ROWS, 128)
        narrow = value[:, 256 + 64 * side : 320 + 64 * side]
        held[at, :, narrow_at : narrow_at + 64] = narrow.reshape(BLOCKS, BLOCK_ROWS, 64)


def half_shapes(width):
    return [shape((BLOCKS, PART_ROWS, width), LOW)] * 4


def half_specs(width):
    return [pl.BlockSpec((BLOCKS, PART_ROWS, width), lambda *_: (0, 0, 0))] * 4


def held_blocks(width):
    return pltpu.VMEM((2 * BLOCKS, BLOCK_ROWS, width), LOW)


def pack_first_kernel(w, exit_layer, out):
    wide = [w[i][:, :128] for i in range(3)]
    narrow = [w[i][:, 128:] for i in range(3)]
    live = jnp.float32(0.0)
    for i in range(exit_layer.shape[0]):
        live += jnp.where(exit_layer[i] >= LAYER, 1.0, 0.0)
    row = lax.broadcasted_iota(jnp.int32, (out.shape[0], 64), 0)
    marks = jnp.where(row == 0, live, 0.0)
    out[...] = jnp.concatenate(wide + narrow + [marks], axis=1).astype(LOW)


def pack_first(qkv, exit_layer):
    return pl.pallas_call(
        pack_first_kernel,
        in_specs=[whole(qkv), pl.BlockSpec(memory_space=pltpu.SMEM)],
        out_shape=shape((qkv.shape[1], 640), LOW),
        name="pack_first",
    )(qkv, exit_layer)


def pack_kernel(places, up, out, down, pool, qv, upb, up_out, down_pool, biases):
    quarter = 2 * places[CORE_AT] + places[0]
    mine = jnp.zeros((pool.shape[0], 192), WIDE)
    for i in range(4):
        mine = jnp.where(quarter == i, pool[:, 192 * i : 192 * (i + 1)], mine)
    up_out[:, 0:D] = up[...].astype(LOW)
    up_out[:, D : D + 256] = jnp.concatenate([out[...].T, mine[:, 0:64]], axis=1).astype(LOW)
    down_pool[:, 0:D] = down[...].astype(LOW)
    down_pool[:, D : D + 128] = mine[:, 64:192].astype(LOW)
    biases[...] = jnp.zeros_like(biases)
    biases[0:1, :] = upb[...].reshape(1, D)
    biases[1:2, 0:192] = qv[0:1, :]
    biases[2:3, 0:192] = qv[1:2, :]


def pack(places, up, out, down, pool, qv, upb):
    share = up.shape[0]
    args = (up, out, down, pool, qv, upb)
    return call(
        pack_kernel,
        "pack",
        (1,),
        [whole(a) for a in args],
        [pl.BlockSpec((share, 1024), lambda *_: (0, 0)), pl.BlockSpec((share, 896), lambda *_: (0, 0))]
        + [pl.BlockSpec((8, D), lambda *_: (0, 0))],
        [shape((share, 1024), LOW), shape((share, 896), LOW), shape((8, D), WIDE)],
        [],
        places,
        args,
        1,
        vmem=60,
    )


def by_side(places, mine, other):
    upper = places[0] == 1
    return jnp.where(upper, other, mine), jnp.where(upper, mine, other)


def project_kernel(places, x, bias, bias_other, h0, h1, h2, h3, q, k, v, w, count, held, pairs):
    @pl.when(pl.program_id(0) == 0)
    def _():
        gather_blocks(places, (h0, h1, h2, h3), held)
        for i in range(3):
            w[i] = to_pairs(held, 128 * i, 512 + 64 * i - 128)
        live = jnp.sum(side_of(held, 0, 576, 64).astype(WIDE), axis=0, keepdims=True)
        count[...] = jnp.broadcast_to(live[:, 0:1], count.shape)
        left, right = by_side(places, bias[...], bias_other[...])
        pairs[...] = jnp.concatenate(
            [left[:, :128], right[:, :128], left[:, 128:192], right[:, 128:192]], axis=1
        )

    left = x[...]
    q[...] = (dot(left, w[0]) + pairs[1:2, :]).astype(LOW)
    k[...] = dot(left, w[1]).astype(LOW)
    v[...] = (dot(left, w[2]) + pairs[2:3, :]).astype(LOW)


def project(places, tokens, bias, bias_other, halves):
    step = 256
    args = (tokens, bias, bias_other, *halves)
    return call(
        project_kernel,
        "project",
        (LEN // step,),
        [pl.BlockSpec((step, D), lambda i, places: (places[0] * (LEN // step) + i, 0))]
        + [whole(a) for a in args[1:]],
        [rows(step, 384)] * 3
        + [pl.BlockSpec((3, D, 384), lambda *_: (0, 0, 0)), pl.BlockSpec((8, 128), lambda *_: (0, 0))],
        [shape((LEN, 384), LOW)] * 3 + [shape((3, D, 384), LOW), shape((8, 128), WIDE)],
        [held_blocks(640), pltpu.VMEM((8, 384), WIDE)],
        places,
        args,
        2 * LEN * D * 1152,
    )


def first_of_pair():
    return lax.broadcasted_iota(jnp.int32, (1, 128), 1) < HD


def attend_kernel(places, q_ref, k_ref, v_ref, o_ref, inv_ref, p_ref, vx):
    first = first_of_pair()
    zero, one = jnp.zeros((), LOW), jnp.ones((), LOW)
    k = k_ref[...]
    v = v_ref[...]
    n = k.shape[0]
    vx[0:n, 0:128] = jnp.where(first, v, zero)
    vx[n : 2 * n, 0:128] = jnp.where(first, zero, v)
    vx[0:n, 128:256] = jnp.broadcast_to(jnp.where(first, one, zero), (n, 128))
    vx[n : 2 * n, 128:256] = jnp.broadcast_to(jnp.where(first, zero, one), (n, 128))
    step = 256
    for i in range(n // step):
        at = pl.ds(i * step, step)
        q = q_ref[at, :]
        result = None
        for head in range(2):
            mine = jnp.where(first, q, zero) if head == 0 else jnp.where(first, zero, q)
            score = dot_nt(mine, k)
            top = jnp.max(score, axis=1, keepdims=True)
            weight = jnp.exp2((score - top) * (HD**-0.5 * LOG2_E)).astype(LOW)
            p_ref[head, at, :] = weight
            part = dot(weight, vx[head * n : (head + 1) * n, :])
            result = part if result is None else result + part
        inv = 1.0 / result[:, 128:256]
        inv_ref[at, :] = inv
        o_ref[at, :] = (result[:, 0:128] * inv).astype(LOW)


def attend(places, q, k, v):
    pair = pl.BlockSpec((LEN, 128), lambda i, *_: (0, i))
    return call(
        attend_kernel,
        "attend_forward",
        (3,),
        [pair] * 3,
        [pair, pair, pl.BlockSpec((2, LEN, LEN), lambda i, *_: (i, 0, 0))],
        [shape((LEN, 384), LOW), shape((LEN, 384), WIDE), shape((6, LEN, LEN), LOW)],
        [pltpu.VMEM((2 * LEN, 256), LOW)],
        places,
        (q, k, v),
        4 * 6 * LEN * LEN * 256,
        vmem=12,
    )


def out_kernel(places, o, h0, h1, h2, h3, z0, z1, w_out, w_up, pool, held):
    @pl.when(pl.program_id(0) == 0)
    def _():
        gather_blocks(places, (h0, h1, h2, h3), held)
        w_out[...] = to_pairs(held, D, D + 128)
        w_up[:, 0:D] = side_of(held, 0, 0, D)
        w_up[:, D : 2 * D] = side_of(held, 1, 0, D)
        pool[...] = jnp.concatenate([side_of(held, i, 960, 64) for i in range(2)], axis=1)

    z = dot_nt(o[...], w_out[...]).astype(LOW)
    for i, out in enumerate((z0, z1)):

        @pl.when(pl.program_id(0) == i)
        def _(out=out):
            out[...] = z


def project_out(places, o, halves):
    step = 512
    return call(
        out_kernel,
        "project_out",
        (LEN // step,),
        [rows(step, 384)] + [whole(a) for a in halves],
        [pl.BlockSpec((step, D), lambda *_: (0, 0))] * 2
        + [pl.BlockSpec((D, 384), lambda *_: (0, 0))]
        + [pl.BlockSpec((D, 2 * D), lambda *_: (0, 0)), pl.BlockSpec((D, 128), lambda *_: (0, 0))],
        [shape((step, D), LOW)] * 2
        + [shape((D, 384), LOW), shape((D, 2 * D), LOW), shape((D, 128), LOW)],
        [held_blocks(1024)],
        places,
        (o, *halves),
        2 * LEN * D * 384,
    )


def normalize(hidden):
    centred = hidden - jnp.mean(hidden, axis=-1, keepdims=True)
    spread = lax.rsqrt(jnp.mean(centred * centred, axis=-1, keepdims=True) + EPS_NORM)
    return centred * spread, spread


def norm_back(grad_normed, normed, spread):
    return spread * (
        grad_normed
        - jnp.mean(grad_normed, axis=-1, keepdims=True)
        - normed * jnp.mean(grad_normed * normed, axis=-1, keepdims=True)
    )


def up_kernel(
    places, x, z0, z1, zp0, zp1, vec, bias_mine, bias_other, w, m, slope, n1, rs1, low, bias
):
    @pl.when(pl.program_id(0) == 0)
    def _():
        left, right = by_side(places, bias_mine[0:1, :], bias_other[0:1, :])
        bias[:, 0:D] = left
        bias[:, D : 2 * D] = right

    early = pl.program_id(0) < 2
    mine = jnp.where(early, z0[...], z1[...]).astype(WIDE)
    other = jnp.where(early, zp0[...], zp1[...]).astype(WIDE)
    total = mine + other
    normed, spread = normalize(x[...].astype(WIDE) + total + vec[4:5, :])
    n1[...] = normed
    rs1[...] = jnp.broadcast_to(spread, rs1.shape)
    middle = (normed * vec[0:1, :] + vec[1:2, :]).astype(LOW)
    low[...] = middle
    for c in range(4):
        at = pl.ds(c * 384, 384)
        u = dot(middle, w[:, at]) + bias[0:1, at]
        half = 0.5 * (1.0 + lax.erf(u * 0.7071067811865476))
        m[:, at] = (u * half).astype(LOW)
        slope[:, at] = (half + u * (jnp.exp(-0.5 * u * u) * 0.3989422804014327)).astype(LOW)


def feed_up(places, tokens, z, zp, vec, bias, bias_other, w_up):
    step = 256
    args = (tokens, *z, *zp, vec, bias, bias_other, w_up)
    return call(
        up_kernel,
        "feed_up",
        (LEN // step,),
        [pl.BlockSpec((step, D), lambda i, places: (places[0] * (LEN // step) + i, 0))]
        + [
            pl.BlockSpec((step, D), lambda i, *_, at=at: (jnp.clip(i - at, 0, 1), 0))
            for at in (0, 2, 0, 2)
        ]
        + [whole(a) for a in args[5:]],
        [rows(step, 2 * D)] * 2
        + [rows(step, D), rows(step, 128), rows(step, D)],
        [shape((LEN, 2 * D), LOW)] * 2
        + [shape((LEN, D), WIDE), shape((LEN, 128), WIDE), shape((LEN, D), LOW)],
        [pltpu.VMEM((1, 2 * D), WIDE)],
        places,
        args,
        2 * LEN * D * 2 * D,
    )


def down_kernel(places, m, pool_part, h0, h1, h2, h3, f, w, pool, held):
    @pl.when(pl.program_id(0) == 0)
    def _():
        gather_blocks(places, (h0, h1, h2, h3), held)
        pieces = []
        for side in range(2):
            w[:, D * side : D * (side + 1)] = side_of(held, side, 0, D)
            pieces += [pool_part[:, 64 * side : 64 * (side + 1)], side_of(held, side, D, 128)]
        pool[...] = jnp.concatenate(pieces, axis=1)

    f[...] = dot_nt(m[...], w[...]).astype(LOW)


def feed_down(places, m, pool_part, halves):
    step = 512
    return call(
        down_kernel,
        "feed_down",
        (LEN // step,),
        [rows(step, 2 * D), whole(pool_part)] + [whole(a) for a in halves],
        [rows(step, D), pl.BlockSpec((D, 2 * D), lambda *_: (0, 0))]
        + [pl.BlockSpec((D, 384), lambda *_: (0, 0))],
        [shape((LEN, D), LOW), shape((D, 2 * D), LOW), shape((D, 384), LOW)],
        [held_blocks(896)],
        places,
        (m, pool_part, *halves),
        2 * LEN * D * 2 * D,
    )


def turn_kernel(
    places, exit_layer, labels, n1, f, fp, cot, vec, pool_a, pool_b, classes, bias, live_count,
    y, half, low, sums, ramp, pool, dy
):
    step = pl.program_id(0)
    middle = n1[...] * vec[0:1, :] + vec[1:2, :]
    total = f[...].astype(WIDE) + fp[...].astype(WIDE)
    normed, spread = normalize(middle + total + vec[5:6, :])
    result = normed * vec[2:3, :] + vec[3:4, :]
    low_result = result.astype(LOW)
    y[...] = low_result

    @pl.when(step // 2 == places[CORE_AT])
    def _():
        half[...] = low_result

    leaves = exit_layer[places[0]]
    grad = cot[...].astype(WIDE) * jnp.where(leaves > LAYER, 1.0, 0.0)
    dy[...] = grad

    @pl.when(step == 0)
    def _():
        sums[...] = jnp.zeros_like(sums)
        own = places[CORE_AT]

        @pl.when(own == 0)
        def _():
            pool[:, 0:384] = pool_a[...]
            pool[:, 384:D] = pool_b[...]

        @pl.when(own == 1)
        def _():
            pool[:, 0:384] = pool_b[...]
            pool[:, 384:D] = pool_a[...]

        count = 16
        head = result[0:count, :].astype(LOW)
        pooled = jnp.tanh(dot(head, pool[...]) + vec[6:7, :])
        pooled_low = pooled.astype(LOW)
        lane = lax.broadcasted_iota(jnp.int32, (count, 128), 1)
        row = lax.broadcasted_iota(jnp.int32, (count, 128), 0)
        valid = lane < 3
        logits = dot(pooled_low, classes[...]) + bias[0:1, :]
        top = jnp.max(jnp.where(valid, logits, -jnp.inf), axis=1, keepdims=True)
        shifted = logits - top
        log_sum = jnp.log(
            jnp.sum(jnp.where(valid, jnp.exp(shifted), 0.0), axis=1, keepdims=True)
        )
        log_probs = jnp.where(valid, shifted - log_sum, 0.0)
        probs = jnp.where(valid, jnp.exp(log_probs), 0.0)
        live = jnp.where(leaves >= LAYER, 1.0, 0.0)
        entropy = -live * jnp.sum(probs * log_probs, axis=1, keepdims=True)
        onehot = jnp.where(lane == labels[places[0]], 1.0, 0.0)
        grad_logits = live * (probs - onehot) / live_count[0:1, 0:1]
        grad_logits = jnp.where(valid & (row == 0), grad_logits, 0.0).astype(LOW)
        grad_pre = (dot_nt(grad_logits, classes[...]) * (1.0 - pooled * pooled)).astype(LOW)
        grad_head = dot_nt(grad_pre, pool[...])
        dy[0:count, :] = dy[0:count, :] + grad_head
        sums[3:4, :] = grad_pre[0:1, :].astype(WIDE)
        of_class = dot_tn(grad_logits, pooled_low)
        sums[4:7, :] = of_class[0:3, :]
        last = jnp.where(lane == 3, entropy, grad_logits.astype(WIDE))
        sums[7:8, 0:128] = last[0:1, :]
        ramp[0:1, :] = head[0:1, :].astype(WIDE)
        ramp[1:2, :] = grad_pre[0:1, :].astype(WIDE)

    grad = dy[...]
    sums[0:1, :] += jnp.sum(grad * normed, axis=0, keepdims=True)
    sums[1:2, :] += jnp.sum(grad, axis=0, keepdims=True)
    back = norm_back(grad * vec[2:3, :], normed, spread)
    sums[2:3, :] += jnp.sum(back, axis=0, keepdims=True)
    low[...] = back.astype(LOW)


def own_rows(step):
    return pl.BlockSpec((step, D), lambda i, places: (places[0] * (LEN // step) + i, 0))


def half_rows(step, sibling=False):
    count = LEN // step // 2

    def at(i, places):
        core = 1 - places[CORE_AT] if sibling else places[CORE_AT]
        return jnp.clip(i - count * core, 0, count - 1), 0

    return pl.BlockSpec((step, D), at)


def turn(places, exit_layer, labels, n1, f, fp, cotangent, vec, pool_a, pool_b, classes, bias, live_count):
    step = 256
    args = (exit_layer, labels, n1, f, fp, cotangent, vec, pool_a, pool_b, classes, bias, live_count)
    return call(
        turn_kernel,
        "turn",
        (LEN // step,),
        [pl.BlockSpec(memory_space=pltpu.SMEM)] * 2
        + [rows(step, D)] * 3
        + [own_rows(step)]
        + [whole(a) for a in args[6:]],
        [own_rows(step), half_rows(step)]
        + [rows(step, D)]
        + [pl.BlockSpec((8, D), lambda *_: (0, 0))] * 2,
        [shape((2 * LEN, D), LOW), shape((LEN // 2, D), LOW), shape((LEN, D), LOW)]
        + [shape((8, D), WIDE)] * 2,
        [pltpu.VMEM((D, D), LOW), pltpu.VMEM((step, D), WIDE)],
        places,
        args,
        LEN * D * 60,
    )


def feed_back_kernel(places, dh2, slope, w_down, w_up, du, dx, sums):
    grad = dot(dh2[...], w_down[...]) * slope[...].astype(WIDE)
    grad = grad.astype(LOW)
    du[...] = grad
    dx[...] = dot_nt(grad, w_up[...]).astype(LOW)

    @pl.when(pl.program_id(0) == 0)
    def _():
        sums[...] = jnp.zeros_like(sums)

    sums[0:1, :] += jnp.sum(grad.astype(WIDE), axis=0, keepdims=True)


def feed_back(places, dh2, slope, w_down, w_up):
    step = 512
    args = (dh2, slope, w_down, w_up)
    return call(
        feed_back_kernel,
        "feed_back",
        (LEN // step,),
        [rows(step, D), rows(step, 2 * D), whole(w_down), whole(w_up)],
        [rows(step, 2 * D), rows(step, D), pl.BlockSpec((8, 2 * D), lambda *_: (0, 0))],
        [shape((LEN, 2 * D), LOW), shape((LEN, D), LOW), shape((8, 2 * D), WIDE)],
        [],
        places,
        args,
        4 * LEN * D * 2 * D,
        vmem=14,
    )


def feed_grad_kernel(places, dh2, m, middle, du, ramp, h0, h1, h2, h3, held, turned):
    for at, left, right in ((0, dh2, m), (D, middle, du)):
        turned[...] = left[...].T
        for side in range(2):
            for c in range(0, D, 256):
                part = dot(turned[...], right[:, D * side + c : D * side + c + 256]).astype(LOW)
                held[side * BLOCKS : (side + 1) * BLOCKS, :, at + c : at + c + 256] = part.reshape(
                    BLOCKS, BLOCK_ROWS, 256
                )
    row = lax.broadcasted_iota(jnp.int32, (BLOCK_ROWS, 256), 0)
    for group in range((held.shape[2] - 2 * D) // 256):
        slot = places[SLOT_AT] - 16 * group
        block = jnp.zeros((BLOCK_ROWS, 256), WIDE)
        for i in range(6):
            values = ramp[i // 3 : i // 3 + 1, 256 * (i % 3) : 256 * (i % 3 + 1)]
            mine = (row == 6 * slot + i) & (slot >= 0) & (slot < 16)
            block = jnp.where(mine, values, block)
        block = block.astype(LOW)
        at = 2 * D + 256 * group
        for p in range(2 * BLOCKS):
            held[p, :, at : at + 256] = block
    scatter_blocks(places, held, (h0, h1, h2, h3), ALONG)


def feed_grad(places, slots, dh2, m, middle, du, ramp):
    args = (dh2, m, middle, du, ramp)
    width = 2 * D + 16 * slots
    return call(
        feed_grad_kernel,
        "feed_grad",
        (1,),
        [whole(a) for a in args],
        half_specs(width),
        half_shapes(width),
        [held_blocks(width), pltpu.VMEM((D, LEN), LOW)],
        places,
        args,
        4 * LEN * D * 2 * D,
        vmem=12 if slots == 16 else 56,
    )


def mid_kernel(places, dh2, dx, dxp, n1, rs1, vec, w_out, turn_sums, up_sums, dh1, low, do, sums):
    @pl.when(pl.program_id(0) == 0)
    def _():
        sums[...] = jnp.zeros_like(sums)
        sums[0:8, :] = turn_sums[...]
        sums[11:12, :] = up_sums[0:1, 0:D]
        sums[12:13, :] = up_sums[0:1, D : 2 * D]

    total = dx[...].astype(WIDE) + dxp[...].astype(WIDE)
    grad = dh2[...].astype(WIDE) + total
    normed = n1[...]
    sums[8:9, :] += jnp.sum(grad * normed, axis=0, keepdims=True)
    sums[9:10, :] += jnp.sum(grad, axis=0, keepdims=True)
    back = norm_back(grad * vec[0:1, :], normed, rs1[:, 0:1])
    sums[10:11, :] += jnp.sum(back, axis=0, keepdims=True)
    dh1[...] = back
    back_low = back.astype(LOW)
    low[...] = back_low
    do[...] = dot(back_low, w_out[...]).astype(LOW)


def mid(places, dh2, dx, dxp, n1, rs1, vec, w_out, turn_sums, up_sums):
    step = 256
    args = (dh2, dx, dxp, n1, rs1, vec, w_out, turn_sums, up_sums)
    count = 16
    return call(
        mid_kernel,
        "middle_back",
        (LEN // step,),
        [rows(step, D)] * 4 + [rows(step, 128)] + [whole(a) for a in args[5:]],
        [rows(step, D)] * 2 + [rows(step, 384), pl.BlockSpec((count, D), lambda *_: (0, 0))],
        [shape((LEN, D), WIDE), shape((LEN, D), LOW), shape((LEN, 384), LOW), shape((count, D), WIDE)],
        [],
        places,
        args,
        2 * LEN * D * 384,
    )


def attend_back_kernel(
    places, q_ref, k_ref, v_ref, do_ref, inv_ref, p_ref, dq_ref, dk_ref, dv_ref, ds_ref, held
):
    first = first_of_pair()
    zero = jnp.zeros((), LOW)
    n = k_ref.shape[0]
    k = k_ref[...]
    v = v_ref[...]
    k_own = [jnp.where(first, k, zero), jnp.where(first, zero, k)]
    scaled = (do_ref[...].astype(WIDE) * inv_ref[...]).astype(LOW)
    held[...] = scaled
    step = 512
    for i in range(n // step):
        at = pl.ds(i * step, step)
        d = held[at, :]
        total = None
        for head in range(2):
            mine = jnp.where(first, d, zero) if head == 0 else jnp.where(first, zero, d)
            grad_weight = dot_nt(mine, v)
            weight = p_ref[head, at, :].astype(WIDE)
            product = weight * grad_weight
            inner = jnp.sum(product, axis=1, keepdims=True)
            inner = inner * inv_ref[at, pl.ds(HD * head, 1)]
            grad_score = (product - weight * inner).astype(LOW)
            ds_ref[head, at, :] = grad_score
            part = dot(grad_score, k_own[head])
            total = part if total is None else total + part
        dq_ref[at, :] = (total * HD**-0.5).astype(LOW)
    scaled_t = scaled.T
    q_t = q_ref[...].T
    grad_v = jnp.concatenate(
        [dot(scaled_t[0:HD], p_ref[0]), dot(scaled_t[HD : 2 * HD], p_ref[1])], axis=0
    )
    dv_ref[...] = grad_v.T.astype(LOW)
    grad_k = jnp.concatenate(
        [dot(q_t[0:HD], ds_ref[0]), dot(q_t[HD : 2 * HD], ds_ref[1])], axis=0
    )
    dk_ref[...] = (grad_k * HD**-0.5).T.astype(LOW)


def attend_back(places, q, k, v, do, inv, p):
    at = pl.BlockSpec((LEN, 128), lambda i, *_: (0, i))
    return call(
        attend_back_kernel,
        "attend_backward",
        (3,),
        [at] * 5 + [pl.BlockSpec((2, LEN, LEN), lambda i, *_: (i, 0, 0))],
        [at] * 3,
        [shape((LEN, 384), LOW)] * 3,
        [pltpu.VMEM((2, LEN, LEN), LOW), pltpu.VMEM((LEN, 128), LOW)],
        places,
        (q, k, v, do, inv, p),
        8 * 6 * LEN * LEN * 256,
        vmem=19,
    )


MARK_ROWS = 6


def narrow_grad_kernel(places, left, dh1, o, dq, dk, dv, sums, h0, h1, h2, h3, held, turned, marks):
    turned[...] = left[...].T
    marks[...] = jnp.zeros_like(marks)
    for i, right in enumerate((dq, dk, dv)):
        value = right[...]
        from_pairs(dot(turned[...], value).astype(LOW), held, 128 * i, 512 + 64 * i)
        if i != 1:
            total = jnp.sum(value.astype(WIDE), axis=0, keepdims=True)
            for k in range(3):
                at = 13 * MARK_ROWS + 3 * (i // 2) + k
                marks[at : at + 1, :] = total[:, 128 * k : 128 * (k + 1)]
    turned[...] = dh1[...].T
    from_pairs(dot(turned[...], o[...]).astype(LOW), held, 384, 704)
    for i in range(13):
        for k in range(MARK_ROWS):
            at = i * MARK_ROWS + k
            marks[at : at + 1, :] = sums[i : i + 1, 128 * k : 128 * (k + 1)]
    block = marks[...].astype(LOW)
    for p in range(2 * BLOCKS):
        held[p, :, D : D + 128] = block
    scatter_blocks(places, held, (h0, h1, h2, h3), BESIDE)


def narrow_grad(places, tokens, dh1, o, grads, sums):
    args = (tokens, dh1, o, *grads, sums)
    width = D + 128
    return call(
        narrow_grad_kernel,
        "narrow_grad",
        (1,),
        [own_rows(LEN)] + [whole(a) for a in args[1:]],
        half_specs(width),
        half_shapes(width),
        [held_blocks(width), pltpu.VMEM((D, LEN), LOW), pltpu.VMEM((BLOCK_ROWS, 128), WIDE)],
        places,
        args,
        2 * LEN * D * 1536,
        vmem=12,
    )


def input_kernel(places, *refs):
    grads, w, (keep, send) = refs[:3], refs[3], refs[4:]
    total = None
    for i in range(3):
        part = dot_nt(grads[i][...], w[i])
        total = part if total is None else total + part
    total = total.astype(LOW)
    mine = pl.program_id(0) == places[CORE_AT]

    @pl.when(mine)
    def _():
        keep[...] = total

    @pl.when(jnp.logical_not(mine))
    def _():
        send[...] = total


def input_grad(places, grads, w):
    step = 512
    return call(
        input_kernel,
        "input_grad",
        (LEN // step,),
        [rows(step, 384)] * 3 + [whole(w)],
        [half_rows(step), half_rows(step, True)],
        [shape((LEN // 2, D), LOW)] * 2,
        [],
        places,
        (*grads, w),
        2 * LEN * D * 1152,
    )


def finish_kernel(places, dh1, keep, other, half):
    total = keep[...].astype(WIDE) + other[...].astype(WIDE)
    half[...] = (dh1[...] + total).astype(LOW)


def finish(places, dh1, keep, other):
    step = 128
    count = LEN // 2 // step
    return call(
        finish_kernel,
        "finish",
        (count,),
        [pl.BlockSpec((step, D), lambda i, places: (count * places[CORE_AT] + i, 0))]
        + [rows(step, D)] * 2,
        [rows(step, D)],
        [shape((LEN // 2, D), LOW)],
        [],
        places,
        (dh1, keep, other),
        LEN * D * 3,
    )[0]


def place_kernel(count, places, *refs):
    half = LEN // 2
    ins, out, sems = refs[-2 - count : -2], refs[-2], refs[-1]
    side, core = places[0], places[CORE_AT]
    at = [(1 - side, core), (1 - side, 1 - core), (side, core), (side, 1 - core)]
    copies = []
    for i, ref in enumerate(ins):
        first = pl.multiple_of((2 * at[i][0] + at[i][1]) * half, half)
        copies.append(pltpu.make_async_copy(ref, out.at[pl.ds(first, half)], sems.at[i]))
        copies[-1].start()
    for copy in copies:
        copy.wait()


def place(places, kept, quarters):
    first = [] if kept is None else [kept]
    return call(
        functools.partial(place_kernel, len(quarters)),
        "place",
        (1,),
        [pl.BlockSpec(memory_space=pl.ANY)] * len(first) + [whole(a) for a in quarters],
        [pl.BlockSpec(memory_space=pl.ANY)],
        [shape((2 * LEN, D), LOW)],
        [pltpu.SemaphoreType.DMA((len(quarters),))],
        places,
        (*first, *quarters),
        1,
        vmem=12,
        aliases={} if kept is None else {1: 0},
    )[0]


def update(places, name, pieces, width, ins, kernel, outs, scratch):
    counts = tuple(len(group) for group in pieces)
    args = [a for group in pieces for a in group]
    specs = [
        pl.BlockSpec((1, a.shape[1], width), lambda *_: (0, 0, 0)) if a.ndim == 3 else whole(a)
        for a in args
    ]
    return call(
        functools.partial(kernel, counts),
        name,
        (1,),
        specs + [whole(a) for a in ins],
        [whole(o) for o in outs],
        outs,
        scratch,
        places,
        (*args, *ins),
        1,
        vmem=60,
    )


def matrix_outs(weight):
    return [shape(weight.shape, WIDE)] * 3 + [shape(weight.shape, LOW)]


def step_matrix(ins, outs, at, grad, rate):
    new, first, second = adamw(ins[0][at], ins[1][at], ins[2][at], grad, rate, DECAY)
    outs[0][at] = new
    outs[1][at] = first
    outs[2][at] = second
    outs[3][at] = new.astype(LOW)


def step_vector(ins, outs, at, grad, rate=VECTOR_RATE, decay=0.0):
    results = adamw(ins[0][at], ins[1][at], ins[2][at], grad, rate, decay)
    for out, result in zip(outs, results, strict=True):
        out[at] = result


def update_feed_kernel(counts, places, *refs):
    total = sum(counts)
    grad, marks = sum_pieces(refs[:total], counts, 2 * D)
    ins, outs = refs[total : total + 9], refs[total + 9 : total + 21]
    heads, slopes = refs[total + 21 :]
    step_matrix(ins[0:3], outs[0:4], ..., grad[:, 0:D], RATE * FF ** (-0.5))
    step_matrix(ins[3:6], outs[4:8], ..., grad[:, D : 2 * D], RATE * D ** (-0.5))
    for s in range(heads.shape[0]):
        at = 256 * (s // 16)
        for i, target in enumerate((heads, slopes)):
            for k in range(3):
                row = 6 * (s % 16) + 3 * i + k
                target[s : s + 1, 256 * k : 256 * (k + 1)] = marks[row : row + 1, at : at + 256]
    share = ins[6].shape[0]
    column = lax.broadcasted_iota(jnp.int32, (D, share), 0)
    own = column == lax.broadcasted_iota(jnp.int32, (D, share), 1) + places[DP_AT] * share
    picked = dot(heads[...].astype(LOW), jnp.where(own, 1.0, 0.0).astype(LOW)).astype(LOW)
    pool = dot_tn(picked, slopes[...].astype(LOW))
    step_matrix(ins[6:9], outs[8:12], ..., pool, RATE * D ** (-0.5))


def update_narrow_kernel(counts, places, *refs):
    total = sum(counts)
    grad, marks = sum_pieces(refs[:total], counts, D)
    ins, outs = refs[total : total + 19], refs[total + 19 : total + 40]
    rows_of = refs[total + 40]

    def columns(i):
        return jnp.concatenate(
            [grad[:, 128 * i : 128 * (i + 1)], grad[:, 512 + 64 * i : 576 + 64 * i]], axis=1
        )

    for i in range(3):
        step_matrix(ins[0:3], outs[0:4], i, columns(i), RATE * D ** (-0.5))
    step_matrix(ins[3:6], outs[4:8], ..., columns(3).T, RATE * max(1, 2 * D // LEN) ** (-0.5))
    for i in range(14):
        for k in range(MARK_ROWS):
            at = i * MARK_ROWS + k
            rows_of[i : i + 1, 128 * k : 128 * (k + 1)] = marks[at : at + 1, :]
    side = places[0]
    pairs = rows_of[13:14, :]
    for i in range(2):
        pair = pairs[:, 384 * i : 384 * (i + 1)]
        wide = jnp.where(side == 0, pair[:, 0:128], pair[:, 128:256])
        narrow = jnp.where(side == 0, pair[:, 256:320], pair[:, 320:384])
        own = jnp.concatenate([wide, narrow], axis=1)
        step_vector(ins[6:9], outs[8:11], pl.ds(i, 1), own)
    hidden = jnp.where(side == 0, rows_of[11:12, :], rows_of[12:13, :])
    step_vector(ins[9:12], outs[11:14], ..., hidden.reshape(D))
    for i, at in enumerate((8, 9, 0, 1, 10, 2, 3)):
        step_vector(ins[12:15], outs[14:17], pl.ds(i, 1), rows_of[at : at + 1, :])
    for i in range(3):
        one = jnp.concatenate([rows_of[4 + i : 5 + i, :], rows_of[7:8, i : i + 1]], axis=1)
        step_vector(
            ins[15:18], outs[17:20], pl.ds(i, 1), one, RATE * (D // 4) ** (-0.5), DECAY
        )
    outs[20][...] = rows_of[7:8, 3:4] / ins[18][0:1, 0:1]


def per_device(
    dp_count,
    mp_count,
    tokens,
    cotangent,
    exit_layer,
    labels,
    qkv_weight,
    qkv_first,
    qkv_second,
    out_weight,
    out_first,
    out_second,
    up_weight,
    up_first,
    up_second,
    down_weight,
    down_first,
    down_second,
    pool_weight,
    pool_first,
    pool_second,
    qv_bias,
    qv_first,
    qv_second,
    up_bias,
    upb_first,
    upb_second,
    layer_vectors,
    vector_first,
    vector_second,
    class_weight,
    class_first,
    class_second,
):
    links = Links(dp_count, mp_count)
    side, core = links.side, links.core

    slot = 2 * links.dp + side
    places = jnp.concatenate(
        [side[None], links.places(), core[None], slot[None], links.dp[None]]
    ).astype(jnp.int32)
    share = D // dp_count

    by_kind = [a.transpose(1, 0, 2) for a in (qkv_weight, qkv_first, qkv_second)]
    down_turned = [a.T for a in (down_weight, down_first, down_second)]
    qkv_spread = links.spread(pack_first(by_kind[0], exit_layer))
    sent = qkv_spread.step()
    up_out, down_pool, biases = pack(
        places,
        after(up_weight, *sent),
        out_weight,
        down_turned[0],
        pool_weight,
        qv_bias,
        up_bias,
    )
    other_biases = links.swap(biases, SIDE)
    qkv_z = tuple(qkv_spread.last)
    sent = qkv_spread.step(up_out, other_biases)
    up_out_spread = links.spread(up_out)
    up_out_spread.step(*qkv_z)
    class_low = after(class_weight, *sent)
    classes = jnp.pad(class_low[:D].astype(LOW), ((0, 0), (0, 125)))
    class_bias = jnp.pad(class_low[D:], ((0, 0), (0, 125)))
    sent = qkv_spread.step(classes, class_bias)
    sent = up_out_spread.step(*sent)
    down_spread = links.spread(down_pool)
    sent = down_spread.step(*sent)

    biases = after(biases, *sent)
    q, k, v, w_qkv, live_count = project(places, tokens, biases, other_biases, qkv_spread.halves())
    sent = up_out_spread.step(q)
    q = after(q, *sent)
    o, inv, p = attend(places, q, k, v)
    sent = down_spread.step(o)
    o = after(o, *sent)
    *z, w_out, w_up, pool_part = project_out(places, o, up_out_spread.halves())
    zp = [links.swap(part, CORE) for part in z]
    sent = down_spread.step(w_up)
    z = after(z, *sent)
    m, slope, n1, rs1, middle_low = feed_up(
        places, tokens, z, zp, layer_vectors, biases, other_biases, w_up
    )
    f, w_down, pool_mine = feed_down(places, m, pool_part, down_spread.halves())
    fp = links.swap(f, CORE)
    pool_other = links.swap(pool_mine, CORE)
    y, y_half, dh2_low, turn_sums, ramp = turn(
        places, exit_layer, labels, n1, f, fp, cotangent, layer_vectors, pool_mine, pool_other,
        classes, class_bias, live_count,
    )

    y_first = links.swap(y_half, SIDE)
    du, dx, up_sums = feed_back(places, dh2_low, slope, w_down, w_up)
    dxp = links.swap(dx, CORE)
    m, dh2_low = after((m, dh2_low), dx)
    slots = 2 * dp_count
    feed_halves = feed_grad(places, slots, dh2_low, m, middle_low, du, ramp)
    feed_fold = links.fold(feed_halves, ALONG, 2 * D)
    feed_fold.step()
    dx = after(dx, *feed_halves)
    dh1, dh1_low, do, sums = mid(
        places, dh2_low, dx, dxp, n1, rs1, layer_vectors, w_out, turn_sums, up_sums
    )
    grads = attend_back(places, q, k, v, do, inv, p)
    token_keep, token_send = input_grad(places, grads, w_qkv)
    token_other = links.swap(token_send, CORE)
    sent = feed_fold.step(token_keep, y_first)
    grads = after(grads, *sent)
    narrow_halves = narrow_grad(places, tokens, dh1_low, o, grads, sums)
    narrow_fold = links.fold(narrow_halves, BESIDE, D)
    narrow_fold.step()
    token_keep = after(token_keep, *narrow_halves)
    grad_half = finish(places, dh1, token_keep, token_other)
    first = links.swap(grad_half, SIDE)
    second_own = links.swap(grad_half, CORE)
    sent = feed_fold.step(grad_half)
    sent = narrow_fold.step(*sent)
    sent = feed_fold.step(*sent)
    sent = narrow_fold.step(*sent)
    first, y_first = after((first, y_first), *sent)
    second, y_second = links.swap(first, CORE), links.swap(y_first, CORE)
    tokens_grad = place(places, None, [first, second, grad_half, second_own])
    result = place(places, y, [y_first, after(y_second, tokens_grad)])
    sent = narrow_fold.step(result)
    masters = [*down_turned, up_weight, up_first, up_second, pool_weight, pool_first, pool_second]
    feed_new = update(
        places,
        "update_feed",
        after(feed_fold.pieces(), *sent),
        2 * D + 16 * slots,
        masters,
        update_feed_kernel,
        [o for a in masters[0::3] for o in matrix_outs(a)],
        [pltpu.VMEM((slots, D), WIDE)] * 2,
    )
    down_new, down_first_new, down_second_new, down_copy = (a.T for a in feed_new[0:4])
    up_new, up_first_new, up_second_new, up_copy = feed_new[4:8]
    pool_new, pool_first_new, pool_second_new, pool_copy = feed_new[8:12]
    by_class = [a.T for a in (class_weight, class_first, class_second)]
    masters = [*by_kind, out_weight, out_first, out_second]
    vectors = [qv_bias, qv_first, qv_second, up_bias, upb_first, upb_second]
    vectors += [layer_vectors, vector_first, vector_second, *by_class]
    narrow_new = update(
        places,
        "update_narrow",
        after(narrow_fold.pieces(), feed_new[0]),
        D + 128,
        [*masters, *vectors, live_count],
        update_narrow_kernel,
        [o for a in masters[0::3] for o in matrix_outs(a)]
        + [shape(a.shape, WIDE) for a in vectors]
        + [shape((1, 1), WIDE)],
        [pltpu.VMEM((16, D), WIDE)],
    )
    qkv_new, qkv_first_new, qkv_second_new, qkv_copy = (
        a.transpose(1, 0, 2) for a in narrow_new[0:4]
    )
    out_new, out_first_new, out_second_new, out_copy = narrow_new[4:8]
    qv_new, qv_first_new, qv_second_new = narrow_new[8:11]
    upb_new, upb_first_new, upb_second_new = narrow_new[11:14]
    vector_new, vector_first_new, vector_second_new = narrow_new[14:17]
    class_new, class_first_new, class_second_new = (a.T for a in narrow_new[17:20])
    entropy = narrow_new[20].reshape(())
    return (
        result,
        tokens_grad,
        entropy,
        qkv_new,
        qkv_first_new,
        qkv_second_new,
        qkv_copy,
        out_new,
        out_first_new,
        out_second_new,
        out_copy,
        up_new,
        up_first_new,
        up_second_new,
        up_copy,
        down_new,
        down_first_new,
        down_second_new,
        down_copy,
        pool_new,
        pool_first_new,
        pool_second_new,
        pool_copy,
        qv_new,
        qv_first_new,
        qv_second_new,
        upb_new,
        upb_first_new,
        upb_second_new,
        vector_new,
        vector_first_new,
        vector_second_new,
        class_new,
        class_first_new,
        class_second_new,
    )


def solution(mesh):
    in_specs = (
        P("dp", None),
        P("dp", None),
        P("dp"),
        P("dp"),
        P("dp", None, "mp"),
        P("dp", None, "mp"),
        P("dp", None, "mp"),
        P("mp", "dp"),
        P("mp", "dp"),
        P("mp", "dp"),
        P("dp", "mp"),
        P("dp", "mp"),
        P("dp", "mp"),
        P("mp", "dp"),
        P("mp", "dp"),
        P("mp", "dp"),
        P("dp", None),
        P("dp", None),
        P("dp", None),
        P(None, "mp"),
        P(None, "mp"),
        P(None, "mp"),
        P("mp"),
        P("mp"),
        P("mp"),
        P(),
        P(),
        P(),
        P(),
        P(),
        P(),
    )
    out_specs = (
        P("dp", None),
        P("dp", None),
        P(),
        P("dp", None, "mp"),
        P("dp", None, "mp"),
        P("dp", None, "mp"),
        P("dp", None, "mp"),
        P("mp", "dp"),
        P("mp", "dp"),
        P("mp", "dp"),
        P("mp", "dp"),
        P("dp", "mp"),
        P("dp", "mp"),
        P("dp", "mp"),
        P("dp", "mp"),
        P("mp", "dp"),
        P("mp", "dp"),
        P("mp", "dp"),
        P("mp", "dp"),
        P("dp", None),
        P("dp", None),
        P("dp", None),
        P("dp", None),
        P(None, "mp"),
        P(None, "mp"),
        P(None, "mp"),
        P("mp"),
        P("mp"),
        P("mp"),
        P(),
        P(),
        P(),
        P(),
        P(),
        P(),
    )
    one_device = functools.partial(per_device, mesh.shape["dp"], mesh.shape["mp"])
    return jax.shard_map(
        one_device, mesh=mesh, in_specs=in_specs, out_specs=out_specs, check_vma=False
    )
```

```python
import functools

import jax
import jax.numpy as jnp
import numpy as np
from jax import lax
from jax.experimental import pallas as pl
from jax.experimental.pallas import tpu as pltpu
from jax.sharding import PartitionSpec as P

D = 768
HD = 64
FF = 3072
LAYER = 6
STEP = 10
LEN = 1024


EPS_NORM = 1e-06
BETA_ONE = 0.9
BETA_TWO = 0.98
EPS_ADAM = 1e-08
DECAY = 0.01
RATE = 0.8
VECTOR_RATE = 0.3

LOW = jnp.bfloat16
WIDE = jnp.float32
LOG2_E = 1.4426950408889634
MIB = 2**20
COST_SCALE = 16

CORE, SIDE, X_BIT, Z_LOW, Z_HIGH = 1, 2, 4, 8, 16
BLOCKS = 8
BLOCK_ROWS = D // BLOCKS
PART_ROWS = BLOCK_ROWS // 2
ACROSS = ((Z_HIGH, Z_LOW, X_BIT, SIDE), (Z_HIGH, Z_LOW, SIDE, X_BIT))
ALONG = ((Z_HIGH, Z_LOW, SIDE, X_BIT), (SIDE, Z_HIGH, X_BIT, Z_LOW))
Z_LINE = (Z_HIGH, Z_LOW, Z_HIGH | Z_LOW)
BESIDE = ((Z_HIGH, Z_LOW, SIDE, X_BIT), (Z_HIGH, SIDE, X_BIT, Z_LOW))
ROUTES = (ACROSS, ALONG, BESIDE)


def dot(left, right):
    return lax.dot_general(
        left, right, (((1,), (0,)), ((), ())), preferred_element_type=WIDE
    )


def dot_nt(left, right):
    return lax.dot_general(
        left, right, (((1,), (1,)), ((), ())), preferred_element_type=WIDE
    )


def dot_tn(left, right):
    return lax.dot_general(
        left, right, (((0,), (0,)), ((), ())), preferred_element_type=WIDE
    )


def adamw(weight, first, second, grad, rate, decay):
    first_new = BETA_ONE * first + (1.0 - BETA_ONE) * grad
    second_new = BETA_TWO * second + (1.0 - BETA_TWO) * grad * grad
    first_hat = first_new / (1.0 - BETA_ONE**STEP)
    second_hat = second_new / (1.0 - BETA_TWO**STEP)
    weight_new = weight - rate * (first_hat / (jnp.sqrt(second_hat) + EPS_ADAM) + decay * weight)
    return (weight_new, first_new, second_new)


class Links:
    def __init__(self, dp_count, mp_count):
        self.dp_count = dp_count
        self.total = dp_count * mp_count
        self.cube = dp_count == BLOCKS
        self.dp = lax.axis_index("dp").astype(jnp.int32)
        mp = lax.axis_index("mp").astype(jnp.int32)
        self.side = mp // 2
        self.core = mp % 2

    def swap(self, value, bit):
        pairs = [(i, i ^ bit) for i in range(self.total)]
        return lax.ppermute(value, ("dp", "mp"), pairs)

    def places(self):
        flips = []
        for order in sum(ROUTES, ()):
            for j in range(2 * BLOCKS):
                if self.cube:
                    bits = 0
                    for k, bit in enumerate(order):
                        bits ^= bit if (j >> k) & 1 else 0
                    flips.append((bits // SIDE & 1, bits // X_BIT))
                else:
                    flips.append((j // BLOCKS, j % BLOCKS))
        flips = np.array(flips, np.int32)
        mine = self.dp if self.cube else 0
        return (self.side ^ flips[:, 0]) * BLOCKS + (mine ^ flips[:, 1])

    def spread(self, share):
        return (Spread if self.cube else WholeSpread)(self, share)

    def fold(self, halves, route, base):
        return (Fold if self.cube else WholeFold)(self, halves, route, base)


class Spread:
    def __init__(self, links, share):
        self.links = links
        self.held = [share[None]]
        self.last = None
        self.round = 0

    def step(self, *others):
        links = self.links
        if others:
            (self.held, self.last), *_ = lax.optimization_barrier(((self.held, self.last), *others))
        if self.round == 0:
            self.last = [links.swap(self.held[0], bits) for bits in Z_LINE]
        elif self.round == 1:
            line = [self.held[0], *self.last]
            at = (slice(0, PART_ROWS), slice(PART_ROWS, BLOCK_ROWS))
            self.held = [jnp.concatenate([a[:, i] for a in line], axis=0) for i in at]
        else:
            self.held = [
                jnp.concatenate([mine, other], axis=0)
                for mine, other in zip(self.held, self.last, strict=True)
            ]
        if self.round:
            self.last = [
                links.swap(part, ACROSS[i][self.round + 1]) for i, part in enumerate(self.held)
            ]
        self.round += 1
        return tuple(self.held)

    def halves(self):
        return (self.held[0], self.last[0], self.held[1], self.last[1])


class WholeSpread:
    def __init__(self, links, share):
        self.last = ()
        near = lax.all_gather(share, "dp", axis=0, tiled=True)
        near = near.reshape(BLOCKS, BLOCK_ROWS, share.shape[1])
        far = links.swap(near, SIDE)
        self.parts = (
            near[:, :PART_ROWS],
            far[:, :PART_ROWS],
            near[:, PART_ROWS:],
            far[:, PART_ROWS:],
        )

    def step(self, *others):
        return ()

    def halves(self):
        return self.parts


class Fold:
    def __init__(self, links, halves, route, base):
        self.links = links
        self.route = route
        self.base = base
        self.parts = [[halves[0]], [halves[2]]]
        self.far = [halves[1], halves[3]]
        self.joined = []
        self.round = 0

    def step(self, *others, vmem=16):
        links, k = self.links, 3 - self.round
        if others:
            (self.parts, self.joined, self.far), *_ = lax.optimization_barrier(
                ((self.parts, self.joined, self.far), *others)
            )
        if self.route is ACROSS and self.round == 2:
            sent = fold_add(self.parts, 2, False, self.base, vmem)
            self.joined = [links.swap(a, bits) for a, bits in zip(sent, Z_LINE, strict=True)]
        else:
            if self.round == 0:
                sent = self.far
            else:
                sent = fold_add(self.parts, 2**k, True, self.base, vmem)
            for i, order in enumerate(self.route):
                self.parts[i].append(links.swap(sent[i], order[k]))
        self.round += 1
        return tuple(sent)

    def pieces(self):
        return (self.parts[0], self.parts[1], self.joined)


class WholeFold:
    def __init__(self, links, halves, route, base):
        near, far = (
            jnp.concatenate([halves[i], halves[i + 2]], axis=1).reshape(D, -1) for i in range(2)
        )
        total = near.astype(WIDE) + links.swap(far, SIDE).astype(WIDE)
        share = lax.psum_scatter(total[:, :base], "dp", scatter_dimension=0, tiled=True)
        self.parts = [share, lax.psum(total[:BLOCK_ROWS, base:], "dp")]

    def step(self, *others, vmem=16):
        return ()

    def pieces(self):
        return ([], [], self.parts)


def add_marked(refs, at, base):
    total = sum(ref[at, :, 0:base].astype(WIDE) for ref in refs)
    marks = refs[0][at, :, base:].astype(WIDE)
    for ref in refs[1:]:
        marks = marks.astype(LOW).astype(WIDE) + ref[at, :, base:].astype(WIDE)
    return total, marks


def sum_pieces(refs, counts, base, at=0):
    first, second, joined = counts
    if not first:
        return refs[0][...], refs[1][...]
    tops = add_marked(refs[:first], at, base)
    ends = add_marked(refs[first : first + second], at, base)
    total, marks = (jnp.concatenate(pair, axis=0) for pair in zip(tops, ends, strict=True))
    joints = refs[first + second :]
    for ref in joints:
        total = total + ref[at, :, 0:base].astype(WIDE)
    if joints:
        high, low, both = (ref[at, :, base:].astype(WIDE) for ref in joints)
        marks = (marks.astype(LOW).astype(WIDE) + high) + (low + both)
    return total, marks


def fold_add_kernel(count, half, apart, base, *refs):
    ins, outs = refs[: 2 * count], refs[2 * count :]
    if apart:
        for i in range(half):
            for j in range(2):
                total, marks = add_marked(ins[j * count : (j + 1) * count], i, base)
                outs[j][i, :, 0:base] = total.astype(LOW)
                outs[j][i, :, base:] = marks.astype(LOW)
    else:
        for i, out in enumerate(outs):
            total, marks = sum_pieces(ins, (count, count, 0), base, i + 1)
            out[0, :, 0:base] = total.astype(LOW)
            out[0, :, base:] = marks.astype(LOW)


def fold_add(parts, half, apart, base, vmem):
    args = [*parts[0], *parts[1]]
    width = args[0].shape[2]
    if apart:
        outs = [shape((half, PART_ROWS, width), LOW)] * 2
        specs = [pl.BlockSpec((half, PART_ROWS, width), lambda i: (1, 0, 0))] * len(args)
    else:
        outs = [shape((1, BLOCK_ROWS, width), LOW)] * 3
        specs = [pl.BlockSpec((4, PART_ROWS, width), lambda i: (0, 0, 0))] * len(args)
    return pl.pallas_call(
        functools.partial(fold_add_kernel, len(parts[0]), half, apart, base),
        grid=(1,),
        in_specs=specs,
        out_specs=[pl.BlockSpec(o.shape, lambda i: (0, 0, 0)) for o in outs],
        out_shape=outs,
        compiler_params=pltpu.CompilerParams(vmem_limit_bytes=vmem * MIB),
        cost_estimate=pl.CostEstimate(
            flops=half * BLOCK_ROWS * width, bytes_accessed=half * width, transcendentals=0
        ),
        name="fold_add",
    )(*args)


def after(value, *others):
    return lax.optimization_barrier((value, *others))[0]


def call(kernel, name, grid, in_specs, out_specs, out_shape, scratch, places, args, flops, vmem=10, aliases=None):
    moved = sum(a.size * a.dtype.itemsize for a in args)
    moved += sum(int(np.prod(s.shape)) * np.dtype(s.dtype).itemsize for s in out_shape)
    return pl.pallas_call(
        kernel,
        out_shape=out_shape,
        grid_spec=pltpu.PrefetchScalarGridSpec(
            num_scalar_prefetch=1,
            grid=grid,
            in_specs=in_specs,
            out_specs=out_specs,
            scratch_shapes=scratch,
        ),
        input_output_aliases=aliases or {},
        compiler_params=pltpu.CompilerParams(vmem_limit_bytes=vmem * MIB),
        cost_estimate=pl.CostEstimate(
            flops=int(flops) // COST_SCALE, bytes_accessed=int(moved) // COST_SCALE, transcendentals=0
        ),
        name=name,
    )(places, *args)


def whole(array):
    return pl.BlockSpec(array.shape, lambda *_: (0,) * len(array.shape))


def rows(count, width):
    return pl.BlockSpec((count, width), lambda i, *_: (i, 0))


def shape(dims, kind):
    return jax.ShapeDtypeStruct(dims, kind)


def gather_blocks(places, halves, held, route=ACROSS):
    for i in range(2):
        for j in range(2 * BLOCKS):
            source = halves[2 * i + j // BLOCKS]
            target = places[1 + 2 * BLOCKS * (2 * ROUTES.index(route) + i) + j]
            held[target, i * PART_ROWS : (i + 1) * PART_ROWS, :] = source[j % BLOCKS]


def scatter_blocks(places, held, halves, route=ACROSS, at=0):
    for i in range(2):
        for j in range(2 * BLOCKS):
            target = halves[2 * i + j // BLOCKS]
            source = places[1 + 2 * BLOCKS * (2 * ROUTES.index(route) + i) + j]
            block = held[source, i * PART_ROWS : (i + 1) * PART_ROWS, :]
            target[j % BLOCKS, :, at : at + held.shape[2]] = block


CORE_AT = 1 + 4 * BLOCKS * len(ROUTES)
SLOT_AT = CORE_AT + 1
DP_AT = CORE_AT + 2


def side_of(held, side, at, width):
    return held[side * BLOCKS : (side + 1) * BLOCKS, :, at : at + width].reshape(D, width)


def to_pairs(held, wide_at, narrow_at):
    return jnp.concatenate(
        [side_of(held, side, wide_at, 128) for side in range(2)]
        + [side_of(held, side, narrow_at, 64) for side in range(2)],
        axis=1,
    )


def from_pairs(value, held, wide_at, narrow_at):
    for side in range(2):
        at = slice(side * BLOCKS, (side + 1) * BLOCKS)
        wide = value[:, 128 * side : 128 * (side + 1)]
        held[at, :, wide_at : wide_at + 128] = wide.reshape(BLOCKS, BLOCK_ROWS, 128)
        narrow = value[:, 256 + 64 * side : 320 + 64 * side]
        held[at, :, narrow_at : narrow_at + 64] = narrow.reshape(BLOCKS, BLOCK_ROWS, 64)


def half_shapes(width):
    return [shape((BLOCKS, PART_ROWS, width), LOW)] * 4


def half_specs(width):
    return [pl.BlockSpec((BLOCKS, PART_ROWS, width), lambda *_: (0, 0, 0))] * 4


def held_blocks(width):
    return pltpu.VMEM((2 * BLOCKS, BLOCK_ROWS, width), LOW)


def pack_first_kernel(w, exit_layer, out):
    wide = [w[i][:, :128] for i in range(3)]
    narrow = [w[i][:, 128:] for i in range(3)]
    live = jnp.float32(0.0)
    for i in range(exit_layer.shape[0]):
        live += jnp.where(exit_layer[i] >= LAYER, 1.0, 0.0)
    row = lax.broadcasted_iota(jnp.int32, (out.shape[0], 64), 0)
    marks = jnp.where(row == 0, live, 0.0)
    out[...] = jnp.concatenate(wide + narrow + [marks], axis=1).astype(LOW)


def pack_first(qkv, exit_layer):
    return pl.pallas_call(
        pack_first_kernel,
        in_specs=[whole(qkv), pl.BlockSpec(memory_space=pltpu.SMEM)],
        out_shape=shape((qkv.shape[1], 640), LOW),
        name="pack_first",
    )(qkv, exit_layer)


def pack_kernel(places, up, out, down, pool, qv, upb, up_out, down_pool, biases):
    quarter = 2 * places[CORE_AT] + places[0]
    mine = jnp.zeros((pool.shape[0], 192), WIDE)
    for i in range(4):
        mine = jnp.where(quarter == i, pool[:, 192 * i : 192 * (i + 1)], mine)
    up_out[:, 0:D] = up[...].astype(LOW)
    up_out[:, D : D + 256] = jnp.concatenate([out[...].T, mine[:, 0:64]], axis=1).astype(LOW)
    down_pool[:, 0:D] = down[...].astype(LOW)
    down_pool[:, D : D + 128] = mine[:, 64:192].astype(LOW)
    biases[...] = jnp.zeros_like(biases)
    biases[0:1, :] = upb[...].reshape(1, D)
    biases[1:2, 0:192] = qv[0:1, :]
    biases[2:3, 0:192] = qv[1:2, :]


def pack(places, up, out, down, pool, qv, upb):
    share = up.shape[0]
    args = (up, out, down, pool, qv, upb)
    return call(
        pack_kernel,
        "pack",
        (1,),
        [whole(a) for a in args],
        [pl.BlockSpec((share, 1024), lambda *_: (0, 0)), pl.BlockSpec((share, 896), lambda *_: (0, 0))]
        + [pl.BlockSpec((8, D), lambda *_: (0, 0))],
        [shape((share, 1024), LOW), shape((share, 896), LOW), shape((8, D), WIDE)],
        [],
        places,
        args,
        1,
        vmem=60,
    )


def by_side(places, mine, other):
    upper = places[0] == 1
    return jnp.where(upper, other, mine), jnp.where(upper, mine, other)


def project_kernel(places, x, bias, bias_other, h0, h1, h2, h3, q, k, v, w, count, held, pairs):
    @pl.when(pl.program_id(0) == 0)
    def _():
        gather_blocks(places, (h0, h1, h2, h3), held)
        for i in range(3):
            w[i] = to_pairs(held, 128 * i, 512 + 64 * i - 128)
        live = jnp.sum(side_of(held, 0, 576, 64).astype(WIDE), axis=0, keepdims=True)
        count[...] = jnp.broadcast_to(live[:, 0:1], count.shape)
        left, right = by_side(places, bias[...], bias_other[...])
        pairs[...] = jnp.concatenate(
            [left[:, :128], right[:, :128], left[:, 128:192], right[:, 128:192]], axis=1
        )

    left = x[...]
    q[...] = (dot(left, w[0]) + pairs[1:2, :]).astype(LOW)
    k[...] = dot(left, w[1]).astype(LOW)
    v[...] = (dot(left, w[2]) + pairs[2:3, :]).astype(LOW)


def project(places, tokens, bias, bias_other, halves):
    step = 512
    args = (tokens, bias, bias_other, *halves)
    return call(
        project_kernel,
        "project",
        (LEN // step,),
        [pl.BlockSpec((step, D), lambda i, places: (places[0] * (LEN // step) + i, 0))]
        + [whole(a) for a in args[1:]],
        [rows(step, 384)] * 3
        + [pl.BlockSpec((3, D, 384), lambda *_: (0, 0, 0)), pl.BlockSpec((8, 128), lambda *_: (0, 0))],
        [shape((LEN, 384), LOW)] * 3 + [shape((3, D, 384), LOW), shape((8, 128), WIDE)],
        [held_blocks(640), pltpu.VMEM((8, 384), WIDE)],
        places,
        args,
        2 * LEN * D * 1152,
    )


def first_of_pair():
    return lax.broadcasted_iota(jnp.int32, (1, 128), 1) < HD


def attend_kernel(places, q_ref, k_ref, v_ref, o_ref, inv_ref, p_ref, vx):
    first = first_of_pair()
    zero, one = jnp.zeros((), LOW), jnp.ones((), LOW)
    k = k_ref[...]
    v = v_ref[...]
    n = k.shape[0]
    vx[0:n, 0:128] = jnp.where(first, v, zero)
    vx[n : 2 * n, 0:128] = jnp.where(first, zero, v)
    vx[0:n, 128:256] = jnp.broadcast_to(jnp.where(first, one, zero), (n, 128))
    vx[n : 2 * n, 128:256] = jnp.broadcast_to(jnp.where(first, zero, one), (n, 128))
    step = 256
    for i in range(n // step):
        at = pl.ds(i * step, step)
        q = q_ref[at, :]
        result = None
        for head in range(2):
            mine = jnp.where(first, q, zero) if head == 0 else jnp.where(first, zero, q)
            score = dot_nt(mine, k)
            top = jnp.max(score, axis=1, keepdims=True)
            weight = jnp.exp2((score - top) * (HD**-0.5 * LOG2_E)).astype(LOW)
            p_ref[head, at, :] = weight
            part = dot(weight, vx[head * n : (head + 1) * n, :])
            result = part if result is None else result + part
        inv = 1.0 / result[:, 128:256]
        inv_ref[at, :] = inv
        o_ref[at, :] = (result[:, 0:128] * inv).astype(LOW)


def attend(places, q, k, v):
    pair = pl.BlockSpec((LEN, 128), lambda i, *_: (0, i))
    return call(
        attend_kernel,
        "attend_forward",
        (3,),
        [pair] * 3,
        [pair, pair, pl.BlockSpec((2, LEN, LEN), lambda i, *_: (i, 0, 0))],
        [shape((LEN, 384), LOW), shape((LEN, 384), WIDE), shape((6, LEN, LEN), LOW)],
        [pltpu.VMEM((2 * LEN, 256), LOW)],
        places,
        (q, k, v),
        4 * 6 * LEN * LEN * 256,
        vmem=12,
    )


def out_kernel(places, o, h0, h1, h2, h3, z0, z1, w_out, w_up, pool, held):
    @pl.when(pl.program_id(0) == 0)
    def _():
        gather_blocks(places, (h0, h1, h2, h3), held)
        w_out[...] = to_pairs(held, D, D + 128)
        w_up[:, 0:D] = side_of(held, 0, 0, D)
        w_up[:, D : 2 * D] = side_of(held, 1, 0, D)
        pool[...] = jnp.concatenate([side_of(held, i, 960, 64) for i in range(2)], axis=1)

    z = dot_nt(o[...], w_out[...]).astype(LOW)
    for i, out in enumerate((z0, z1)):

        @pl.when(pl.program_id(0) == i)
        def _(out=out):
            out[...] = z


def project_out(places, o, halves):
    step = 512
    return call(
        out_kernel,
        "project_out",
        (LEN // step,),
        [rows(step, 384)] + [whole(a) for a in halves],
        [pl.BlockSpec((step, D), lambda *_: (0, 0))] * 2
        + [pl.BlockSpec((D, 384), lambda *_: (0, 0))]
        + [pl.BlockSpec((D, 2 * D), lambda *_: (0, 0)), pl.BlockSpec((D, 128), lambda *_: (0, 0))],
        [shape((step, D), LOW)] * 2
        + [shape((D, 384), LOW), shape((D, 2 * D), LOW), shape((D, 128), LOW)],
        [held_blocks(1024)],
        places,
        (o, *halves),
        2 * LEN * D * 384,
    )


def normalize(hidden):
    centred = hidden - jnp.mean(hidden, axis=-1, keepdims=True)
    spread = lax.rsqrt(jnp.mean(centred * centred, axis=-1, keepdims=True) + EPS_NORM)
    return centred * spread, spread


def norm_back(grad_normed, normed, spread):
    return spread * (
        grad_normed
        - jnp.mean(grad_normed, axis=-1, keepdims=True)
        - normed * jnp.mean(grad_normed * normed, axis=-1, keepdims=True)
    )


def up_kernel(
    places, x, z0, z1, zp0, zp1, vec, bias_mine, bias_other, w, m, slope, n1, rs1, low_t, bias
):
    @pl.when(pl.program_id(0) == 0)
    def _():
        left, right = by_side(places, bias_mine[0:1, :], bias_other[0:1, :])
        bias[:, 0:D] = left
        bias[:, D : 2 * D] = right

    early = pl.program_id(0) < 2
    mine = jnp.where(early, z0[...], z1[...]).astype(WIDE)
    other = jnp.where(early, zp0[...], zp1[...]).astype(WIDE)
    total = mine + other
    normed, spread = normalize(x[...].astype(WIDE) + total + vec[4:5, :])
    n1[...] = normed
    rs1[...] = jnp.broadcast_to(spread, rs1.shape)
    middle = (normed * vec[0:1, :] + vec[1:2, :]).astype(LOW)
    low_t[...] = middle.T
    for c in range(4):
        at = pl.ds(c * 384, 384)
        u = dot(middle, w[:, at]) + bias[0:1, at]
        half = 0.5 * (1.0 + lax.erf(u * 0.7071067811865476))
        m[:, at] = (u * half).astype(LOW)
        slope[:, at] = (half + u * (jnp.exp(-0.5 * u * u) * 0.3989422804014327)).astype(LOW)


def feed_up(places, tokens, z, zp, vec, bias, bias_other, w_up):
    step = 256
    args = (tokens, *z, *zp, vec, bias, bias_other, w_up)
    return call(
        up_kernel,
        "feed_up",
        (LEN // step,),
        [pl.BlockSpec((step, D), lambda i, places: (places[0] * (LEN // step) + i, 0))]
        + [
            pl.BlockSpec((step, D), lambda i, *_, at=at: (jnp.clip(i - at, 0, 1), 0))
            for at in (0, 2, 0, 2)
        ]
        + [whole(a) for a in args[5:]],
        [rows(step, 2 * D)] * 2
        + [rows(step, D), rows(step, 128)]
        + [pl.BlockSpec((D, step), lambda i, *_: (0, i))],
        [shape((LEN, 2 * D), LOW)] * 2
        + [shape((LEN, D), WIDE), shape((LEN, 128), WIDE), shape((D, LEN), LOW)],
        [pltpu.VMEM((1, 2 * D), WIDE)],
        places,
        args,
        2 * LEN * D * 2 * D,
    )


def down_kernel(places, m, pool_part, h0, h1, h2, h3, f, w, pool, held):
    @pl.when(pl.program_id(0) == 0)
    def _():
        gather_blocks(places, (h0, h1, h2, h3), held)
        pieces = []
        for side in range(2):
            w[:, D * side : D * (side + 1)] = side_of(held, side, 0, D)
            pieces += [pool_part[:, 64 * side : 64 * (side + 1)], side_of(held, side, D, 128)]
        pool[...] = jnp.concatenate(pieces, axis=1)

    f[...] = dot_nt(m[...], w[...]).astype(LOW)


def feed_down(places, m, pool_part, halves):
    step = 512
    return call(
        down_kernel,
        "feed_down",
        (LEN // step,),
        [rows(step, 2 * D), whole(pool_part)] + [whole(a) for a in halves],
        [rows(step, D), pl.BlockSpec((D, 2 * D), lambda *_: (0, 0))]
        + [pl.BlockSpec((D, 384), lambda *_: (0, 0))],
        [shape((LEN, D), LOW), shape((D, 2 * D), LOW), shape((D, 384), LOW)],
        [held_blocks(896)],
        places,
        (m, pool_part, *halves),
        2 * LEN * D * 2 * D,
    )


def turn_kernel(
    places, exit_layer, labels, n1, f, fp, cot, vec, pool_a, pool_b, classes, bias, live_count,
    y, half, low, sums, ramp, pool, dy
):
    step = pl.program_id(0)
    middle = n1[...] * vec[0:1, :] + vec[1:2, :]
    total = f[...].astype(WIDE) + fp[...].astype(WIDE)
    normed, spread = normalize(middle + total + vec[5:6, :])
    result = normed * vec[2:3, :] + vec[3:4, :]
    low_result = result.astype(LOW)
    y[...] = low_result

    @pl.when(step // 2 == places[CORE_AT])
    def _():
        half[...] = low_result

    leaves = exit_layer[places[0]]
    grad = cot[...].astype(WIDE) * jnp.where(leaves > LAYER, 1.0, 0.0)
    dy[...] = grad

    @pl.when(step == 0)
    def _():
        sums[...] = jnp.zeros_like(sums)
        own = places[CORE_AT]

        @pl.when(own == 0)
        def _():
            pool[:, 0:384] = pool_a[...]
            pool[:, 384:D] = pool_b[...]

        @pl.when(own == 1)
        def _():
            pool[:, 0:384] = pool_b[...]
            pool[:, 384:D] = pool_a[...]

        count = 16
        head = result[0:count, :].astype(LOW)
        pooled = jnp.tanh(dot(head, pool[...]) + vec[6:7, :])
        pooled_low = pooled.astype(LOW)
        lane = lax.broadcasted_iota(jnp.int32, (count, 128), 1)
        row = lax.broadcasted_iota(jnp.int32, (count, 128), 0)
        valid = lane < 3
        logits = dot(pooled_low, classes[...]) + bias[0:1, :]
        top = jnp.max(jnp.where(valid, logits, -jnp.inf), axis=1, keepdims=True)
        shifted = logits - top
        log_sum = jnp.log(
            jnp.sum(jnp.where(valid, jnp.exp(shifted), 0.0), axis=1, keepdims=True)
        )
        log_probs = jnp.where(valid, shifted - log_sum, 0.0)
        probs = jnp.where(valid, jnp.exp(log_probs), 0.0)
        live = jnp.where(leaves >= LAYER, 1.0, 0.0)
        entropy = -live * jnp.sum(probs * log_probs, axis=1, keepdims=True)
        onehot = jnp.where(lane == labels[places[0]], 1.0, 0.0)
        grad_logits = live * (probs - onehot) / live_count[0:1, 0:1]
        grad_logits = jnp.where(valid & (row == 0), grad_logits, 0.0).astype(LOW)
        grad_pre = (dot_nt(grad_logits, classes[...]) * (1.0 - pooled * pooled)).astype(LOW)
        grad_head = dot_nt(grad_pre, pool[...])
        dy[0:count, :] = dy[0:count, :] + grad_head
        sums[3:4, :] = grad_pre[0:1, :].astype(WIDE)
        of_class = dot_tn(grad_logits, pooled_low)
        sums[4:7, :] = of_class[0:3, :]
        last = jnp.where(lane == 3, entropy, grad_logits.astype(WIDE))
        sums[7:8, 0:128] = last[0:1, :]
        ramp[0:1, :] = head[0:1, :].astype(WIDE)
        ramp[1:2, :] = grad_pre[0:1, :].astype(WIDE)

    grad = dy[...]
    sums[0:1, :] += jnp.sum(grad * normed, axis=0, keepdims=True)
    sums[1:2, :] += jnp.sum(grad, axis=0, keepdims=True)
    back = norm_back(grad * vec[2:3, :], normed, spread)
    sums[2:3, :] += jnp.sum(back, axis=0, keepdims=True)
    low[...] = back.astype(LOW)


def own_rows(step):
    return pl.BlockSpec((step, D), lambda i, places: (places[0] * (LEN // step) + i, 0))


def half_rows(step, sibling=False):
    count = LEN // step // 2

    def at(i, places):
        core = 1 - places[CORE_AT] if sibling else places[CORE_AT]
        return jnp.clip(i - count * core, 0, count - 1), 0

    return pl.BlockSpec((step, D), at)


def turn(places, exit_layer, labels, n1, f, fp, cotangent, vec, pool_a, pool_b, classes, bias, live_count):
    step = 256
    args = (exit_layer, labels, n1, f, fp, cotangent, vec, pool_a, pool_b, classes, bias, live_count)
    return call(
        turn_kernel,
        "turn",
        (LEN // step,),
        [pl.BlockSpec(memory_space=pltpu.SMEM)] * 2
        + [rows(step, D)] * 3
        + [own_rows(step)]
        + [whole(a) for a in args[6:]],
        [own_rows(step), half_rows(step)]
        + [rows(step, D)]
        + [pl.BlockSpec((8, D), lambda *_: (0, 0))] * 2,
        [shape((2 * LEN, D), LOW), shape((LEN // 2, D), LOW), shape((LEN, D), LOW)]
        + [shape((8, D), WIDE)] * 2,
        [pltpu.VMEM((D, D), LOW), pltpu.VMEM((step, D), WIDE)],
        places,
        args,
        LEN * D * 60,
    )


def feed_back_kernel(places, dh2, slope, w_down, w_up, du, dx, sums):
    grad = dot(dh2[...], w_down[...]) * slope[...].astype(WIDE)
    grad = grad.astype(LOW)
    du[...] = grad
    dx[...] = dot_nt(grad, w_up[...]).astype(LOW)

    @pl.when(pl.program_id(0) == 0)
    def _():
        sums[...] = jnp.zeros_like(sums)

    sums[0:1, :] += jnp.sum(grad.astype(WIDE), axis=0, keepdims=True)


def feed_back(places, dh2, slope, w_down, w_up):
    step = 512
    args = (dh2, slope, w_down, w_up)
    return call(
        feed_back_kernel,
        "feed_back",
        (LEN // step,),
        [rows(step, D), rows(step, 2 * D), whole(w_down), whole(w_up)],
        [rows(step, 2 * D), rows(step, D), pl.BlockSpec((8, 2 * D), lambda *_: (0, 0))],
        [shape((LEN, 2 * D), LOW), shape((LEN, D), LOW), shape((8, 2 * D), WIDE)],
        [],
        places,
        args,
        4 * LEN * D * 2 * D,
        vmem=14,
    )


def feed_grad_kernel(places, dh2, m, middle_t, du, ramp, h0, h1, h2, h3, held, turned):
    turned[...] = dh2[...].T
    for at, left, right in ((0, turned, m), (D, middle_t, du)):
        for side in range(2):
            for c in range(0, D, 256):
                part = dot(left[...], right[:, D * side + c : D * side + c + 256]).astype(LOW)
                held[side * BLOCKS : (side + 1) * BLOCKS, :, c : c + 256] = part.reshape(
                    BLOCKS, BLOCK_ROWS, 256
                )
        scatter_blocks(places, held, (h0, h1, h2, h3), ALONG, at)
    row = lax.broadcasted_iota(jnp.int32, (BLOCK_ROWS, 256), 0)
    for group in range((h0.shape[2] - 2 * D) // 256):
        slot = places[SLOT_AT] - 16 * group
        block = jnp.zeros((BLOCK_ROWS, 256), WIDE)
        for i in range(6):
            values = ramp[i // 3 : i // 3 + 1, 256 * (i % 3) : 256 * (i % 3 + 1)]
            mine = (row == 6 * slot + i) & (slot >= 0) & (slot < 16)
            block = jnp.where(mine, values, block)
        block = block.astype(LOW)
        at = 2 * D + 256 * group
        for i, half in enumerate((h0, h1, h2, h3)):
            first = PART_ROWS * (i // 2)
            for p in range(BLOCKS):
                half[p, :, at : at + 256] = block[first : first + PART_ROWS, :]


def feed_grad(places, slots, dh2, m, middle_t, du, ramp):
    args = (dh2, m, middle_t, du, ramp)
    width = 2 * D + 16 * slots
    return call(
        feed_grad_kernel,
        "feed_grad",
        (1,),
        [whole(a) for a in args],
        half_specs(width),
        half_shapes(width),
        [held_blocks(D), pltpu.VMEM((D, LEN), LOW)],
        places,
        args,
        4 * LEN * D * 2 * D,
        vmem=9 if slots == 16 else 48,
    )


def mid_kernel(places, dh2, dx, dxp, n1, rs1, vec, w_out, turn_sums, up_sums, dh1, low, do, sums):
    @pl.when(pl.program_id(0) == 0)
    def _():
        sums[...] = jnp.zeros_like(sums)
        sums[0:8, :] = turn_sums[...]
        sums[11:12, :] = up_sums[0:1, 0:D]
        sums[12:13, :] = up_sums[0:1, D : 2 * D]

    total = dx[...].astype(WIDE) + dxp[...].astype(WIDE)
    grad = dh2[...].astype(WIDE) + total
    normed = n1[...]
    sums[8:9, :] += jnp.sum(grad * normed, axis=0, keepdims=True)
    sums[9:10, :] += jnp.sum(grad, axis=0, keepdims=True)
    back = norm_back(grad * vec[0:1, :], normed, rs1[:, 0:1])
    sums[10:11, :] += jnp.sum(back, axis=0, keepdims=True)
    dh1[...] = back
    back_low = back.astype(LOW)
    low[...] = back_low
    do[...] = dot(back_low, w_out[...]).astype(LOW)


def mid(places, dh2, dx, dxp, n1, rs1, vec, w_out, turn_sums, up_sums):
    step = 512
    args = (dh2, dx, dxp, n1, rs1, vec, w_out, turn_sums, up_sums)
    count = 16
    return call(
        mid_kernel,
        "middle_back",
        (LEN // step,),
        [rows(step, D)] * 4 + [rows(step, 128)] + [whole(a) for a in args[5:]],
        [rows(step, D)] * 2 + [rows(step, 384), pl.BlockSpec((count, D), lambda *_: (0, 0))],
        [shape((LEN, D), WIDE), shape((LEN, D), LOW), shape((LEN, 384), LOW), shape((count, D), WIDE)],
        [],
        places,
        args,
        2 * LEN * D * 384,
    )


def attend_back_kernel(
    places, q_ref, k_ref, v_ref, do_ref, inv_ref, p_ref, dq_ref, dk_ref, dv_ref, ds_ref, held
):
    first = first_of_pair()
    zero = jnp.zeros((), LOW)
    n = k_ref.shape[0]
    k = k_ref[...]
    v = v_ref[...]
    k_own = [jnp.where(first, k, zero), jnp.where(first, zero, k)]
    scaled = (do_ref[...].astype(WIDE) * inv_ref[...]).astype(LOW)
    held[...] = scaled
    step = 512
    for i in range(n // step):
        at = pl.ds(i * step, step)
        d = held[at, :]
        total = None
        for head in range(2):
            mine = jnp.where(first, d, zero) if head == 0 else jnp.where(first, zero, d)
            grad_weight = dot_nt(mine, v)
            weight = p_ref[head, at, :].astype(WIDE)
            product = weight * grad_weight
            inner = jnp.sum(product, axis=1, keepdims=True)
            inner = inner * inv_ref[at, pl.ds(HD * head, 1)]
            grad_score = (product - weight * inner).astype(LOW)
            ds_ref[head, at, :] = grad_score
            part = dot(grad_score, k_own[head])
            total = part if total is None else total + part
        dq_ref[at, :] = (total * HD**-0.5).astype(LOW)
    scaled_t = scaled.T
    q_t = q_ref[...].T
    grad_v = jnp.concatenate(
        [dot(scaled_t[0:HD], p_ref[0]), dot(scaled_t[HD : 2 * HD], p_ref[1])], axis=0
    )
    dv_ref[...] = grad_v.T.astype(LOW)
    grad_k = jnp.concatenate(
        [dot(q_t[0:HD], ds_ref[0]), dot(q_t[HD : 2 * HD], ds_ref[1])], axis=0
    )
    dk_ref[...] = (grad_k * HD**-0.5).T.astype(LOW)


def attend_back(places, q, k, v, do, inv, p):
    at = pl.BlockSpec((LEN, 128), lambda i, *_: (0, i))
    return call(
        attend_back_kernel,
        "attend_backward",
        (3,),
        [at] * 5 + [pl.BlockSpec((2, LEN, LEN), lambda i, *_: (i, 0, 0))],
        [at] * 3,
        [shape((LEN, 384), LOW)] * 3,
        [pltpu.VMEM((2, LEN, LEN), LOW), pltpu.VMEM((LEN, 128), LOW)],
        places,
        (q, k, v, do, inv, p),
        8 * 6 * LEN * LEN * 256,
        vmem=19,
    )


MARK_ROWS = 6


def narrow_grad_kernel(places, left, dh1, o, dq, dk, dv, sums, h0, h1, h2, h3, held, turned, marks):
    turned[...] = left[...].T
    marks[...] = jnp.zeros_like(marks)
    for i, right in enumerate((dq, dk, dv)):
        value = right[...]
        from_pairs(dot(turned[...], value).astype(LOW), held, 128 * i, 512 + 64 * i)
        if i != 1:
            total = jnp.sum(value.astype(WIDE), axis=0, keepdims=True)
            for k in range(3):
                at = 13 * MARK_ROWS + 3 * (i // 2) + k
                marks[at : at + 1, :] = total[:, 128 * k : 128 * (k + 1)]
    turned[...] = dh1[...].T
    from_pairs(dot(turned[...], o[...]).astype(LOW), held, 384, 704)
    for i in range(13):
        for k in range(MARK_ROWS):
            at = i * MARK_ROWS + k
            marks[at : at + 1, :] = sums[i : i + 1, 128 * k : 128 * (k + 1)]
    block = marks[...].astype(LOW)
    for p in range(2 * BLOCKS):
        held[p, :, D : D + 128] = block
    scatter_blocks(places, held, (h0, h1, h2, h3), BESIDE)


def narrow_grad(places, tokens, dh1, o, grads, sums):
    args = (tokens, dh1, o, *grads, sums)
    width = D + 128
    return call(
        narrow_grad_kernel,
        "narrow_grad",
        (1,),
        [own_rows(LEN)] + [whole(a) for a in args[1:]],
        half_specs(width),
        half_shapes(width),
        [held_blocks(width), pltpu.VMEM((D, LEN), LOW), pltpu.VMEM((BLOCK_ROWS, 128), WIDE)],
        places,
        args,
        2 * LEN * D * 1536,
        vmem=12,
    )


def input_kernel(places, *refs):
    grads, w, (keep, send) = refs[:3], refs[3], refs[4:]
    total = None
    for i in range(3):
        part = dot_nt(grads[i][...], w[i])
        total = part if total is None else total + part
    total = total.astype(LOW)
    mine = pl.program_id(0) == places[CORE_AT]

    @pl.when(mine)
    def _():
        keep[...] = total

    @pl.when(jnp.logical_not(mine))
    def _():
        send[...] = total


def input_grad(places, grads, w):
    step = 512
    return call(
        input_kernel,
        "input_grad",
        (LEN // step,),
        [rows(step, 384)] * 3 + [whole(w)],
        [half_rows(step), half_rows(step, True)],
        [shape((LEN // 2, D), LOW)] * 2,
        [],
        places,
        (*grads, w),
        2 * LEN * D * 1152,
    )


def finish_kernel(places, dh1, keep, other, half):
    total = keep[...].astype(WIDE) + other[...].astype(WIDE)
    half[...] = (dh1[...] + total).astype(LOW)


def finish(places, dh1, keep, other):
    step = 128
    count = LEN // 2 // step
    return call(
        finish_kernel,
        "finish",
        (count,),
        [pl.BlockSpec((step, D), lambda i, places: (count * places[CORE_AT] + i, 0))]
        + [rows(step, D)] * 2,
        [rows(step, D)],
        [shape((LEN // 2, D), LOW)],
        [],
        places,
        (dh1, keep, other),
        LEN * D * 3,
    )[0]


def place_kernel(count, places, *refs):
    half = LEN // 2
    ins, out, sems = refs[-2 - count : -2], refs[-2], refs[-1]
    side, core = places[0], places[CORE_AT]
    at = [(1 - side, core), (1 - side, 1 - core), (side, core), (side, 1 - core)]
    copies = []
    for i, ref in enumerate(ins):
        first = pl.multiple_of((2 * at[i][0] + at[i][1]) * half, half)
        copies.append(pltpu.make_async_copy(ref, out.at[pl.ds(first, half)], sems.at[i]))
        copies[-1].start()
    for copy in copies:
        copy.wait()


def place(places, kept, quarters):
    first = [] if kept is None else [kept]
    return call(
        functools.partial(place_kernel, len(quarters)),
        "place",
        (1,),
        [pl.BlockSpec(memory_space=pl.ANY)] * len(first) + [whole(a) for a in quarters],
        [pl.BlockSpec(memory_space=pl.ANY)],
        [shape((2 * LEN, D), LOW)],
        [pltpu.SemaphoreType.DMA((len(quarters),))],
        places,
        (*first, *quarters),
        1,
        vmem=12,
        aliases={} if kept is None else {1: 0},
    )[0]


def update(places, name, pieces, width, ins, kernel, outs, scratch):
    counts = tuple(len(group) for group in pieces)
    args = [a for group in pieces for a in group]
    specs = [
        pl.BlockSpec((1, a.shape[1], width), lambda *_: (0, 0, 0)) if a.ndim == 3 else whole(a)
        for a in args
    ]
    return call(
        functools.partial(kernel, counts),
        name,
        (1,),
        specs + [whole(a) for a in ins],
        [whole(o) for o in outs],
        outs,
        scratch,
        places,
        (*args, *ins),
        1,
        vmem=60,
    )


def matrix_outs(weight):
    return [shape(weight.shape, WIDE)] * 3 + [shape(weight.shape, LOW)]


def step_matrix(ins, outs, at, grad, rate):
    new, first, second = adamw(ins[0][at], ins[1][at], ins[2][at], grad, rate, DECAY)
    outs[0][at] = new
    outs[1][at] = first
    outs[2][at] = second
    outs[3][at] = new.astype(LOW)


def step_vector(ins, outs, at, grad, rate=VECTOR_RATE, decay=0.0):
    results = adamw(ins[0][at], ins[1][at], ins[2][at], grad, rate, decay)
    for out, result in zip(outs, results, strict=True):
        out[at] = result


def update_feed_kernel(counts, places, *refs):
    total = sum(counts)
    grad, marks = sum_pieces(refs[:total], counts, 2 * D)
    ins, outs = refs[total : total + 9], refs[total + 9 : total + 21]
    heads, slopes = refs[total + 21 :]
    step_matrix(ins[0:3], outs[0:4], ..., grad[:, 0:D], RATE * FF ** (-0.5))
    step_matrix(ins[3:6], outs[4:8], ..., grad[:, D : 2 * D], RATE * D ** (-0.5))
    for s in range(heads.shape[0]):
        at = 256 * (s // 16)
        for i, target in enumerate((heads, slopes)):
            for k in range(3):
                row = 6 * (s % 16) + 3 * i + k
                target[s : s + 1, 256 * k : 256 * (k + 1)] = marks[row : row + 1, at : at + 256]
    share = ins[6].shape[0]
    column = lax.broadcasted_iota(jnp.int32, (D, share), 0)
    own = column == lax.broadcasted_iota(jnp.int32, (D, share), 1) + places[DP_AT] * share
    picked = dot(heads[...].astype(LOW), jnp.where(own, 1.0, 0.0).astype(LOW)).astype(LOW)
    pool = dot_tn(picked, slopes[...].astype(LOW))
    step_matrix(ins[6:9], outs[8:12], ..., pool, RATE * D ** (-0.5))


def update_narrow_kernel(counts, places, *refs):
    total = sum(counts)
    grad, marks = sum_pieces(refs[:total], counts, D)
    ins, outs = refs[total : total + 19], refs[total + 19 : total + 40]
    rows_of = refs[total + 40]

    def columns(i):
        return jnp.concatenate(
            [grad[:, 128 * i : 128 * (i + 1)], grad[:, 512 + 64 * i : 576 + 64 * i]], axis=1
        )

    for i in range(3):
        step_matrix(ins[0:3], outs[0:4], i, columns(i), RATE * D ** (-0.5))
    step_matrix(ins[3:6], outs[4:8], ..., columns(3).T, RATE * max(1, 2 * D // LEN) ** (-0.5))
    for i in range(14):
        for k in range(MARK_ROWS):
            at = i * MARK_ROWS + k
            rows_of[i : i + 1, 128 * k : 128 * (k + 1)] = marks[at : at + 1, :]
    side = places[0]
    pairs = rows_of[13:14, :]
    for i in range(2):
        pair = pairs[:, 384 * i : 384 * (i + 1)]
        wide = jnp.where(side == 0, pair[:, 0:128], pair[:, 128:256])
        narrow = jnp.where(side == 0, pair[:, 256:320], pair[:, 320:384])
        own = jnp.concatenate([wide, narrow], axis=1)
        step_vector(ins[6:9], outs[8:11], pl.ds(i, 1), own)
    hidden = jnp.where(side == 0, rows_of[11:12, :], rows_of[12:13, :])
    step_vector(ins[9:12], outs[11:14], ..., hidden.reshape(D))
    for i, at in enumerate((8, 9, 0, 1, 10, 2, 3)):
        step_vector(ins[12:15], outs[14:17], pl.ds(i, 1), rows_of[at : at + 1, :])
    for i in range(3):
        one = jnp.concatenate([rows_of[4 + i : 5 + i, :], rows_of[7:8, i : i + 1]], axis=1)
        step_vector(
            ins[15:18], outs[17:20], pl.ds(i, 1), one, RATE * (D // 4) ** (-0.5), DECAY
        )
    outs[20][...] = rows_of[7:8, 3:4] / ins[18][0:1, 0:1]


def per_device(
    dp_count,
    mp_count,
    tokens,
    cotangent,
    exit_layer,
    labels,
    qkv_weight,
    qkv_first,
    qkv_second,
    out_weight,
    out_first,
    out_second,
    up_weight,
    up_first,
    up_second,
    down_weight,
    down_first,
    down_second,
    pool_weight,
    pool_first,
    pool_second,
    qv_bias,
    qv_first,
    qv_second,
    up_bias,
    upb_first,
    upb_second,
    layer_vectors,
    vector_first,
    vector_second,
    class_weight,
    class_first,
    class_second,
):
    links = Links(dp_count, mp_count)
    side, core = links.side, links.core

    slot = 2 * links.dp + side
    places = jnp.concatenate(
        [side[None], links.places(), core[None], slot[None], links.dp[None]]
    ).astype(jnp.int32)
    share = D // dp_count

    by_kind = [a.transpose(1, 0, 2) for a in (qkv_weight, qkv_first, qkv_second)]
    down_turned = [a.T for a in (down_weight, down_first, down_second)]
    qkv_spread = links.spread(pack_first(by_kind[0], exit_layer))
    sent = qkv_spread.step()
    up_out, down_pool, biases = pack(
        places,
        after(up_weight, *sent),
        out_weight,
        down_turned[0],
        pool_weight,
        qv_bias,
        up_bias,
    )
    other_biases = links.swap(biases, SIDE)
    qkv_z = tuple(qkv_spread.last)
    sent = qkv_spread.step(up_out, other_biases)
    up_out_spread = links.spread(up_out)
    up_out_spread.step(*qkv_z)
    class_low = after(class_weight, *sent)
    classes = jnp.pad(class_low[:D].astype(LOW), ((0, 0), (0, 125)))
    class_bias = jnp.pad(class_low[D:], ((0, 0), (0, 125)))
    sent = qkv_spread.step(classes, class_bias)
    sent = up_out_spread.step(*sent)
    down_spread = links.spread(down_pool)
    sent = down_spread.step(*sent)

    biases = after(biases, *sent)
    q, k, v, w_qkv, live_count = project(places, tokens, biases, other_biases, qkv_spread.halves())
    sent = up_out_spread.step(q)
    q = after(q, *sent)
    o, inv, p = attend(places, q, k, v)
    sent = down_spread.step(o)
    o = after(o, *sent)
    *z, w_out, w_up, pool_part = project_out(places, o, up_out_spread.halves())
    zp = [links.swap(part, CORE) for part in z]
    sent = down_spread.step(w_up)
    z = after(z, *sent)
    m, slope, n1, rs1, middle_t = feed_up(
        places, tokens, z, zp, layer_vectors, biases, other_biases, w_up
    )
    f, w_down, pool_mine = feed_down(places, m, pool_part, down_spread.halves())
    fp = links.swap(f, CORE)
    pool_other = links.swap(pool_mine, CORE)
    y, y_half, dh2_low, turn_sums, ramp = turn(
        places, exit_layer, labels, n1, f, fp, cotangent, layer_vectors, pool_mine, pool_other,
        classes, class_bias, live_count,
    )

    y_first = links.swap(y_half, SIDE)
    du, dx, up_sums = feed_back(places, dh2_low, slope, w_down, w_up)
    dxp = links.swap(dx, CORE)
    m, dh2_low = after((m, dh2_low), dx)
    slots = 2 * dp_count
    feed_halves = feed_grad(places, slots, dh2_low, m, middle_t, du, ramp)
    feed_fold = links.fold(feed_halves, ALONG, 2 * D)
    feed_fold.step()
    dx = after(dx, *feed_halves)
    dh1, dh1_low, do, sums = mid(
        places, dh2_low, dx, dxp, n1, rs1, layer_vectors, w_out, turn_sums, up_sums
    )
    grads = attend_back(places, q, k, v, do, inv, p)
    token_keep, token_send = input_grad(places, grads, w_qkv)
    token_other = links.swap(token_send, CORE)
    sent = feed_fold.step(token_keep, y_first)
    grads = after(grads, *sent)
    narrow_halves = narrow_grad(places, tokens, dh1_low, o, grads, sums)
    narrow_fold = links.fold(narrow_halves, BESIDE, D)
    narrow_fold.step()
    token_keep = after(token_keep, *narrow_halves)
    grad_half = finish(places, dh1, token_keep, token_other)
    first = links.swap(grad_half, SIDE)
    second_own = links.swap(grad_half, CORE)
    sent = feed_fold.step(grad_half)
    sent = narrow_fold.step(*sent)
    sent = feed_fold.step(*sent)
    sent = narrow_fold.step(*sent)
    first, y_first = after((first, y_first), *sent)
    second, y_second = links.swap(first, CORE), links.swap(y_first, CORE)
    tokens_grad = place(places, None, [first, second, grad_half, second_own])
    result = place(places, y, [y_first, after(y_second, tokens_grad)])
    sent = narrow_fold.step(result)
    masters = [*down_turned, up_weight, up_first, up_second, pool_weight, pool_first, pool_second]
    feed_new = update(
        places,
        "update_feed",
        after(feed_fold.pieces(), *sent),
        2 * D + 16 * slots,
        masters,
        update_feed_kernel,
        [o for a in masters[0::3] for o in matrix_outs(a)],
        [pltpu.VMEM((slots, D), WIDE)] * 2,
    )
    down_new, down_first_new, down_second_new, down_copy = (a.T for a in feed_new[0:4])
    up_new, up_first_new, up_second_new, up_copy = feed_new[4:8]
    pool_new, pool_first_new, pool_second_new, pool_copy = feed_new[8:12]
    by_class = [a.T for a in (class_weight, class_first, class_second)]
    masters = [*by_kind, out_weight, out_first, out_second]
    vectors = [qv_bias, qv_first, qv_second, up_bias, upb_first, upb_second]
    vectors += [layer_vectors, vector_first, vector_second, *by_class]
    narrow_new = update(
        places,
        "update_narrow",
        after(narrow_fold.pieces(), feed_new[0]),
        D + 128,
        [*masters, *vectors, live_count],
        update_narrow_kernel,
        [o for a in masters[0::3] for o in matrix_outs(a)]
        + [shape(a.shape, WIDE) for a in vectors]
        + [shape((1, 1), WIDE)],
        [pltpu.VMEM((16, D), WIDE)],
    )
    qkv_new, qkv_first_new, qkv_second_new, qkv_copy = (
        a.transpose(1, 0, 2) for a in narrow_new[0:4]
    )
    out_new, out_first_new, out_second_new, out_copy = narrow_new[4:8]
    qv_new, qv_first_new, qv_second_new = narrow_new[8:11]
    upb_new, upb_first_new, upb_second_new = narrow_new[11:14]
    vector_new, vector_first_new, vector_second_new = narrow_new[14:17]
    class_new, class_first_new, class_second_new = (a.T for a in narrow_new[17:20])
    entropy = narrow_new[20].reshape(())
    return (
        result,
        tokens_grad,
        entropy,
        qkv_new,
        qkv_first_new,
        qkv_second_new,
        qkv_copy,
        out_new,
        out_first_new,
        out_second_new,
        out_copy,
        up_new,
        up_first_new,
        up_second_new,
        up_copy,
        down_new,
        down_first_new,
        down_second_new,
        down_copy,
        pool_new,
        pool_first_new,
        pool_second_new,
        pool_copy,
        qv_new,
        qv_first_new,
        qv_second_new,
        upb_new,
        upb_first_new,
        upb_second_new,
        vector_new,
        vector_first_new,
        vector_second_new,
        class_new,
        class_first_new,
        class_second_new,
    )


def solution(mesh):
    in_specs = (
        P("dp", None),
        P("dp", None),
        P("dp"),
        P("dp"),
        P("dp", None, "mp"),
        P("dp", None, "mp"),
        P("dp", None, "mp"),
        P("mp", "dp"),
        P("mp", "dp"),
        P("mp", "dp"),
        P("dp", "mp"),
        P("dp", "mp"),
        P("dp", "mp"),
        P("mp", "dp"),
        P("mp", "dp"),
        P("mp", "dp"),
        P("dp", None),
        P("dp", None),
        P("dp", None),
        P(None, "mp"),
        P(None, "mp"),
        P(None, "mp"),
        P("mp"),
        P("mp"),
        P("mp"),
        P(),
        P(),
        P(),
        P(),
        P(),
        P(),
    )
    out_specs = (
        P("dp", None),
        P("dp", None),
        P(),
        P("dp", None, "mp"),
        P("dp", None, "mp"),
        P("dp", None, "mp"),
        P("dp", None, "mp"),
        P("mp", "dp"),
        P("mp", "dp"),
        P("mp", "dp"),
        P("mp", "dp"),
        P("dp", "mp"),
        P("dp", "mp"),
        P("dp", "mp"),
        P("dp", "mp"),
        P("mp", "dp"),
        P("mp", "dp"),
        P("mp", "dp"),
        P("mp", "dp"),
        P("dp", None),
        P("dp", None),
        P("dp", None),
        P("dp", None),
        P(None, "mp"),
        P(None, "mp"),
        P(None, "mp"),
        P("mp"),
        P("mp"),
        P("mp"),
        P(),
        P(),
        P(),
        P(),
        P(),
        P(),
    )
    one_device = functools.partial(per_device, mesh.shape["dp"], mesh.shape["mp"])
    return jax.shard_map(
        one_device, mesh=mesh, in_specs=in_specs, out_specs=out_specs, check_vma=False
    )
```
